32 devices in a mesh: own: 4 (over y, x), rep: 8 (over z, core).
Axes of the slice: x: 2, y: 2, z: 4, core: 2. Of those that a mesh axis runs over, the one named last changes fastest.
Arguments:
- tokens: bfloat16 [4096, 2048], P(('own', 'rep')), may hold values from -6 to 6
- cotangent: bfloat16 [4096, 2048], P(('own', 'rep')), may hold values from -3 to 3
- route: int32 [4096, 1], P(('own', 'rep')), may hold values from 0 to 7; in each aligned block of 128 rows (0 to 127, 128 to 255, ...) at most 24 rows name the same one
- host: int32 [8], replicated, may hold values from 0 to 7, each once
- w_gate: bfloat16 [8, 2048, 256], P('rep', 'own'), may hold values from -0.125 to 0.125
- w_up: bfloat16 [8, 2048, 256], P('rep', 'own'), may hold values from -0.125 to 0.125
- w_down_t: bfloat16 [8, 2048, 256], P('rep', 'own'), may hold values from -0.375 to 0.375
Outputs:
- x_grad: bfloat16 [4096, 2048], P(('own', 'rep'))
- grad_gate: float32 [8, 2048, 256], P('rep', 'own')
- grad_up: float32 [8, 2048, 256], P('rep', 'own')
- grad_down_t: float32 [8, 2048, 256], P('rep', 'own')
The draws below stay inside these ranges and needn't reach their ends.
Inputs may be any that keep to these rules, and one draw needn't show every extreme that they name: `route`: among the 128 tokens of one device no hot expert is named more than 24 times, and in every draw some expert is named exactly 24 times on some device. `host`: each replica group serves exactly one hot expert.
All inputs are finite; a program needn't handle non-finite values.
Results may differ from the reference program's by a relative error of at most 0.017.
Values may be sent and summed in bfloat16 or wider, within the bound.
No kernel may reach another device: no remote copies, remote signals or barrier semaphores. Data moves between devices by JAX's collectives and lax.ppermute only.
A program may use at most 64 MiB of HBM per device.

```python
import math
import jax
import jax.numpy as jnp
import numpy as np
from jax import lax

D = 2048
HW = 256
TOK_DEV = 128
HOT = 8
CAP = 24
TOKENS = 4096
N_OWN = 4
N_REP = 8


def shard_levels(rng, dims, shards, smallest, high):
    def one(dim, shards_of):
        draws = jax.random.uniform(jax.random.fold_in(jax.random.fold_in(rng, 6), dim), (shards_of,), jnp.float32, smallest / len(shards), high / len(shards))
        return jnp.repeat(jnp.exp(draws), dims[dim] // shards_of).reshape((-1,) + (1,) * (len(dims) - dim - 1))

    factor_of = one(*shards[0])
    for cut in shards[1:]:
        factor_of = factor_of * one(*cut)
    return factor_of


def assign_block(rng, own, number, rows, number_of, top, reach, skew):
    ranking = jax.random.permutation(rng, number_of)
    crowded, usual = load_shares(number_of, rows * top, reach, skew, True), load_shares(number_of, rows * top, reach, skew, False)
    places = jnp.arange(number_of)

    def named(sizes, offset_by):
        used = int((sizes > 0).sum())
        fixed = max(1, used // 4)
        passed = fixed + (places - fixed + offset_by * (used - fixed)) % max(1, number_of - fixed)
        return jnp.zeros((number_of,), jnp.int32).at[ranking[jnp.where(places < fixed, places, passed)]].set(jnp.asarray(sizes, jnp.int32))

    sizes = jnp.where(number % 4 == 0, named(crowded, number // 4), named(usual, number - number // 4 - 1))
    mixed = jax.random.permutation(jax.random.fold_in(own, 3), number_of)
    donor, receiver = mixed[0:number_of // 2 * 2:2], mixed[1:number_of // 2 * 2:2]
    margin = jnp.minimum(sizes[donor] - 1, reach - sizes[receiver]) // 2
    margin = jnp.where((donor == ranking[0]) | (receiver == ranking[0]) | (sizes[receiver] == 0), 0, jnp.maximum(margin, 0))
    passed = jax.random.randint(jax.random.fold_in(own, 4), (number_of // 2,), 0, 1 << 20) % (margin + 1)
    sizes = sizes.at[donor].add(-passed).at[receiver].add(passed)
    items = jnp.searchsorted(jnp.cumsum(sizes), jnp.arange(rows * top), side="right").astype(jnp.int32)
    grid = items.reshape(top, rows).T
    grid = grid[jax.random.permutation(jax.random.fold_in(own, 1), rows)]
    offset_by = jax.random.randint(jax.random.fold_in(own, 2), (rows, 1), 0, top)
    return jnp.take_along_axis(grid, (jnp.arange(top)[None, :] + offset_by) % top, axis=1)


def load_shares(count, total, limit, lean, full):
    portions = [(1 << 20) // math.isqrt(grade ** lean) + 1 for grade in range(1, count + 1)]
    largest = limit if full else min(limit, max(-(-total // count), total * portions[0] // sum(portions)))
    least = 1 if total - largest >= count - 1 else 0
    given, spare = [largest] + [least] * (count - 1), total - largest - least * (count - 1)
    while spare > 0:
        free = [i for i in range(1, count) if given[i] < largest] or [i for i in range(1, count) if given[i] < limit]
        pool, remaining = sum([portions[i] for i in free]), spare
        for i in free:
            addition = min(limit - given[i], max(1, remaining * portions[i] // pool), spare)
            given[i] = given[i] + addition
            spare = spare - addition
    return np.array(given)


def scatter_about(rng, extent, spread, most, pieces=(), kind=jnp.bfloat16):
    drawn = jax.random.normal(rng, extent, jnp.float32) * spread
    if len(pieces) > 0:
        drawn = shard_levels(rng, extent, pieces, -0.22, 0.18) * drawn
    return jnp.clip(drawn, min=-most, max=most).astype(kind)


def setup_inputs(seed: int = 0) -> dict:
    key_of = jax.random.split(jax.random.key(seed), 8)
    tokens = scatter_about(key_of[0], (TOKENS, D), 1.0, 6.0, ((0, 32),))
    cotangent = scatter_about(key_of[1], (TOKENS, D), 0.5, 3.0, ((0, 32),))
    route_keys = jax.random.split(jax.random.fold_in(key_of[2], 1), TOKENS // TOK_DEV)
    route_turns = jax.random.permutation(jax.random.fold_in(key_of[2], 3), TOKENS // TOK_DEV)
    route = jax.vmap(lambda own, number: assign_block(jax.random.fold_in(key_of[2], 2), own, number, TOK_DEV, HOT, 1, CAP, 2))(route_keys, route_turns).reshape((TOKENS, 1))
    host = jax.random.permutation(key_of[3], HOT).astype(jnp.int32)
    w_gate = scatter_about(key_of[4], (HOT, D, HW), D ** -0.5, 0.125, ((0, 8), (1, 4)))
    w_up = scatter_about(key_of[5], (HOT, D, HW), D ** -0.5, 0.125, ((0, 8), (1, 4)))
    w_down_t = scatter_about(key_of[6], (HOT, D, HW), HW ** -0.5, 0.375, ((0, 8), (1, 4)))
    return {"tokens": tokens, "cotangent": cotangent, "route": route, "host": host, "w_gate": w_gate, "w_up": w_up, "w_down_t": w_down_t}


def reference(tokens, cotangent, route, host, w_gate, w_up, w_down_t):
    target = host[route[:, 0]].reshape(N_OWN, N_REP, TOK_DEV)
    labels = jnp.arange(HOT, dtype=jnp.int32)
    marked = (target[..., None] == labels).astype(jnp.int32)
    arrival = (jnp.sum(jnp.cumsum(marked, axis=2) * marked, axis=3) - 1).astype(jnp.int32)
    x_all = tokens.reshape(N_OWN, N_REP, TOK_DEV, D)
    dy_all = cotangent.reshape(N_OWN, N_REP, TOK_DEV, D)
    source = jnp.broadcast_to(jnp.arange(N_REP, dtype=jnp.int32)[:, None], (N_REP, TOK_DEV))
    gate_f = w_gate.astype(jnp.float32)
    up_f = w_up.astype(jnp.float32)
    down_f = w_down_t.astype(jnp.float32)

    def per_row(totals, item):
        x_row, dy_row, target_row, arrival_row = item
        empty = jnp.zeros((HOT, N_REP, CAP, D), jnp.bfloat16)
        slot_x = empty.at[target_row, source, arrival_row].set(x_row).reshape(HOT, N_REP * CAP, D).astype(jnp.float32)
        slot_dy = empty.at[target_row, source, arrival_row].set(dy_row).reshape(HOT, N_REP * CAP, D).astype(jnp.float32)
        gate_act = jnp.einsum("esd,edh->esh", slot_x, gate_f)
        up_act = jnp.einsum("esd,edh->esh", slot_x, up_f)
        back_grad = jnp.einsum("esd,edh->esh", slot_dy, down_f)
        sigmoid_g = jax.nn.sigmoid(gate_act)
        silu_gate = gate_act * sigmoid_g
        hidden = (silu_gate * up_act).astype(jnp.bfloat16).astype(jnp.float32)
        grad_gate_h = (back_grad * up_act * sigmoid_g * (1.0 + gate_act * (1.0 - sigmoid_g))).astype(jnp.bfloat16).astype(jnp.float32)
        grad_up_h = (back_grad * silu_gate).astype(jnp.bfloat16).astype(jnp.float32)
        slot_grad = jnp.einsum("esh,edh->esd", grad_gate_h, gate_f) + jnp.einsum("esh,edh->esd", grad_up_h, up_f)
        slot_grad = slot_grad.astype(jnp.bfloat16).reshape(HOT, N_REP, CAP, D)
        x_back = slot_grad[target_row, source, arrival_row]
        partial_terms = jnp.stack([
            jnp.einsum("esd,esh->edh", slot_x, grad_gate_h),
            jnp.einsum("esd,esh->edh", slot_x, grad_up_h),
            jnp.einsum("esd,esh->edh", slot_dy, hidden)]).astype(jnp.bfloat16)
        partial_terms = lax.optimization_barrier(partial_terms)
        return totals + partial_terms.astype(jnp.float32), x_back

    start = jnp.zeros((3, HOT, D, HW), jnp.float32)
    totals, x_back = lax.scan(per_row, start, (x_all, dy_all, target, arrival))
    return x_back.reshape(TOKENS, D), totals[0], totals[1], totals[2]
```

```python
import functools

import jax
import jax.numpy as jnp
from jax import lax
from jax.experimental import pallas as pl
from jax.experimental.pallas import tpu as pltpu
from jax.sharding import PartitionSpec as P

VMEM = pl.BlockSpec(memory_space=pltpu.VMEM)
SMEM = pl.BlockSpec(memory_space=pltpu.SMEM)
PARAMS = pltpu.CompilerParams(vmem_limit_bytes=48 * 1024 * 1024)


def dot(left, right, left_dim, right_dim):
    return lax.dot_general(
        left, right, (((left_dim,), (right_dim,)), ((), ())), preferred_element_type=jnp.float32
    )


def pack_kernel(hot, capacity, parts, rank_ref, host_ref, route_ref, x_ref, dy_ref, pick_ref, *send_refs):
    rows = route_ref.shape[0]
    lanes = pick_ref.shape[1]
    width = max(128, hot)
    lane = lax.broadcasted_iota(jnp.int32, (rows, width), 1)
    base = jnp.zeros((1, width), jnp.int32)
    lane_row = lax.broadcasted_iota(jnp.int32, (1, width), 1)
    for e in range(hot):
        base = jnp.where(lane_row == e, (host_ref[e] ^ rank_ref[0]) * capacity, base)
    marked = route_ref[...] == lane
    marked_f = jnp.where(marked, 1.0, 0.0)
    earlier = jnp.where(
        lax.broadcasted_iota(jnp.int32, (rows, rows), 1) < lax.broadcasted_iota(jnp.int32, (rows, rows), 0), 1.0, 0.0
    )
    before = dot(earlier.astype(jnp.bfloat16), marked_f.astype(jnp.bfloat16), 1, 0).astype(jnp.int32)
    position = jnp.sum(jnp.where(marked, before + base, 0), axis=1, keepdims=True)
    pick = jnp.where(lax.broadcasted_iota(jnp.int32, (rows, lanes), 1) == position, 1.0, 0.0)
    pick_ref[...] = pick.astype(jnp.bfloat16)
    turned = pick.T.astype(jnp.bfloat16)
    if parts == 1:
        send_refs[0][...] = jnp.concatenate(
            [dot(turned, x_ref[...], 1, 0), dot(turned, dy_ref[...], 1, 0)], axis=1
        ).astype(jnp.bfloat16)
        return
    for which, ref in enumerate((x_ref, dy_ref)):
        filled = dot(turned, ref[...], 1, 0)
        for k in range(parts):
            send_refs[2 * k + which][...] = filled[k * capacity : (k + 1) * capacity].astype(jnp.bfloat16)


def main_kernel(n_own, parts, capacity, own_ref, x_ref, dy_ref, *refs):
    gates, ups, downs = refs[:n_own], refs[n_own : 2 * n_own], refs[2 * n_own : 3 * n_own]
    back_refs = refs[3 * n_own : 3 * n_own + parts]
    own_term_ref, *term_refs = refs[3 * n_own + parts :]
    slots = x_ref.shape[0]
    depth, hidden_width = gates[0].shape
    own = own_ref[0]
    columns = [pl.ds(pl.multiple_of((own ^ k) * depth, depth), depth) for k in range(n_own)]
    gate_act = jnp.zeros((slots, hidden_width), jnp.float32)
    up_act = jnp.zeros((slots, hidden_width), jnp.float32)
    back_grad = jnp.zeros((slots, hidden_width), jnp.float32)
    for k in range(n_own):
        x_part = x_ref[:, columns[k]]
        gate_act += dot(x_part, gates[k][...], 1, 0)
        up_act += dot(x_part, ups[k][...], 1, 0)
        back_grad += dot(dy_ref[:, columns[k]], downs[k][...], 1, 0)
    sigmoid_g = jax.nn.sigmoid(gate_act)
    silu_gate = gate_act * sigmoid_g
    hidden = (silu_gate * up_act).astype(jnp.bfloat16)
    grad_gate_h = (back_grad * up_act * sigmoid_g * (1.0 + gate_act * (1.0 - sigmoid_g))).astype(jnp.bfloat16)
    grad_up_h = (back_grad * silu_gate).astype(jnp.bfloat16)
    for k in range(n_own):
        slot_grad = dot(grad_gate_h, gates[k][...], 1, 1) + dot(grad_up_h, ups[k][...], 1, 1)
        rows = slots // parts
        for j in range(parts):
            back_refs[j][:, columns[k]] = slot_grad[j * rows : (j + 1) * rows].astype(jnp.bfloat16)
    for k in range(n_own):
        x_part = x_ref[:, columns[k]]
        terms = (
            dot(x_part, grad_gate_h, 0, 0),
            dot(x_part, grad_up_h, 0, 0),
            dot(dy_ref[:, columns[k]], hidden, 0, 0),
        )
        into = own_term_ref if k == 0 else term_refs[k - 1]
        for i, term in enumerate(terms):
            into[:, i * hidden_width : (i + 1) * hidden_width] = term.astype(into.dtype)


def sum_kernel(n_terms, own_ref, *refs):
    hidden_width = refs[-1].shape[1]
    for i, out_ref in enumerate(refs[n_terms:]):
        at = slice(i * hidden_width, (i + 1) * hidden_width)
        total = own_ref[:, at]
        for ref in refs[:n_terms]:
            total = total + ref[:, at].astype(jnp.float32)
        out_ref[...] = total


def shards(n_own, n_rep, tokens, cotangent, route, host, w_gate, w_up, w_down_t):
    tok_rows, model_width = tokens.shape
    hot = host.shape[0]
    hidden_width = w_gate.shape[2]
    depth = w_gate.shape[1]
    capacity = max(2, (3 * tok_rows + 2 * hot - 1) // (2 * hot))
    slots = hot * capacity
    own = lax.axis_index("own").astype(jnp.int32).reshape(1)
    rank = lax.axis_index("rep").astype(jnp.int32).reshape(1)
    parts = n_rep if capacity % 8 == 0 else 1

    def swap(value, axis, size, k):
        return lax.ppermute(value, axis, [(i, i ^ k) for i in range(size)])

    def gather(piece):
        return [piece] + [swap(piece, "own", n_own, k) for k in range(1, n_own)]

    gates, ups, downs = gather(w_gate[0]), gather(w_up[0]), gather(w_down_t[0])

    if parts > 1:
        sends = [jax.ShapeDtypeStruct((capacity, model_width), jnp.bfloat16)] * (2 * parts)
    else:
        sends = [jax.ShapeDtypeStruct((slots, 2 * model_width), jnp.bfloat16)]
        rank = jnp.zeros_like(rank)
    pick, *sent = pl.pallas_call(
        functools.partial(pack_kernel, hot, capacity, parts),
        out_shape=[jax.ShapeDtypeStruct((tok_rows, slots), jnp.bfloat16)] + sends,
        in_specs=[SMEM, SMEM, VMEM, VMEM, VMEM],
        out_specs=[VMEM] * (1 + len(sends)),
        compiler_params=PARAMS,
    )(rank, host, route, tokens, cotangent)

    def whole_exchange(value):
        return lax.all_to_all(
            value.reshape(hot, capacity, -1), "rep", split_axis=0, concat_axis=0, tiled=True
        ).reshape(slots, -1)

    if parts > 1:
        got = sent[:2] + [swap(sent[i], "rep", n_rep, i // 2) for i in range(2, 2 * parts)]
        slot_x, slot_dy = jnp.concatenate(got[0::2]), jnp.concatenate(got[1::2])
    else:
        got = whole_exchange(sent[0])
        slot_x, slot_dy = got[:, :model_width], got[:, model_width:]

    backs = [jax.ShapeDtypeStruct((slots // parts, model_width), jnp.bfloat16)] * parts
    term = (depth, 3 * hidden_width)
    terms = [jax.ShapeDtypeStruct(term, jnp.float32)] + [jax.ShapeDtypeStruct(term, jnp.bfloat16)] * (n_own - 1)
    outs = pl.pallas_call(
        functools.partial(main_kernel, n_own, parts, capacity),
        out_shape=backs + terms,
        in_specs=[SMEM] + [VMEM] * (2 + 3 * n_own),
        out_specs=[VMEM] * (parts + n_own),
        compiler_params=PARAMS,
    )(own, slot_x, slot_dy, *gates, *ups, *downs)
    back, own_term, sent_terms = outs[:parts], outs[parts], outs[parts + 1 :]

    if parts > 1:
        returned = jnp.concatenate([back[0]] + [swap(back[k], "rep", n_rep, k) for k in range(1, parts)])
    else:
        returned = whole_exchange(back[0])
    got_terms = [swap(sent_terms[k - 1], "own", n_own, k) for k in range(1, n_own)]
    x_grad = dot(pick, returned, 1, 0).astype(jnp.bfloat16)
    grads = pl.pallas_call(
        functools.partial(sum_kernel, n_own - 1),
        out_shape=[jax.ShapeDtypeStruct((depth, hidden_width), jnp.float32)] * 3,
        in_specs=[VMEM] * n_own,
        out_specs=[VMEM] * 3,
        compiler_params=PARAMS,
    )(own_term, *got_terms)
    return (x_grad, *(grad[None] for grad in grads))


def solution(mesh):
    return jax.shard_map(
        functools.partial(shards, mesh.shape["own"], mesh.shape["rep"]),
        mesh=mesh,
        in_specs=(
            P(("own", "rep"), None),
            P(("own", "rep"), None),
            P(("own", "rep"), None),
            P(),
            P("rep", "own", None),
            P("rep", "own", None),
            P("rep", "own", None),
        ),
        out_specs=(
            P(("own", "rep"), None),
            P("rep", "own", None),
            P("rep", "own", None),
            P("rep", "own", None),
        ),
        check_vma=False,
    )
```

```python
import functools

import jax
import jax.numpy as jnp
from jax import lax
from jax.experimental import pallas as pl
from jax.experimental.pallas import tpu as pltpu
from jax.sharding import PartitionSpec as P

VMEM = pl.BlockSpec(memory_space=pltpu.VMEM)
SMEM = pl.BlockSpec(memory_space=pltpu.SMEM)
HBM = pl.BlockSpec(memory_space=pltpu.HBM)
PARAMS = pltpu.CompilerParams(vmem_limit_bytes=48 * 1024 * 1024)
BF16 = jnp.bfloat16
F32 = jnp.float32


def dot(left, right, left_dim, right_dim):
    return lax.dot_general(
        left, right, (((left_dim,), (right_dim,)), ((), ())), preferred_element_type=F32
    )


def shape(rows, cols, dtype=BF16):
    return jax.ShapeDtypeStruct((rows, cols), dtype)


def call(kernel, outs, scalars, scratch=(), fetched=0):
    def run(*operands):
        placed = len(operands) - scalars - fetched
        return pl.pallas_call(
            kernel,
            out_shape=outs,
            in_specs=[SMEM] * scalars + [VMEM] * placed + [HBM] * fetched,
            out_specs=[VMEM] * len(outs),
            scratch_shapes=list(scratch),
            compiler_params=PARAMS,
        )(*operands)

    return run


def join_kernel(gate_ref, up_ref, down_ref, first_ref, second_ref, sems):
    depth = gate_ref.shape[0]
    half = depth // 2
    moves = (
        (gate_ref, first_ref.at[pl.ds(0, depth)]),
        (up_ref.at[pl.ds(0, half)], first_ref.at[pl.ds(depth, half)]),
        (up_ref.at[pl.ds(half, half)], second_ref.at[pl.ds(0, half)]),
        (down_ref, second_ref.at[pl.ds(half, depth)]),
    )
    loads = [pltpu.make_async_copy(source, into, sems.at[i]) for i, (source, into) in enumerate(moves)]
    for load in loads:
        load.start()
    for load in loads:
        load.wait()


def pack_kernel(capacity, rank_ref, host_ref, route_a, route_b, x_b, dy_b, *refs):
    sources, (pick_ref, *send_refs), (x_a, dy_a, sems) = refs[:2], refs[2:-3], refs[-3:]
    loads = [
        pltpu.make_async_copy(source, into, sems.at[i]) for i, (source, into) in enumerate(zip(sources, (x_a, dy_a)))
    ]
    for load in loads:
        load.start()
    hot = host_ref.shape[0]
    slots = pick_ref.shape[0]
    tokens = route_a.shape[1]
    block = 2 * capacity
    label = lax.broadcasted_iota(jnp.int32, (hot, tokens), 0)
    base = jnp.zeros((hot, tokens), jnp.int32)
    for e in range(hot):
        apart = host_ref[e] ^ rank_ref[0]
        start = jnp.where((apart & 1) == 0, (apart >> 1) * block, -2 * slots)
        base = jnp.where(label == e, start, base)
    earlier = lax.broadcasted_iota(jnp.int32, (tokens, tokens), 0) < lax.broadcasted_iota(
        jnp.int32, (tokens, tokens), 1
    )
    earlier = jnp.where(earlier, 1.0, 0.0).astype(BF16)
    slot = lax.broadcasted_iota(jnp.int32, (slots, tokens), 0)

    def picks(route_ref, offset):
        marked = route_ref[...] == label
        before = dot(jnp.where(marked, 1.0, 0.0).astype(BF16), earlier, 1, 0).astype(jnp.int32)
        position = jnp.sum(jnp.where(marked, before + base, 0), axis=0, keepdims=True) + offset
        return jnp.where(slot == position, 1.0, 0.0).astype(BF16)

    pick_a, pick_b = picks(route_a, 0), picks(route_b, capacity)
    pick_ref[:, :tokens] = pick_a
    pick_ref[:, tokens:] = pick_b
    for at, (a, b) in enumerate(((x_a, x_b), (dy_a, dy_b))):
        loads[at].wait()
        filled = (dot(pick_a, a[...], 1, 0) + dot(pick_b, b[...], 1, 0)).astype(BF16)
        for k, ref in enumerate(send_refs):
            ref[at * block : (at + 1) * block] = filled[k * block : (k + 1) * block]


def main_kernel(parts, own_ref, *refs):
    got, weights = refs[:parts], refs[parts : parts + 8]
    back_refs = refs[parts + 8 : 2 * parts + 8]
    own_term, one_a, one_b, two_a, two_b, three_a, three_b, x_ref, dy_ref = refs[2 * parts + 8 :]
    block = got[0].shape[0] // 2
    depth = weights[0].shape[0] * 2 // 3
    half = depth // 2
    own = own_ref[0]
    for k in range(parts):
        x_ref[k * block : (k + 1) * block] = got[k][:block]
        dy_ref[k * block : (k + 1) * block] = got[k][block:]

    def gate(k):
        return weights[2 * k][:depth]

    def up(k):
        return jnp.concatenate([weights[2 * k][depth:], weights[2 * k + 1][:half]], axis=0)

    def down(k):
        return weights[2 * k + 1][half:]

    columns = [pl.ds(pl.multiple_of((own ^ k) * depth, depth), depth) for k in range(4)]
    gate_act = sum(dot(x_ref[:, columns[k]], gate(k), 1, 0) for k in range(4))
    up_act = sum(dot(x_ref[:, columns[k]], up(k), 1, 0) for k in range(4))
    back_grad = sum(dot(dy_ref[:, columns[k]], down(k), 1, 0) for k in range(4))
    sigmoid_g = jax.nn.sigmoid(gate_act)
    silu_gate = gate_act * sigmoid_g
    hidden = (silu_gate * up_act).astype(BF16)
    grad_gate_h = (back_grad * up_act * sigmoid_g * (1.0 + gate_act * (1.0 - sigmoid_g))).astype(BF16)
    grad_up_h = (back_grad * silu_gate).astype(BF16)
    for k in range(4):
        slot_grad = (dot(grad_gate_h, gate(k), 1, 1) + dot(grad_up_h, up(k), 1, 1)).astype(BF16)
        for j in range(parts):
            back_refs[j][:, columns[k]] = slot_grad[j * block : (j + 1) * block]
    width = hidden.shape[1]
    for k, into in ((3, (three_a, three_b)), (1, (one_a, one_b)), (2, (two_a, two_b)), (0, (own_term,))):
        x_part, dy_part = x_ref[:, columns[k]], dy_ref[:, columns[k]]
        terms = (dot(x_part, grad_gate_h, 0, 0), dot(x_part, grad_up_h, 0, 0), dot(dy_part, hidden, 0, 0))
        rows = depth // len(into)
        for i, term in enumerate(terms):
            for j, ref in enumerate(into):
                ref[:, i * width : (i + 1) * width] = term[j * rows : (j + 1) * rows].astype(ref.dtype)


def sum_kernel(own_ref, one_a, two_a, one_b, two_b, *out_refs):
    width = out_refs[0].shape[1]
    half = one_a.shape[0]
    for i, out_ref in enumerate(out_refs):
        at = slice(i * width, (i + 1) * width)
        out_ref[:half] = own_ref[:half, at] + one_a[:, at].astype(F32) + two_a[:, at].astype(F32)
        out_ref[half:] = own_ref[half:, at] + one_b[:, at].astype(F32) + two_b[:, at].astype(F32)


def unpack_kernel(pick_ref, *refs):
    returned, (mine_ref, other_ref) = refs[:-2], refs[-2:]
    tokens = mine_ref.shape[0]
    block = returned[0].shape[0]
    for at, ref in enumerate((other_ref, mine_ref)):
        half = slice((1 - at) * tokens, (2 - at) * tokens)
        ref[...] = sum(
            dot(pick_ref[k * block : (k + 1) * block, half], part[...], 0, 0) for k, part in enumerate(returned)
        ).astype(BF16)


def shards_by_partner(n_rep, tokens, cotangent, route, host, w_gate, w_up, w_down_t):
    tok_rows, model_width = tokens.shape
    hot = host.shape[0]
    _, depth, width = w_gate.shape
    half = depth // 2
    capacity = (3 * tok_rows + 2 * hot - 1) // (2 * hot)
    slots = hot * capacity
    parts = n_rep // 2
    block = 2 * capacity
    own = lax.axis_index("own").astype(jnp.int32).reshape(1)
    rank = lax.axis_index("rep").astype(jnp.int32).reshape(1)

    def over_own(value, k):
        return lax.ppermute(value, "own", [(i, i ^ k) for i in range(4)])

    def over_rep(value, k):
        return lax.ppermute(value, "rep", [(i, i ^ k) for i in range(n_rep)])

    route = route.reshape(1, tok_rows)
    route_b, tokens_b, cotangent_b = over_rep(route, 1), over_rep(tokens, 1), over_rep(cotangent, 1)

    first, second = call(
        join_kernel, [shape(3 * half, width)] * 2, 0, [pltpu.SemaphoreType.DMA((4,))], 3
    )(w_gate[0], w_up[0], w_down_t[0])
    first_1, second_2 = over_own(first, 1), over_own(second, 2)

    pick, *sent = call(
        functools.partial(pack_kernel, capacity),
        [shape(slots, 2 * tok_rows)] + [shape(2 * block, model_width)] * parts,
        2,
        [pltpu.VMEM((tok_rows, model_width), BF16)] * 2 + [pltpu.SemaphoreType.DMA((2,))],
        2,
    )(rank, host, route, route_b, tokens_b, cotangent_b, tokens, cotangent)
    got = [sent[0]] + [over_rep(sent[k], 2 * k) for k in range(1, parts)]
    first, second, first_1, second_2, pick = lax.optimization_barrier((first, second, first_1, second_2, pick))
    second_1, first_2 = over_own(second, 1), over_own(first, 2)
    first_3, second_3 = over_own(first_1, 2), over_own(second_2, 1)

    piece = [shape(half, 3 * width), shape(half, 3 * width, F32)]
    outs = call(
        functools.partial(main_kernel, parts),
        [shape(block, model_width)] * parts
        + [shape(depth, 3 * width, F32), piece[0], piece[1], piece[1], piece[0], piece[0], piece[0]],
        1,
        [pltpu.VMEM((slots, model_width), BF16)] * 2,
    )(own, *got, first, second, first_1, second_1, first_2, second_2, first_3, second_3)
    back, (own_term, one_a, one_b, two_a, two_b, three_a, three_b) = outs[:parts], outs[parts:]

    far_a, far_b = over_own(three_a, 1), over_own(three_b, 2)
    returned = [back[0]] + [over_rep(back[k], 2 * k) for k in range(1, parts)]
    got_1a, got_2b = over_own(one_a, 1), over_own(two_b, 2)
    got_2a = over_own((two_a + far_a.astype(F32)).astype(BF16), 2)
    got_1b = over_own((one_b + far_b.astype(F32)).astype(BF16), 1)

    mine, other = call(unpack_kernel, [shape(tok_rows, model_width)] * 2, 0)(pick, *returned)
    x_grad = mine + over_rep(other, 1)
    grads = call(sum_kernel, [shape(depth, width, F32)] * 3, 0)(own_term, got_1a, got_2a, got_1b, got_2b)
    return (x_grad, *(grad[None] for grad in grads))


def shards_whole(tokens, cotangent, route, host, w_gate, w_up, w_down_t):
    tok_rows, model_width = tokens.shape
    hot = host.shape[0]
    width = w_gate.shape[2]
    capacity = max(2, (3 * tok_rows + 2 * hot - 1) // (2 * hot))
    slots = hot * capacity
    labels = lax.broadcasted_iota(jnp.int32, (tok_rows, hot), 1)
    target = jnp.sum(jnp.where(route == labels, host[None, :], 0), axis=1)
    marked = (target[:, None] == labels).astype(jnp.int32)
    arrival = jnp.sum(jnp.cumsum(marked, axis=0) * marked, axis=1) - 1
    position = target * capacity + arrival
    pick = (lax.broadcasted_iota(jnp.int32, (slots, tok_rows), 0) == position[None, :]).astype(BF16)

    def exchange(value):
        split = value.astype(BF16).reshape(hot, capacity, model_width)
        return lax.all_to_all(split, "rep", split_axis=0, concat_axis=0, tiled=True).reshape(slots, model_width)

    slot_x, slot_dy = exchange(dot(pick, tokens, 1, 0)), exchange(dot(pick, cotangent, 1, 0))
    gate, up, down = (lax.all_gather(w[0], "own", axis=0, tiled=True) for w in (w_gate, w_up, w_down_t))
    gate_act, up_act, back_grad = dot(slot_x, gate, 1, 0), dot(slot_x, up, 1, 0), dot(slot_dy, down, 1, 0)
    sigmoid_g = jax.nn.sigmoid(gate_act)
    silu_gate = gate_act * sigmoid_g
    hidden = (silu_gate * up_act).astype(BF16)
    grad_gate_h = (back_grad * up_act * sigmoid_g * (1.0 + gate_act * (1.0 - sigmoid_g))).astype(BF16)
    grad_up_h = (back_grad * silu_gate).astype(BF16)
    returned = exchange(dot(grad_gate_h, gate, 1, 1) + dot(grad_up_h, up, 1, 1))
    x_grad = dot(pick, returned, 0, 0).astype(BF16)
    terms = [dot(slot_x, grad_gate_h, 0, 0), dot(slot_x, grad_up_h, 0, 0), dot(slot_dy, hidden, 0, 0)]
    summed = lax.psum_scatter(
        jnp.concatenate(terms, axis=1).astype(BF16), "own", scatter_dimension=0, tiled=True
    ).astype(F32)
    return (x_grad, *(summed[None, :, i * width : (i + 1) * width] for i in range(3)))


def solution(mesh):
    n_own, n_rep = mesh.shape["own"], mesh.shape["rep"]

    def shards(tokens, *rest):
        capacity = (3 * tokens.shape[0] + 2 * n_rep - 1) // (2 * n_rep)
        if n_own == 4 and n_rep & (n_rep - 1) == 0 and capacity % 8 == 0:
            return shards_by_partner(n_rep, tokens, *rest)
        return shards_whole(tokens, *rest)

    return jax.shard_map(
        shards,
        mesh=mesh,
        in_specs=(
            P(("own", "rep"), None),
            P(("own", "rep"), None),
            P(("own", "rep"), None),
            P(),
            P("rep", "own", None),
            P("rep", "own", None),
            P("rep", "own", None),
        ),
        out_specs=(
            P(("own", "rep"), None),
            P("rep", "own", None),
            P("rep", "own", None),
            P("rep", "own", None),
        ),
        check_vma=False,
    )
```

```python
import functools

import jax
import jax.numpy as jnp
from jax import lax
from jax.experimental import pallas as pl
from jax.experimental.pallas import tpu as pltpu
from jax.sharding import PartitionSpec as P

VMEM = pl.BlockSpec(memory_space=pltpu.VMEM)
SMEM = pl.BlockSpec(memory_space=pltpu.SMEM)
HBM = pl.BlockSpec(memory_space=pltpu.HBM)
MIB = 1024 * 1024
BF16 = jnp.bfloat16
F32 = jnp.float32


def dot(left, right, left_dim, right_dim):
    return lax.dot_general(
        left, right, (((left_dim,), (right_dim,)), ((), ())), preferred_element_type=F32
    )


def shape(rows, cols, dtype=BF16):
    return jax.ShapeDtypeStruct((rows, cols), dtype)


def call(kernel, outs, scalars=0, scratch=(), fetched=0, room=32):
    def run(*operands):
        placed = len(operands) - scalars - fetched
        moved = sum(value.size * value.dtype.itemsize for value in (*operands, *outs))
        return pl.pallas_call(
            kernel,
            out_shape=outs,
            in_specs=[SMEM] * scalars + [VMEM] * placed + [HBM] * fetched,
            out_specs=[VMEM] * len(outs),
            scratch_shapes=list(scratch),
            cost_estimate=pl.CostEstimate(flops=0, bytes_accessed=moved, transcendentals=0),
            compiler_params=pltpu.CompilerParams(vmem_limit_bytes=room * MIB),
        )(*operands)

    return run


def after(values, *earlier):
    return lax.optimization_barrier((values, earlier))[0]


def join_kernel(gate_ref, up_ref, down_ref, joined_ref, sems):
    depth = gate_ref.shape[0]
    loads = [
        pltpu.make_async_copy(source, joined_ref.at[pl.ds(i * depth, depth)], sems.at[i])
        for i, source in enumerate((gate_ref, up_ref, down_ref))
    ]
    for load in loads:
        load.start()
    for load in loads:
        load.wait()


def pack_kernel(capacity, rank_ref, host_ref, route_a, *refs):
    sources, outs, (route_b, x_a, x_b, dy_a, dy_b, sems) = refs[:5], refs[5:-6], refs[-6:]
    pick_ref, *send_refs = outs
    loads = [
        pltpu.make_async_copy(source, into, sems.at[i])
        for i, (source, into) in enumerate(zip(sources, (route_b, x_a, x_b, dy_a, dy_b)))
    ]
    for load in loads:
        load.start()
    hot = host_ref.shape[0]
    slots = pick_ref.shape[0]
    tokens = route_a.shape[1]
    block = 2 * capacity
    parts = slots // block
    label = lax.broadcasted_iota(jnp.int32, (hot, tokens), 0)
    base = jnp.zeros((hot, tokens), jnp.int32)
    for e in range(hot):
        apart = host_ref[e] ^ rank_ref[0]
        start = jnp.where((apart & 1) == 0, (apart >> 1) * block, -2 * slots)
        base = jnp.where(label == e, start, base)
    earlier = lax.broadcasted_iota(jnp.int32, (tokens, tokens), 0) < lax.broadcasted_iota(
        jnp.int32, (tokens, tokens), 1
    )
    earlier = jnp.where(earlier, 1.0, 0.0).astype(BF16)
    slot = lax.broadcasted_iota(jnp.int32, (slots, tokens), 0)

    def picks(route_ref, offset):
        marked = route_ref[...] == label
        before = dot(jnp.where(marked, 1.0, 0.0).astype(BF16), earlier, 1, 0).astype(jnp.int32)
        position = jnp.sum(jnp.where(marked, before + base, 0), axis=0, keepdims=True) + offset
        return jnp.where(slot == position, 1.0, 0.0).astype(BF16)

    pick_a = picks(route_a, 0)
    loads[0].wait()
    pick_b = picks(route_b, capacity)
    pick_ref[:, :tokens] = pick_a
    pick_ref[:, tokens:] = pick_b
    for at, (a, b) in enumerate(((x_a, x_b), (dy_a, dy_b))):
        loads[1 + 2 * at].wait()
        loads[2 + 2 * at].wait()
        filled = (dot(pick_a, a[...], 1, 0) + dot(pick_b, b[...], 1, 0)).astype(BF16)
        for k in range(parts):
            rows = filled[k * block : (k + 1) * block]
            if k < 2:
                send_refs[k][at * block : (at + 1) * block] = rows
            else:
                send_refs[2 * k - 2 + at][...] = rows


def columns_of(own_ref, depth):
    return [pl.ds(pl.multiple_of((own_ref[0] ^ k) * depth, depth), depth) for k in range(4)]


def spread_kernel(depth, own_ref, *refs):
    got, (x_ref, *piece_refs) = refs[:-5], refs[-5:]
    block = x_ref.shape[0] // len(got)
    columns = columns_of(own_ref, depth)
    for j, ref in enumerate(got):
        rows = slice(j * block, (j + 1) * block)
        x_ref[rows] = ref[:block]
        for k, piece_ref in enumerate(piece_refs):
            piece_ref[rows] = ref[:block, columns[k]]


def weight_rows(weights, k, start, rows):
    if k < 3:
        return weights[k][start : start + rows]
    split = weights[3].shape[0]
    half, start = divmod(start, split)
    return weights[3 + half][start : start + rows]


def act_kernel(*refs):
    own_ref, x_ref, weights, (gate_ref, up_ref) = refs[0], refs[1], refs[2:-2], refs[-2:]
    depth = weights[0].shape[0] // 3
    half = depth // 2
    gate_act = jnp.zeros(gate_ref.shape, F32)
    up_act = jnp.zeros(up_ref.shape, F32)
    for k, cols in enumerate(columns_of(own_ref, depth)):
        x = x_ref[:, cols]
        gate_act += dot(x, weight_rows(weights, k, 0, depth), 1, 0)
        up_act += dot(x[:, :half], weight_rows(weights, k, depth, half), 1, 0)
        up_act += dot(x[:, half:], weight_rows(weights, k, depth + half, half), 1, 0)
    gate_ref[...] = gate_act
    up_ref[...] = up_act


def grad_kernel(parts, own_ref, gate_ref, up_ref, *refs):
    got, weights, outs, dy_ref = refs[:parts], refs[parts : parts + 5], refs[parts + 5 : -1], refs[-1]
    back_refs, own_term, (own_grads, *messages) = outs[:parts], outs[parts], outs[parts + 1 :]
    slots, width = gate_ref.shape
    block = slots // parts
    depth = weights[0].shape[0] // 3
    half = depth // 2
    columns = columns_of(own_ref, depth)
    for j, ref in enumerate(got):
        dy_ref[j * block : (j + 1) * block] = ref[ref.shape[0] - block :]
    back_grad = sum(dot(dy_ref[:, columns[k]], weight_rows(weights, k, 2 * depth, depth), 1, 0) for k in range(4))
    gate_act, up_act = gate_ref[...], up_ref[...]
    sigmoid_g = jax.nn.sigmoid(gate_act)
    silu_gate = gate_act * sigmoid_g
    hidden = (silu_gate * up_act).astype(BF16)
    gate_h = (back_grad * up_act * sigmoid_g * (1.0 + gate_act * (1.0 - sigmoid_g))).astype(BF16)
    up_h = (back_grad * silu_gate).astype(BF16)
    for ref in (own_grads, *messages):
        ref[:slots, :width] = gate_h
        ref[:slots, width:] = up_h
    for k in range(4):
        term = dot(dy_ref[:, columns[k]], hidden, 0, 0)
        if k == 0:
            own_term[...] = term
        else:
            messages[k - 1][slots:, :width] = term[:half].astype(BF16)
            messages[k - 1][slots:, width:] = term[half:].astype(BF16)
    for k in range(4):
        for at in range(2):
            gate_rows = weight_rows(weights, k, at * half, half)
            up_rows = weight_rows(weights, k, depth + at * half, half)
            slot_grad = (dot(gate_h, gate_rows, 1, 1) + dot(up_h, up_rows, 1, 1)).astype(BF16)
            cols = pl.ds(pl.multiple_of((own_ref[0] ^ k) * depth + at * half, half), half)
            for j, back_ref in enumerate(back_refs):
                back_ref[:, cols] = slot_grad[j * block : (j + 1) * block]


def sum_kernel(*refs):
    pieces, messages, own_term, (gate_ref, up_ref, down_ref) = refs[:4], refs[4:8], refs[8], refs[9:]
    slots = pieces[0].shape[0]
    depth, width = gate_ref.shape
    half = depth // 2
    gate_ref[...] = sum(dot(piece[...], got[:slots, :width], 0, 0) for piece, got in zip(pieces, messages))
    up_ref[...] = sum(dot(piece[...], got[:slots, width:], 0, 0) for piece, got in zip(pieces, messages))
    for rows, cols in ((slice(0, half), slice(0, width)), (slice(half, depth), slice(width, 2 * width))):
        down_ref[rows] = own_term[rows] + sum(got[slots:, cols].astype(F32) for got in messages[1:])


def unpack_kernel(pick_ref, *refs):
    returned, (mine_ref, other_ref) = refs[:-2], refs[-2:]
    tokens = mine_ref.shape[0]
    block = returned[0].shape[0]
    for at, ref in enumerate((other_ref, mine_ref)):
        half = slice((1 - at) * tokens, (2 - at) * tokens)
        ref[...] = sum(
            dot(pick_ref[k * block : (k + 1) * block, half], part[...], 0, 0) for k, part in enumerate(returned)
        ).astype(BF16)


def shards_by_partner(n_rep, tokens, cotangent, route, host, w_gate, w_up, w_down_t):
    tok_rows, model_width = tokens.shape
    hot = host.shape[0]
    _, depth, width = w_gate.shape
    capacity = (3 * tok_rows + 2 * hot - 1) // (2 * hot)
    slots = hot * capacity
    parts = n_rep // 2
    block = 2 * capacity
    own = lax.axis_index("own").astype(jnp.int32).reshape(1)
    rank = lax.axis_index("rep").astype(jnp.int32).reshape(1)

    def over_own(value, k):
        return lax.ppermute(value, "own", [(i, i ^ k) for i in range(4)])

    def over_rep(value, k):
        return lax.ppermute(value, "rep", [(i, i ^ k) for i in range(n_rep)])

    route = route.reshape(1, tok_rows)
    route_b, tokens_b, cotangent_b = over_rep(route, 1), over_rep(tokens, 1), over_rep(cotangent, 1)
    joined = call(join_kernel, [shape(3 * depth, width)], 0, [pltpu.SemaphoreType.DMA((3,))], 3, 62)(
        w_gate[0], w_up[0], w_down_t[0]
    )[0]
    joined_1, joined_2 = over_own(joined, 1), over_own(joined, 2)

    token_rows = pltpu.VMEM((tok_rows, model_width), BF16)
    pick, *sent = call(
        functools.partial(pack_kernel, capacity),
        [shape(slots, 2 * tok_rows)]
        + [shape(2 * block, model_width)] * 2
        + [shape(block, model_width)] * (2 * parts - 4),
        2,
        [pltpu.VMEM((1, tok_rows), jnp.int32)] + [token_rows] * 4 + [pltpu.SemaphoreType.DMA((5,))],
        5,
        62,
    )(rank, host, route, route_b, tokens, tokens_b, cotangent, cotangent_b)
    far = range(2, parts)
    near = over_rep(sent[1], 2)
    far_x = [over_rep(sent[2 * k - 2], 2 * k) for k in far]
    (sent_dy, joined_1, joined_2) = after(
        ([sent[2 * k - 1] for k in far], joined_1, joined_2), near, *far_x
    )
    far_dy = [over_rep(value, 2 * k) for k, value in zip(far, sent_dy)]
    split = 3 * depth // 2
    joined_3 = [over_own(joined_1[:split], 2), over_own(joined_2[split:], 1)]

    x, *pieces = call(
        functools.partial(spread_kernel, depth), [shape(slots, model_width)] + [shape(slots, depth)] * 4, 1
    )(own, sent[0], near, *far_x)
    pieces = [pieces[0]] + [over_own(after(pieces[k], *joined_3), k) for k in range(1, 4)]
    weights = [joined, joined_1, joined_2, *joined_3]
    gate_act, up_act = call(act_kernel, [shape(slots, width, F32)] * 2, 1)(own, x, *weights)
    far_dy = after(far_dy, *pieces)
    message = shape(slots + depth // 2, 2 * width)
    outs = call(
        functools.partial(grad_kernel, parts),
        [shape(block, model_width)] * parts
        + [shape(depth, width, F32), shape(slots, 2 * width), message, message, message],
        1,
        [pltpu.VMEM((slots, model_width), BF16)],
    )(own, gate_act, up_act, sent[0], near, *far_dy, *weights)
    back, own_term, grads, messages = outs[:parts], outs[parts], outs[parts + 1], outs[parts + 2 :]
    returned = [over_rep(back[k], 2 * k) for k in range(1, parts)]
    messages = [over_own(messages[k - 1], k) for k in range(1, 4)]

    returned = after(returned, *messages)
    mine, other = call(unpack_kernel, [shape(tok_rows, model_width)] * 2)(pick, back[0], *returned)
    x_grad = mine + over_rep(other, 1)
    out = call(sum_kernel, [shape(depth, width, F32)] * 3)(*pieces, grads, *messages, own_term)
    return (x_grad, *(grad[None] for grad in out))


def shards_whole(tokens, cotangent, route, host, w_gate, w_up, w_down_t):
    tok_rows, model_width = tokens.shape
    hot = host.shape[0]
    width = w_gate.shape[2]
    capacity = max(2, (3 * tok_rows + 2 * hot - 1) // (2 * hot))
    slots = hot * capacity
    labels = lax.broadcasted_iota(jnp.int32, (tok_rows, hot), 1)
    target = jnp.sum(jnp.where(route == labels, host[None, :], 0), axis=1)
    marked = (target[:, None] == labels).astype(jnp.int32)
    arrival = jnp.sum(jnp.cumsum(marked, axis=0) * marked, axis=1) - 1
    position = target * capacity + arrival
    pick = (lax.broadcasted_iota(jnp.int32, (slots, tok_rows), 0) == position[None, :]).astype(BF16)

    def exchange(value):
        split = value.astype(BF16).reshape(hot, capacity, model_width)
        return lax.all_to_all(split, "rep", split_axis=0, concat_axis=0, tiled=True).reshape(slots, model_width)

    slot_x, slot_dy = exchange(dot(pick, tokens, 1, 0)), exchange(dot(pick, cotangent, 1, 0))
    gate, up, down = (lax.all_gather(w[0], "own", axis=0, tiled=True) for w in (w_gate, w_up, w_down_t))
    gate_act, up_act, back_grad = dot(slot_x, gate, 1, 0), dot(slot_x, up, 1, 0), dot(slot_dy, down, 1, 0)
    sigmoid_g = jax.nn.sigmoid(gate_act)
    silu_gate = gate_act * sigmoid_g
    hidden = (silu_gate * up_act).astype(BF16)
    grad_gate_h = (back_grad * up_act * sigmoid_g * (1.0 + gate_act * (1.0 - sigmoid_g))).astype(BF16)
    grad_up_h = (back_grad * silu_gate).astype(BF16)
    returned = exchange(dot(grad_gate_h, gate, 1, 1) + dot(grad_up_h, up, 1, 1))
    x_grad = dot(pick, returned, 0, 0).astype(BF16)
    terms = [dot(slot_x, grad_gate_h, 0, 0), dot(slot_x, grad_up_h, 0, 0), dot(slot_dy, hidden, 0, 0)]
    summed = lax.psum_scatter(
        jnp.concatenate(terms, axis=1).astype(BF16), "own", scatter_dimension=0, tiled=True
    ).astype(F32)
    return (x_grad, *(summed[None, :, i * width : (i + 1) * width] for i in range(3)))


def solution(mesh):
    n_own, n_rep = mesh.shape["own"], mesh.shape["rep"]

    def shards(tokens, *rest):
        capacity = (3 * tokens.shape[0] + 2 * n_rep - 1) // (2 * n_rep)
        if n_own == 4 and n_rep & (n_rep - 1) == 0 and capacity % 8 == 0:
            return shards_by_partner(n_rep, tokens, *rest)
        return shards_whole(tokens, *rest)

    return jax.shard_map(
        shards,
        mesh=mesh,
        in_specs=(
            P(("own", "rep"), None),
            P(("own", "rep"), None),
            P(("own", "rep"), None),
            P(),
            P("rep", "own", None),
            P("rep", "own", None),
            P("rep", "own", None),
        ),
        out_specs=(
            P(("own", "rep"), None),
            P("rep", "own", None),
            P("rep", "own", None),
            P("rep", "own", None),
        ),
        check_vma=False,
    )
```

```python
import functools

import jax
import jax.numpy as jnp
from jax import lax
from jax.experimental import pallas as pl
from jax.experimental.pallas import tpu as pltpu
from jax.sharding import PartitionSpec as P

VMEM = pl.BlockSpec(memory_space=pltpu.VMEM)
SMEM = pl.BlockSpec(memory_space=pltpu.SMEM)
HBM = pl.BlockSpec(memory_space=pltpu.HBM)
ANY = pl.BlockSpec(memory_space=pl.ANY)
MIB = 1024 * 1024
BF16 = jnp.bfloat16
F32 = jnp.float32


def dot(left, right, left_dim, right_dim):
    return lax.dot_general(
        left, right, (((left_dim,), (right_dim,)), ((), ())), preferred_element_type=F32
    )


def shape(rows, cols, dtype=BF16):
    return jax.ShapeDtypeStruct((rows, cols), dtype)


def call(kernel, outs, scalars=0, scratch=(), fetched=0, room=32, earlier=(), stored=()):
    earlier = list(earlier)

    def body(*refs):
        inputs = len(refs) - len(outs) - len(scratch)
        kernel(*refs[: inputs - len(earlier)], *refs[inputs:])

    def run(*operands):
        placed = len(operands) - scalars - fetched
        moved = sum(value.size * value.dtype.itemsize for value in (*operands, *outs))
        return pl.pallas_call(
            body,
            out_shape=outs,
            in_specs=[SMEM] * scalars + [VMEM] * placed + [HBM] * fetched + [ANY] * len(earlier),
            out_specs=[HBM if i in stored else VMEM for i in range(len(outs))],
            scratch_shapes=list(scratch),
            cost_estimate=pl.CostEstimate(flops=0, bytes_accessed=moved, transcendentals=0),
            compiler_params=pltpu.CompilerParams(vmem_limit_bytes=room * MIB),
        )(*operands, *earlier)

    return run


def after(values, *earlier):
    return pl.pallas_call(
        lambda *refs: None,
        out_shape=[shape(*value.shape, value.dtype) for value in values],
        in_specs=[HBM] * len(values) + [ANY] * len(earlier),
        out_specs=[HBM] * len(values),
        input_output_aliases={i: i for i in range(len(values))},
        compiler_params=pltpu.CompilerParams(vmem_limit_bytes=MIB),
    )(*values, *earlier)


def start_copies(pairs, sems):
    copies = [pltpu.make_async_copy(source, into, sems.at[i]) for i, (source, into) in enumerate(pairs)]
    for copy in copies:
        copy.start()
    return copies


def join_kernel(gate_ref, up_ref, down_ref, joined_ref, sems):
    depth = gate_ref.shape[0]
    rows = depth // 4
    copies = start_copies(
        [
            (source.at[pl.ds(at * rows, rows)], joined_ref.at[pl.ds(i * depth + at * rows, rows)])
            for i, source in enumerate((gate_ref, up_ref, down_ref))
            for at in range(4)
        ],
        sems,
    )
    for copy in copies:
        copy.wait()


def pack_kernel(capacity, rank_ref, host_ref, route_a, *refs):
    sources, outs, (route_b, x, dy, filled_x, filled_dy, sems, out_sems) = refs[:5], refs[5:-7], refs[-7:]
    pick_ref, *send_refs = outs
    tokens = route_a.shape[1]
    own_rows, other_rows = pl.ds(0, tokens), pl.ds(tokens, tokens)
    loads = start_copies(
        zip(sources, (route_b, x.at[own_rows], x.at[other_rows], dy.at[own_rows], dy.at[other_rows])), sems
    )
    hot = host_ref.shape[0]
    slots = pick_ref.shape[0]
    block = 2 * capacity
    parts = slots // block
    label = lax.broadcasted_iota(jnp.int32, (hot, tokens), 0)
    base = jnp.zeros((hot, tokens), jnp.int32)
    for e in range(hot):
        apart = host_ref[e] ^ rank_ref[0]
        start = jnp.where((apart & 1) == 0, (apart >> 1) * block, -2 * slots)
        base = jnp.where(label == e, start, base)
    earlier = lax.broadcasted_iota(jnp.int32, (tokens, tokens), 0) < lax.broadcasted_iota(
        jnp.int32, (tokens, tokens), 1
    )
    earlier = jnp.where(earlier, 1.0, 0.0).astype(BF16)
    slot = lax.broadcasted_iota(jnp.int32, (slots, tokens), 0)

    def picks(route_ref, offset):
        marked = route_ref[...] == label
        before = dot(jnp.where(marked, 1.0, 0.0).astype(BF16), earlier, 1, 0).astype(jnp.int32)
        position = jnp.sum(jnp.where(marked, before + base, 0), axis=0, keepdims=True) + offset
        return jnp.where(slot == position, 1.0, 0.0).astype(BF16)

    pick_ref[:, :tokens] = picks(route_a, 0)
    loads[0].wait()
    pick_ref[:, tokens:] = picks(route_b, capacity)
    stores = []
    for at, (rows, filled) in enumerate(((x, filled_x), (dy, filled_dy))):
        loads[1 + 2 * at].wait()
        loads[2 + 2 * at].wait()
        filled[...] = dot(pick_ref[...], rows[...], 1, 0).astype(BF16)
        targets = [ref.at[pl.ds(at * block, block)] for ref in send_refs[:2]] + send_refs[2 + at :: 2]
        stores += start_copies(
            [(filled.at[pl.ds(k * block, block)], target) for k, target in enumerate(targets)],
            out_sems.at[at],
        )
    for store in stores:
        store.wait()


def columns_of(own_ref, depth):
    return [pl.ds(pl.multiple_of((own_ref[0] ^ k) * depth, depth), depth) for k in range(4)]


def spread_kernel(depth, own_ref, *refs):
    got, (x_ref, *piece_refs) = refs[:-5], refs[-5:]
    block = x_ref.shape[0] // len(got)
    columns = columns_of(own_ref, depth)
    for j, ref in enumerate(got):
        rows = slice(j * block, (j + 1) * block)
        x_ref[rows] = ref[:block]
        for k, piece_ref in enumerate(piece_refs):
            piece_ref[rows] = ref[:block, columns[k]]


def weight_rows(weights, k, start, rows):
    if k < 3:
        return weights[k][start : start + rows]
    split = weights[3].shape[0]
    half, start = divmod(start, split)
    return weights[3 + half][start : start + rows]


def hidden_grads(gate_act, up_act, back_grad):
    sigmoid_g = jax.nn.sigmoid(gate_act)
    silu_gate = gate_act * sigmoid_g
    gate_h = back_grad * up_act * sigmoid_g * (1.0 + gate_act * (1.0 - sigmoid_g))
    return (silu_gate * up_act).astype(BF16), gate_h.astype(BF16), (back_grad * silu_gate).astype(BF16)


def back_columns(own_ref, weights, gate_h, up_h, back_refs):
    depth = weights[0].shape[0] // 3
    half = depth // 2
    block = back_refs[0].shape[0]
    for k in range(4):
        for at in range(2):
            gate_rows = weight_rows(weights, k, at * half, half)
            up_rows = weight_rows(weights, k, depth + at * half, half)
            slot_grad = (dot(gate_h, gate_rows, 1, 1) + dot(up_h, up_rows, 1, 1)).astype(BF16)
            cols = pl.ds(pl.multiple_of((own_ref[0] ^ k) * depth + at * half, half), half)
            for j, back_ref in enumerate(back_refs):
                back_ref[:, cols] = slot_grad[j * block : (j + 1) * block]


def near_kernel(own_ref, x_ref, *refs):
    got, weights, outs, dy_ref = refs[:2], refs[2:7], refs[7:-1], refs[-1]
    gate_ref, up_ref, grads_ref, hidden_ref, *back_refs = outs
    near, width = hidden_ref.shape
    block = near // 2
    depth = weights[0].shape[0] // 3
    half = depth // 2
    gate_act = jnp.zeros((x_ref.shape[0], width), F32)
    up_act = jnp.zeros((x_ref.shape[0], width), F32)
    back_grad = jnp.zeros((near, width), F32)
    for j, ref in enumerate(got):
        dy_ref[j * block : (j + 1) * block] = ref[block:]
    for k, cols in enumerate(columns_of(own_ref, depth)):
        x = x_ref[:, cols]
        gate_act += dot(x, weight_rows(weights, k, 0, depth), 1, 0)
        up_act += dot(x[:, :half], weight_rows(weights, k, depth, half), 1, 0)
        up_act += dot(x[:, half:], weight_rows(weights, k, depth + half, half), 1, 0)
        back_grad += dot(dy_ref[:, cols], weight_rows(weights, k, 2 * depth, depth), 1, 0)
    gate_ref[...] = gate_act[near:]
    up_ref[...] = up_act[near:]
    hidden, gate_h, up_h = hidden_grads(gate_act[:near], up_act[:near], back_grad)
    hidden_ref[...] = hidden
    grads_ref[:, :width] = gate_h
    grads_ref[:, width:] = up_h
    back_columns(own_ref, weights, gate_h, up_h, back_refs)


def far_kernel(own_ref, gate_ref, up_ref, near_grads, near_hidden, *refs):
    got, weights, outs, (dy_ref, hidden_ref) = refs[:4], refs[4:9], refs[9:-2], refs[-2:]
    back_refs, own_term, (own_grads, *messages) = outs[:2], outs[2], outs[3:]
    near, width = near_hidden.shape
    slots = dy_ref.shape[0]
    block = near // 2
    depth = weights[0].shape[0] // 3
    half = depth // 2
    columns = columns_of(own_ref, depth)
    for j, ref in enumerate(got):
        dy_ref[j * block : (j + 1) * block] = ref[ref.shape[0] - block :]
    back_grad = sum(
        dot(dy_ref[near:, columns[k]], weight_rows(weights, k, 2 * depth, depth), 1, 0) for k in range(4)
    )
    hidden, gate_h, up_h = hidden_grads(gate_ref[...], up_ref[...], back_grad)
    hidden_ref[:near] = near_hidden[...]
    hidden_ref[near:] = hidden
    for ref in (own_grads, *messages):
        ref[:near] = near_grads[...]
        ref[near:slots, :width] = gate_h
        ref[near:slots, width:] = up_h
    for k in range(4):
        term = dot(dy_ref[:, columns[k]], hidden_ref[...], 0, 0)
        if k == 0:
            own_term[...] = term
        else:
            messages[k - 1][slots:, :width] = term[:half].astype(BF16)
            messages[k - 1][slots:, width:] = term[half:].astype(BF16)
    back_columns(own_ref, weights, gate_h, up_h, back_refs)


def sum_kernel(*refs):
    pieces, messages, own_term, (gate_ref, up_ref, down_ref) = refs[:4], refs[4:8], refs[8], refs[9:]
    slots = pieces[0].shape[0]
    depth, width = gate_ref.shape
    half = depth // 2
    gate_ref[...] = sum(dot(piece[...], got[:slots, :width], 0, 0) for piece, got in zip(pieces, messages))
    up_ref[...] = sum(dot(piece[...], got[:slots, width:], 0, 0) for piece, got in zip(pieces, messages))
    for rows, cols in ((slice(0, half), slice(0, width)), (slice(half, depth), slice(width, 2 * width))):
        down_ref[rows] = own_term[rows] + sum(got[slots:, cols].astype(F32) for got in messages[1:])


def unpack_kernel(pick_ref, *refs):
    returned, (mine_ref, other_ref) = refs[:-2], refs[-2:]
    tokens = mine_ref.shape[0]
    block = returned[0].shape[0]
    for at, ref in enumerate((other_ref, mine_ref)):
        half = slice((1 - at) * tokens, (2 - at) * tokens)
        ref[...] = sum(
            dot(pick_ref[k * block : (k + 1) * block, half], part[...], 0, 0) for k, part in enumerate(returned)
        ).astype(BF16)


def shards_by_partner(n_rep, tokens, cotangent, route, host, w_gate, w_up, w_down_t):
    tok_rows, model_width = tokens.shape
    hot = host.shape[0]
    _, depth, width = w_gate.shape
    capacity = (3 * tok_rows + 2 * hot - 1) // (2 * hot)
    slots = hot * capacity
    parts = n_rep // 2
    block = 2 * capacity
    own = lax.axis_index("own").astype(jnp.int32).reshape(1)
    rank = lax.axis_index("rep").astype(jnp.int32).reshape(1)

    def over_own(value, k):
        return lax.ppermute(value, "own", [(i, i ^ k) for i in range(4)])

    def over_rep(value, k):
        return lax.ppermute(value, "rep", [(i, i ^ k) for i in range(n_rep)])

    route = route.reshape(1, tok_rows)
    route_b, tokens_b, cotangent_b = over_rep(route, 1), over_rep(tokens, 1), over_rep(cotangent, 1)
    joined = call(
        join_kernel, [shape(3 * depth, width)], 0, [pltpu.SemaphoreType.DMA((12,))], 3, 62, (), [0]
    )(w_gate[0], w_up[0], w_down_t[0])[0]

    token_rows = pltpu.VMEM((2 * tok_rows, model_width), BF16)
    slot_rows = pltpu.VMEM((slots, model_width), BF16)
    dma = pltpu.SemaphoreType.DMA
    pick, *sent = call(
        functools.partial(pack_kernel, capacity),
        [shape(slots, 2 * tok_rows)] + [shape(2 * block, model_width)] * 2 + [shape(block, model_width)] * 4,
        2,
        [pltpu.VMEM((1, tok_rows), jnp.int32)]
        + [token_rows, token_rows, slot_rows, slot_rows, dma((5,)), dma((2, parts))],
        5,
        62,
        (),
        range(1, 7),
    )(rank, host, route, route_b, tokens, tokens_b, cotangent, cotangent_b)
    near = over_rep(sent[1], 2)
    far_x = [over_rep(sent[2], 4), over_rep(sent[4], 6)]
    joined = after([joined], pick)[0]
    joined_1, joined_2 = over_own(joined, 1), over_own(joined, 2)
    split = 3 * depth // 2
    *far_dy, onward_1, onward_2 = after([sent[3], sent[5], joined_1[:split], joined_2[split:]], *far_x)
    far_dy = [over_rep(far_dy[0], 4), over_rep(far_dy[1], 6)]
    joined_3 = [over_own(onward_1, 2), over_own(onward_2, 1)]
    weights = [joined, joined_1, joined_2, *joined_3]

    x, *pieces = call(
        functools.partial(spread_kernel, depth),
        [shape(slots, model_width)] + [shape(slots, depth)] * 4,
        1,
        earlier=joined_3,
    )(own, sent[0], near, *far_x)
    pieces = [pieces[0]] + [over_own(pieces[k], k) for k in range(1, 4)]
    acts = shape(block * 2, width, F32)
    gate_act, up_act, near_grads, near_hidden, *back = call(
        near_kernel,
        [acts, acts, shape(2 * block, 2 * width), shape(2 * block, width)] + [shape(block, model_width)] * 2,
        1,
        [pltpu.VMEM((2 * block, model_width), BF16)],
    )(own, x, sent[0], near, *weights)
    returned = [back[0], over_rep(back[1], 2)]
    message = shape(slots + depth // 2, 2 * width)
    *back, own_term, grads, message_1, message_2, message_3 = call(
        far_kernel,
        [shape(block, model_width)] * 2
        + [shape(depth, width, F32), shape(slots, 2 * width), message, message, message],
        1,
        [pltpu.VMEM((slots, model_width), BF16), pltpu.VMEM((slots, width), BF16)],
        earlier=[*pieces[1:], returned[1]],
    )(own, gate_act, up_act, near_grads, near_hidden, sent[0], near, *far_dy, *weights)
    returned += [over_rep(back[0], 4), over_rep(back[1], 6)]
    messages = [over_own(message_1, 1), over_own(message_2, 2), over_own(message_3, 3)]

    mine, other = call(unpack_kernel, [shape(tok_rows, model_width)] * 2, earlier=messages)(pick, *returned)
    x_grad = mine + over_rep(other, 1)
    out = call(sum_kernel, [shape(depth, width, F32)] * 3)(*pieces, grads, *messages, own_term)
    return (x_grad, *(grad[None] for grad in out))


def shards_whole(tokens, cotangent, route, host, w_gate, w_up, w_down_t):
    tok_rows, model_width = tokens.shape
    hot = host.shape[0]
    width = w_gate.shape[2]
    capacity = max(2, (3 * tok_rows + 2 * hot - 1) // (2 * hot))
    slots = hot * capacity
    labels = lax.broadcasted_iota(jnp.int32, (tok_rows, hot), 1)
    target = jnp.sum(jnp.where(route == labels, host[None, :], 0), axis=1)
    marked = (target[:, None] == labels).astype(jnp.int32)
    arrival = jnp.sum(jnp.cumsum(marked, axis=0) * marked, axis=1) - 1
    position = target * capacity + arrival
    pick = (lax.broadcasted_iota(jnp.int32, (slots, tok_rows), 0) == position[None, :]).astype(BF16)

    def exchange(value):
        split = value.astype(BF16).reshape(hot, capacity, model_width)
        return lax.all_to_all(split, "rep", split_axis=0, concat_axis=0, tiled=True).reshape(slots, model_width)

    slot_x, slot_dy = exchange(dot(pick, tokens, 1, 0)), exchange(dot(pick, cotangent, 1, 0))
    gate, up, down = (lax.all_gather(w[0], "own", axis=0, tiled=True) for w in (w_gate, w_up, w_down_t))
    gate_act, up_act, back_grad = dot(slot_x, gate, 1, 0), dot(slot_x, up, 1, 0), dot(slot_dy, down, 1, 0)
    sigmoid_g = jax.nn.sigmoid(gate_act)
    silu_gate = gate_act * sigmoid_g
    hidden = (silu_gate * up_act).astype(BF16)
    grad_gate_h = (back_grad * up_act * sigmoid_g * (1.0 + gate_act * (1.0 - sigmoid_g))).astype(BF16)
    grad_up_h = (back_grad * silu_gate).astype(BF16)
    returned = exchange(dot(grad_gate_h, gate, 1, 1) + dot(grad_up_h, up, 1, 1))
    x_grad = dot(pick, returned, 0, 0).astype(BF16)
    terms = [dot(slot_x, grad_gate_h, 0, 0), dot(slot_x, grad_up_h, 0, 0), dot(slot_dy, hidden, 0, 0)]
    summed = lax.psum_scatter(
        jnp.concatenate(terms, axis=1).astype(BF16), "own", scatter_dimension=0, tiled=True
    ).astype(F32)
    return (x_grad, *(summed[None, :, i * width : (i + 1) * width] for i in range(3)))


def solution(mesh):
    n_own, n_rep = mesh.shape["own"], mesh.shape["rep"]

    def shards(tokens, *rest):
        capacity = (3 * tokens.shape[0] + 2 * n_rep - 1) // (2 * n_rep)
        if n_own == 4 and n_rep == 8 and capacity % 8 == 0:
            return shards_by_partner(n_rep, tokens, *rest)
        return shards_whole(tokens, *rest)

    return jax.shard_map(
        shards,
        mesh=mesh,
        in_specs=(
            P(("own", "rep"), None),
            P(("own", "rep"), None),
            P(("own", "rep"), None),
            P(),
            P("rep", "own", None),
            P("rep", "own", None),
            P("rep", "own", None),
        ),
        out_specs=(
            P(("own", "rep"), None),
            P("rep", "own", None),
            P("rep", "own", None),
            P("rep", "own", None),
        ),
        check_vma=False,
    )
```

```python
import functools

import jax
import jax.numpy as jnp
from jax import lax
from jax.experimental import pallas as pl
from jax.experimental.pallas import tpu as pltpu
from jax.sharding import PartitionSpec as P

VMEM = pl.BlockSpec(memory_space=pltpu.VMEM)
SMEM = pl.BlockSpec(memory_space=pltpu.SMEM)
HBM = pl.BlockSpec(memory_space=pltpu.HBM)
ANY = pl.BlockSpec(memory_space=pl.ANY)
MIB = 1024 * 1024
BF16 = jnp.bfloat16
F32 = jnp.float32


def dot(left, right, left_dim, right_dim):
    return lax.dot_general(
        left, right, (((left_dim,), (right_dim,)), ((), ())), preferred_element_type=F32
    )


def shape(rows, cols, dtype=BF16):
    return jax.ShapeDtypeStruct((rows, cols), dtype)


def call(kernel, outs, scalars=0, scratch=(), fetched=0, room=32, earlier=(), stored=()):
    earlier = list(earlier)

    def body(*refs):
        inputs = len(refs) - len(outs) - len(scratch)
        kernel(*refs[: inputs - len(earlier)], *refs[inputs:])

    def run(*operands):
        placed = len(operands) - scalars - fetched
        moved = sum(value.size * value.dtype.itemsize for value in (*operands, *outs))
        return pl.pallas_call(
            body,
            out_shape=outs,
            in_specs=[SMEM] * scalars + [VMEM] * placed + [HBM] * fetched + [ANY] * len(earlier),
            out_specs=[HBM if i in stored else VMEM for i in range(len(outs))],
            scratch_shapes=list(scratch),
            cost_estimate=pl.CostEstimate(flops=0, bytes_accessed=moved, transcendentals=0),
            compiler_params=pltpu.CompilerParams(vmem_limit_bytes=room * MIB),
        )(*operands, *earlier)

    return run


def after(values, *earlier):
    return pl.pallas_call(
        lambda *refs: None,
        out_shape=[shape(*value.shape, value.dtype) for value in values],
        in_specs=[ANY] * (len(values) + len(earlier)),
        out_specs=[ANY] * len(values),
        input_output_aliases={i: i for i in range(len(values))},
        compiler_params=pltpu.CompilerParams(vmem_limit_bytes=MIB),
    )(*values, *earlier)


def start_copies(pairs, sems):
    copies = [pltpu.make_async_copy(source, into, sems.at[i]) for i, (source, into) in enumerate(pairs)]
    for copy in copies:
        copy.start()
    return copies


def pack_kernel(capacity, rank_ref, host_ref, route_a, *refs):
    sources, outs, (route_b, x, filled, weights, sems, out_sems) = refs[:6], refs[6:-6], refs[-6:]
    pick_ref, joined_ref, *send_refs = outs
    tokens = route_a.shape[1]
    width = weights.shape[1] // 3
    loads = start_copies(
        zip(
            sources,
            (route_b, x.at[pl.ds(0, tokens)], x.at[pl.ds(tokens, tokens)])
            + tuple(weights.at[:, pl.ds(i * width, width)] for i in range(3)),
        ),
        sems,
    )
    hot = host_ref.shape[0]
    slots = pick_ref.shape[0]
    block = 2 * capacity
    label = lax.broadcasted_iota(jnp.int32, (hot, tokens), 0)
    base = jnp.zeros((hot, tokens), jnp.int32)
    for e in range(hot):
        apart = host_ref[e] ^ rank_ref[0]
        start = jnp.where((apart & 1) == 0, (apart >> 1) * block, -2 * slots)
        base = jnp.where(label == e, start, base)
    earlier = lax.broadcasted_iota(jnp.int32, (tokens, tokens), 0) < lax.broadcasted_iota(
        jnp.int32, (tokens, tokens), 1
    )
    earlier = jnp.where(earlier, 1.0, 0.0).astype(BF16)
    slot = lax.broadcasted_iota(jnp.int32, (slots, tokens), 0)

    def picks(route_ref, offset):
        marked = route_ref[...] == label
        before = dot(jnp.where(marked, 1.0, 0.0).astype(BF16), earlier, 1, 0).astype(jnp.int32)
        position = jnp.sum(jnp.where(marked, before + base, 0), axis=0, keepdims=True) + offset
        return jnp.where(slot == position, 1.0, 0.0).astype(BF16)

    pick_ref[:, :tokens] = picks(route_a, 0)
    loads[0].wait()
    pick_ref[:, tokens:] = picks(route_b, capacity)
    loads[1].wait()
    loads[2].wait()
    filled[...] = dot(pick_ref[...], x[...], 1, 0).astype(BF16)
    for load in loads[3:]:
        load.wait()
    stores = start_copies(
        [(filled.at[pl.ds(k * block, block)], ref) for k, ref in enumerate(send_refs)] + [(weights, joined_ref)],
        out_sems,
    )
    for store in stores:
        store.wait()


def pack_more_kernel(pick_ref, *refs):
    sources, send_refs, (rows, filled, sems, out_sems) = refs[:2], refs[2:-4], refs[-4:]
    tokens = sources[0].shape[0]
    block = send_refs[0].shape[0]
    loads = start_copies(zip(sources, (rows.at[pl.ds(0, tokens)], rows.at[pl.ds(tokens, tokens)])), sems)
    for load in loads:
        load.wait()
    filled[...] = dot(pick_ref[...], rows[...], 1, 0).astype(BF16)
    stores = start_copies(
        [(filled.at[pl.ds(k * block, block)], ref) for k, ref in enumerate(send_refs)], out_sems
    )
    for store in stores:
        store.wait()


def weight_parts(own_ref, weights):
    depth = weights[0].shape[0]
    half = depth // 2
    for k, ref in enumerate(weights):
        partner, start = (k, 0) if k < 3 else (3, (k - 3) * half)
        yield pl.ds(pl.multiple_of((own_ref[0] ^ partner) * depth + start, half), ref.shape[0]), ref


def columns_of(own_ref, depth):
    return [pl.ds(pl.multiple_of((own_ref[0] ^ k) * depth, depth), depth) for k in range(4)]


def spread_kernel(own_ref, *refs):
    got, (x_ref, *piece_refs) = refs[:-5], refs[-5:]
    block = got[0].shape[0]
    columns = columns_of(own_ref, piece_refs[0].shape[1])
    for j, ref in enumerate(got):
        rows = slice(j * block, (j + 1) * block)
        x_ref[rows] = ref[...]
        for k, piece_ref in enumerate(piece_refs):
            piece_ref[rows] = ref[:, columns[k]]


def act_kernel(own_ref, x_ref, *refs):
    weights, acts_ref = refs[:-1], refs[-1]
    both = acts_ref.shape[1]
    acts_ref[...] = sum(dot(x_ref[:, cols], ref[:, :both], 1, 0) for cols, ref in weight_parts(own_ref, weights))


def grad_kernel(parts, own_ref, acts_ref, *refs):
    got, weights, outs, dy_ref = refs[:parts], refs[parts : parts + 5], refs[parts + 5 : -1], refs[-1]
    back_refs, own_term, (own_grads, *messages) = outs[:parts], outs[parts], outs[parts + 1 :]
    slots, both = acts_ref.shape
    width = both // 2
    block = slots // parts
    depth = weights[0].shape[0]
    half = depth // 2
    for j, ref in enumerate(got):
        dy_ref[j * block : (j + 1) * block] = ref[...]
    back_grad = sum(dot(dy_ref[:, cols], ref[:, both:], 1, 0) for cols, ref in weight_parts(own_ref, weights))
    gate_act, up_act = acts_ref[:, :width], acts_ref[:, width:]
    sigmoid_g = jax.nn.sigmoid(gate_act)
    silu_gate = gate_act * sigmoid_g
    hidden = (silu_gate * up_act).astype(BF16)
    gate_h = back_grad * up_act * sigmoid_g * (1.0 + gate_act * (1.0 - sigmoid_g))
    own_grads[:, :width] = gate_h.astype(BF16)
    own_grads[:, width:] = (back_grad * silu_gate).astype(BF16)
    grads = own_grads[...]
    for k, cols in enumerate(columns_of(own_ref, depth)):
        term = dot(dy_ref[:, cols], hidden, 0, 0)
        if k == 0:
            own_term[...] = term
        else:
            messages[k - 1][:slots] = grads
            messages[k - 1][slots:, :width] = term[:half].astype(BF16)
            messages[k - 1][slots:, width:] = term[half:].astype(BF16)
    for cols, ref in weight_parts(own_ref, weights):
        slot_grad = dot(grads, ref[:, :both], 1, 1).astype(BF16)
        for j, back_ref in enumerate(back_refs):
            back_ref[:, cols] = slot_grad[j * block : (j + 1) * block]


def sum_kernel(*refs):
    pieces, messages, own_term, (gate_ref, up_ref, down_ref) = refs[:4], refs[4:8], refs[8], refs[9:]
    slots = pieces[0].shape[0]
    depth, width = gate_ref.shape
    half = depth // 2
    total = sum(dot(piece[...], got[:slots], 0, 0) for piece, got in zip(pieces, messages))
    gate_ref[...] = total[:, :width]
    up_ref[...] = total[:, width:]
    for rows, cols in ((slice(0, half), slice(0, width)), (slice(half, depth), slice(width, 2 * width))):
        down_ref[rows] = own_term[rows] + sum(got[slots:, cols].astype(F32) for got in messages[1:])


def unpack_kernel(pick_ref, *refs):
    returned, (mine_ref, other_ref) = refs[:-2], refs[-2:]
    tokens = mine_ref.shape[0]
    block = returned[0].shape[0]
    for at, ref in enumerate((other_ref, mine_ref)):
        half = slice((1 - at) * tokens, (2 - at) * tokens)
        ref[...] = sum(
            dot(pick_ref[k * block : (k + 1) * block, half], part[...], 0, 0) for k, part in enumerate(returned)
        ).astype(BF16)


def shards_by_partner(n_rep, tokens, cotangent, route, host, w_gate, w_up, w_down_t):
    tok_rows, model_width = tokens.shape
    hot = host.shape[0]
    _, depth, width = w_gate.shape
    capacity = (3 * tok_rows + 2 * hot - 1) // (2 * hot)
    slots = hot * capacity
    parts = n_rep // 2
    block = 2 * capacity
    own = lax.axis_index("own").astype(jnp.int32).reshape(1)
    rank = lax.axis_index("rep").astype(jnp.int32).reshape(1)

    def over_own(value, k):
        return lax.ppermute(value, "own", [(i, i ^ k) for i in range(4)])

    def over_rep(value, k):
        return lax.ppermute(value, "rep", [(i, i ^ k) for i in range(n_rep)])

    route = route.reshape(1, tok_rows)
    route_b, tokens_b, cotangent_b = over_rep(route, 1), over_rep(tokens, 1), over_rep(cotangent, 1)
    token_rows = pltpu.VMEM((2 * tok_rows, model_width), BF16)
    slot_rows = pltpu.VMEM((slots, model_width), BF16)
    dma = pltpu.SemaphoreType.DMA
    pick, joined, *sent_x = call(
        functools.partial(pack_kernel, capacity),
        [shape(slots, 2 * tok_rows), shape(depth, 3 * width)] + [shape(block, model_width)] * parts,
        2,
        [pltpu.VMEM((1, tok_rows), jnp.int32), token_rows, slot_rows, pltpu.VMEM((depth, 3 * width), BF16)]
        + [dma((6,)), dma((parts + 1,))],
        6,
        62,
        [cotangent_b],
        range(1, 2 + parts),
    )(rank, host, route, route_b, tokens, tokens_b, w_gate[0], w_up[0], w_down_t[0])
    got_x = [over_rep(sent_x[k], 2 * k) for k in range(1, parts)]
    joined_1, joined_2 = over_own(joined, 1), over_own(joined, 2)
    sent_dy = call(
        pack_more_kernel,
        [shape(block, model_width)] * parts,
        0,
        [token_rows, slot_rows, dma((2,)), dma((parts,))],
        2,
        62,
        (),
        range(parts),
    )(pick, cotangent, cotangent_b)
    *far_dy, onward_1, onward_2 = after(
        [*sent_dy[1:], joined_1[: depth // 2], joined_2[depth // 2 :]], *got_x
    )
    got_dy = [over_rep(far_dy[k - 1], 2 * k) for k in range(1, parts)]
    joined_3 = [over_own(onward_1, 2), over_own(onward_2, 1)]
    weights = [joined, joined_1, joined_2, *joined_3]

    x, *pieces = call(
        spread_kernel, [shape(slots, model_width)] + [shape(slots, depth)] * 4, 1, earlier=joined_3
    )(own, sent_x[0], *got_x)
    pieces = [pieces[0]] + [over_own(pieces[k], k) for k in range(1, 4)]
    acts = call(act_kernel, [shape(slots, 2 * width, F32)], 1)(own, x, *weights)[0]
    message = shape(slots + depth // 2, 2 * width)
    outs = call(
        functools.partial(grad_kernel, parts),
        [shape(block, model_width)] * parts
        + [shape(depth, width, F32), shape(slots, 2 * width), message, message, message],
        1,
        [slot_rows],
        earlier=pieces[1:],
    )(own, acts, sent_dy[0], *got_dy, *weights)
    back, own_term, grads, messages = outs[:parts], outs[parts], outs[parts + 1], outs[parts + 2 :]
    returned = [back[0]] + [over_rep(back[k], 2 * k) for k in range(1, parts)]
    messages = [over_own(messages[k - 1], k) for k in range(1, 4)]

    mine, other = call(unpack_kernel, [shape(tok_rows, model_width)] * 2, earlier=messages)(pick, *returned)
    x_grad = mine + over_rep(other, 1)
    out = call(sum_kernel, [shape(depth, width, F32)] * 3)(*pieces, grads, *messages, own_term)
    return (x_grad, *(grad[None] for grad in out))


def shards_whole(tokens, cotangent, route, host, w_gate, w_up, w_down_t):
    tok_rows, model_width = tokens.shape
    hot = host.shape[0]
    width = w_gate.shape[2]
    capacity = max(2, (3 * tok_rows + 2 * hot - 1) // (2 * hot))
    slots = hot * capacity
    labels = lax.broadcasted_iota(jnp.int32, (tok_rows, hot), 1)
    target = jnp.sum(jnp.where(route == labels, host[None, :], 0), axis=1)
    marked = (target[:, None] == labels).astype(jnp.int32)
    arrival = jnp.sum(jnp.cumsum(marked, axis=0) * marked, axis=1) - 1
    position = target * capacity + arrival
    pick = (lax.broadcasted_iota(jnp.int32, (slots, tok_rows), 0) == position[None, :]).astype(BF16)

    def exchange(value):
        split = value.astype(BF16).reshape(hot, capacity, model_width)
        return lax.all_to_all(split, "rep", split_axis=0, concat_axis=0, tiled=True).reshape(slots, model_width)

    slot_x, slot_dy = exchange(dot(pick, tokens, 1, 0)), exchange(dot(pick, cotangent, 1, 0))
    gate, up, down = (lax.all_gather(w[0], "own", axis=0, tiled=True) for w in (w_gate, w_up, w_down_t))
    gate_act, up_act, back_grad = dot(slot_x, gate, 1, 0), dot(slot_x, up, 1, 0), dot(slot_dy, down, 1, 0)
    sigmoid_g = jax.nn.sigmoid(gate_act)
    silu_gate = gate_act * sigmoid_g
    hidden = (silu_gate * up_act).astype(BF16)
    grad_gate_h = (back_grad * up_act * sigmoid_g * (1.0 + gate_act * (1.0 - sigmoid_g))).astype(BF16)
    grad_up_h = (back_grad * silu_gate).astype(BF16)
    returned = exchange(dot(grad_gate_h, gate, 1, 1) + dot(grad_up_h, up, 1, 1))
    x_grad = dot(pick, returned, 0, 0).astype(BF16)
    terms = [dot(slot_x, grad_gate_h, 0, 0), dot(slot_x, grad_up_h, 0, 0), dot(slot_dy, hidden, 0, 0)]
    summed = lax.psum_scatter(
        jnp.concatenate(terms, axis=1).astype(BF16), "own", scatter_dimension=0, tiled=True
    ).astype(F32)
    return (x_grad, *(summed[None, :, i * width : (i + 1) * width] for i in range(3)))


def solution(mesh):
    n_own, n_rep = mesh.shape["own"], mesh.shape["rep"]

    def shards(tokens, *rest):
        capacity = (3 * tokens.shape[0] + 2 * n_rep - 1) // (2 * n_rep)
        if n_own == 4 and n_rep == 8 and capacity % 8 == 0:
            return shards_by_partner(n_rep, tokens, *rest)
        return shards_whole(tokens, *rest)

    return jax.shard_map(
        shards,
        mesh=mesh,
        in_specs=(
            P(("own", "rep"), None),
            P(("own", "rep"), None),
            P(("own", "rep"), None),
            P(),
            P("rep", "own", None),
            P("rep", "own", None),
            P("rep", "own", None),
        ),
        out_specs=(
            P(("own", "rep"), None),
            P("rep", "own", None),
            P("rep", "own", None),
            P("rep", "own", None),
        ),
        check_vma=False,
    )
```

```python
import functools

import jax
import jax.numpy as jnp
from jax import lax
from jax.experimental import pallas as pl
from jax.experimental.pallas import tpu as pltpu
from jax.sharding import PartitionSpec as P

VMEM = pl.BlockSpec(memory_space=pltpu.VMEM)
SMEM = pl.BlockSpec(memory_space=pltpu.SMEM)
HBM = pl.BlockSpec(memory_space=pltpu.HBM)
ANY = pl.BlockSpec(memory_space=pl.ANY)
MIB = 1024 * 1024
BF16 = jnp.bfloat16
F32 = jnp.float32


def dot(left, right, left_dim, right_dim):
    return lax.dot_general(
        left, right, (((left_dim,), (right_dim,)), ((), ())), preferred_element_type=F32
    )


def shape(rows, cols, dtype=BF16):
    return jax.ShapeDtypeStruct((rows, cols), dtype)


def call(kernel, outs, scalars=0, scratch=(), fetched=0, room=32, earlier=(), stored=()):
    earlier = list(earlier)

    def body(*refs):
        inputs = len(refs) - len(outs) - len(scratch)
        kernel(*refs[: inputs - len(earlier)], *refs[inputs:])

    def run(*operands):
        placed = len(operands) - scalars - fetched
        moved = sum(value.size * value.dtype.itemsize for value in (*operands, *outs))
        return pl.pallas_call(
            body,
            out_shape=outs,
            in_specs=[SMEM] * scalars + [VMEM] * placed + [HBM] * fetched + [ANY] * len(earlier),
            out_specs=[HBM if i in stored else VMEM for i in range(len(outs))],
            scratch_shapes=list(scratch),
            cost_estimate=pl.CostEstimate(flops=0, bytes_accessed=moved, transcendentals=0),
            compiler_params=pltpu.CompilerParams(vmem_limit_bytes=room * MIB),
        )(*operands, *earlier)

    return run


def after(values, *earlier):
    return pl.pallas_call(
        lambda *refs: None,
        out_shape=[shape(*value.shape, value.dtype) for value in values],
        in_specs=[ANY] * (len(values) + len(earlier)),
        out_specs=[ANY] * len(values),
        input_output_aliases={i: i for i in range(len(values))},
        compiler_params=pltpu.CompilerParams(vmem_limit_bytes=MIB),
    )(*values, *earlier)


def start_copies(pairs, sems):
    copies = [pltpu.make_async_copy(source, into, sems.at[i]) for i, (source, into) in enumerate(pairs)]
    for copy in copies:
        copy.start()
    return copies


def picks(capacity, offset, rank_ref, host_ref, route_ref, slots):
    hot = host_ref.shape[0]
    tokens = route_ref.shape[1]
    label = lax.broadcasted_iota(jnp.int32, (hot, tokens), 0)
    base = jnp.zeros((hot, tokens), jnp.int32)
    for e in range(hot):
        apart = host_ref[e] ^ rank_ref[0]
        start = jnp.where((apart & 1) == 0, (apart >> 1) * (2 * capacity), -2 * slots)
        base = jnp.where(label == e, start, base)
    earlier = lax.broadcasted_iota(jnp.int32, (tokens, tokens), 0) < lax.broadcasted_iota(
        jnp.int32, (tokens, tokens), 1
    )
    marked = route_ref[...] == label
    before = dot(jnp.where(marked, 1.0, 0.0).astype(BF16), jnp.where(earlier, 1.0, 0.0).astype(BF16), 1, 0)
    position = jnp.sum(jnp.where(marked, before.astype(jnp.int32) + base, 0), axis=0, keepdims=True) + offset
    slot = lax.broadcasted_iota(jnp.int32, (slots, tokens), 0)
    return jnp.where(slot == position, 1.0, 0.0).astype(BF16)


def pack_own_kernel(capacity, rank_ref, host_ref, route_ref, *refs):
    sources, (pick_ref, filled_ref, joined_ref), (x, dy, filled, weights, sems, out_sems) = refs[:5], refs[5:8], refs[8:]
    width = weights.shape[1] // 3
    slots = pick_ref.shape[0]
    near = slice(2 * capacity, 4 * capacity)
    loads = start_copies(
        zip(sources, (x, dy) + tuple(weights.at[:, pl.ds(i * width, width)] for i in range(3))), sems
    )
    pick_ref[...] = picks(capacity, 0, rank_ref, host_ref, route_ref, slots)
    for load in loads[2:]:
        load.wait()
    stores = start_copies([(weights, joined_ref)], out_sems.at[0])
    loads[0].wait()
    filled[:slots] = dot(pick_ref[...], x[...], 1, 0).astype(BF16)
    loads[1].wait()
    filled[slots:] = dot(pick_ref[near], dy[...], 1, 0).astype(BF16)
    stores += start_copies([(filled, filled_ref)], out_sems.at[1])
    for store in stores:
        store.wait()


def pack_kernel(capacity, rank_ref, host_ref, route_ref, pick_own, filled_ref, x_ref, dy_ref, *refs):
    pick_ref, *send_refs = refs
    slots, tokens = pick_own.shape
    block = 2 * capacity
    near = slice(block, 2 * block)
    pick = picks(capacity, capacity, rank_ref, host_ref, route_ref, slots)
    pick_ref[:, :tokens] = pick_own[...]
    pick_ref[:, tokens:] = pick
    filled = (dot(pick, x_ref[...], 1, 0) + filled_ref[:slots].astype(F32)).astype(BF16)
    for k, ref in enumerate(send_refs):
        ref[:block] = filled[k * block : (k + 1) * block]
    send_refs[1][block:] = (
        dot(pick_ref[near, tokens:], dy_ref[...], 1, 0) + filled_ref[slots:].astype(F32)
    ).astype(BF16)


def pack_more_kernel(pick_ref, own_ref, other_ref, *send_refs):
    tokens = own_ref.shape[0]
    block = send_refs[0].shape[0]
    filled = (
        dot(pick_ref[:, :tokens], own_ref[...], 1, 0) + dot(pick_ref[:, tokens:], other_ref[...], 1, 0)
    ).astype(BF16)
    for k, ref in zip((0, 2, 3), send_refs):
        ref[...] = filled[k * block : (k + 1) * block]


def columns_of(own_ref, depth):
    return [pl.ds(pl.multiple_of((own_ref[0] ^ k) * depth, depth), depth) for k in range(4)]


def onward_parts(own_ref, onward):
    for at, ref in enumerate(onward):
        half = ref.shape[1] // 2
        quarter = half // 2
        start = ((own_ref[0] ^ 3) * 2 + at) * half
        both = pl.ds(pl.multiple_of(start, half), half), ref[:half]
        downs = [
            (
                pl.ds(pl.multiple_of(start + i * quarter, quarter), quarter),
                ref[half : half + quarter, i * half : (i + 1) * half],
            )
            for i in range(2)
        ]
        yield both, downs


def spread_kernel(own_ref, *refs):
    got, (joined_1, joined_2), (x_ref, piece_0, piece_3, onward_1, onward_2) = refs[:4], refs[4:6], refs[6:]
    slots, depth = piece_0.shape
    block = slots // 4
    half, quarter = depth // 2, depth // 4
    columns = columns_of(own_ref, depth)
    for j, ref in enumerate(got):
        rows = pl.ds(j * block, block)
        x_ref[rows] = ref[:block]
        for into, cols in zip(
            (piece_0, onward_1.at[pl.ds(half + quarter, slots)], onward_2.at[pl.ds(half + quarter, slots)], piece_3),
            columns,
        ):
            into[rows] = ref[:block, cols]
    for joined, start, into in ((joined_2, half, onward_1), (joined_1, 0, onward_2)):
        into[:half] = joined[start : start + half, :depth]
        into[half : half + quarter, :half] = joined[start : start + quarter, depth:]
        into[half : half + quarter, half:] = joined[start + quarter : start + half, depth:]


def act_kernel(own_ref, x_ref, *refs):
    weights, acts_ref = refs[:-1], refs[-1]
    both = acts_ref.shape[1]
    columns = columns_of(own_ref, weights[0].shape[0])
    acts_ref[...] = sum(dot(x_ref[:, cols], ref[:, :both], 1, 0) for cols, ref in zip(columns, weights))


def grad_kernel(own_ref, acts_ref, x_ref, *refs):
    got, weights, onward, outs, dy_ref = refs[:4], refs[4:7], refs[7:9], refs[9:-1], refs[-1]
    back_refs, own_term, (own_grads, *messages) = outs[:4], outs[4], outs[5:]
    slots, both = acts_ref.shape
    width = both // 2
    block = slots // 4
    depth = weights[0].shape[0]
    half = depth // 2
    columns = columns_of(own_ref, depth)
    for j, ref in enumerate(got):
        dy_ref[j * block : (j + 1) * block] = ref[ref.shape[0] - block :]
    acts = acts_ref[...]
    back_grad = sum(dot(dy_ref[:, cols], ref[:, both:], 1, 0) for cols, ref in zip(columns, weights))
    for (cols, rows), downs in onward_parts(own_ref, onward):
        acts += dot(x_ref[:, cols], rows, 1, 0)
        for cols, rows in downs:
            back_grad += dot(dy_ref[:, cols], rows, 1, 0)
    gate_act, up_act = acts[:, :width], acts[:, width:]
    sigmoid_g = jax.nn.sigmoid(gate_act)
    silu_gate = gate_act * sigmoid_g
    hidden = (silu_gate * up_act).astype(BF16)
    gate_h = back_grad * up_act * sigmoid_g * (1.0 + gate_act * (1.0 - sigmoid_g))
    own_grads[:, :width] = gate_h.astype(BF16)
    own_grads[:, width:] = (back_grad * silu_gate).astype(BF16)
    grads = own_grads[...]
    for k, cols in enumerate(columns):
        term = dot(dy_ref[:, cols], hidden, 0, 0)
        if k == 0:
            own_term[...] = term
        else:
            messages[k - 1][:slots] = grads
            messages[k - 1][slots:, :width] = term[:half].astype(BF16)
            messages[k - 1][slots:, width:] = term[half:].astype(BF16)
    pairs = [(cols, ref[:, :both]) for cols, ref in zip(columns, weights)]
    for cols, rows in pairs + [part for part, _ in onward_parts(own_ref, onward)]:
        slot_grad = dot(grads, rows, 1, 1).astype(BF16)
        for j, back_ref in enumerate(back_refs):
            back_ref[:, cols] = slot_grad[j * block : (j + 1) * block]


def sum_kernel(*refs):
    pieces, messages, own_term, (gate_ref, up_ref, down_ref) = refs[:4], refs[4:8], refs[8], refs[9:]
    slots = pieces[0].shape[0]
    depth, width = gate_ref.shape
    half = depth // 2
    total = sum(dot(piece[-slots:], got[:slots], 0, 0) for piece, got in zip(pieces, messages))
    gate_ref[...] = total[:, :width]
    up_ref[...] = total[:, width:]
    for rows, cols in ((slice(0, half), slice(0, width)), (slice(half, depth), slice(width, 2 * width))):
        down_ref[rows] = own_term[rows] + sum(got[slots:, cols].astype(F32) for got in messages[1:])


def unpack_kernel(pick_ref, *refs):
    returned, (mine_ref, other_ref, rows_ref) = refs[:-3], refs[-3:]
    tokens = mine_ref.shape[0]
    block = returned[0].shape[0]
    for k, ref in enumerate(returned):
        rows_ref[k * block : (k + 1) * block] = ref[...]
    both = dot(pick_ref[...], rows_ref[...], 0, 0).astype(BF16)
    mine_ref[...] = both[:tokens]
    other_ref[...] = both[tokens:]


def shards_by_partner(n_rep, tokens, cotangent, route, host, w_gate, w_up, w_down_t):
    tok_rows, model_width = tokens.shape
    hot = host.shape[0]
    _, depth, width = w_gate.shape
    capacity = (3 * tok_rows + 2 * hot - 1) // (2 * hot)
    slots = hot * capacity
    parts = n_rep // 2
    block = 2 * capacity
    own = lax.axis_index("own").astype(jnp.int32).reshape(1)
    rank = lax.axis_index("rep").astype(jnp.int32).reshape(1)

    def over_own(value, k):
        return lax.ppermute(value, "own", [(i, i ^ k) for i in range(4)])

    def over_rep(value, k):
        return lax.ppermute(value, "rep", [(i, i ^ k) for i in range(n_rep)])

    route = route.reshape(1, tok_rows)
    route_b, tokens_b, cotangent_b = over_rep(route, 1), over_rep(tokens, 1), over_rep(cotangent, 1)
    token_rows = pltpu.VMEM((tok_rows, model_width), BF16)
    slot_rows = pltpu.VMEM((slots, model_width), BF16)
    dma = pltpu.SemaphoreType.DMA
    pick, filled, joined = call(
        functools.partial(pack_own_kernel, capacity),
        [shape(slots, tok_rows), shape(slots + block, model_width), shape(depth, 3 * width)],
        2,
        [token_rows, token_rows, pltpu.VMEM((slots + block, model_width), BF16), pltpu.VMEM((depth, 3 * width), BF16)]
        + [dma((5,)), dma((2, 1))],
        5,
        62,
        (),
        (1, 2),
    )(rank, host, route, tokens, cotangent, w_gate[0], w_up[0], w_down_t[0])
    joined_1, joined_2 = over_own(joined, 1), over_own(joined, 2)
    pick, own_x, near, far_xa, far_xb = call(
        functools.partial(pack_kernel, capacity),
        [shape(slots, 2 * tok_rows), shape(block, model_width), shape(2 * block, model_width)]
        + [shape(block, model_width)] * 2,
        2,
    )(rank, host, route_b, pick, filled, tokens_b, cotangent_b)
    near, far_xa, far_xb = over_rep(near, 2), over_rep(far_xa, 4), over_rep(far_xb, 6)
    own_dy, far_a, far_b = call(pack_more_kernel, [shape(block, model_width)] * 3)(pick, cotangent, cotangent_b)

    onward = shape(depth // 2 + depth // 4 + slots, depth)
    x, piece_0, piece_3, onward_1, onward_2 = call(
        spread_kernel,
        [shape(slots, model_width), shape(slots, depth), shape(slots, depth), onward, onward],
        1,
        earlier=[own_dy],
    )(own, own_x, near, far_xa, far_xb, joined_1, joined_2)
    far_a, far_b = after([far_a, far_b], piece_0)
    far_a, far_b = over_rep(far_a, 4), over_rep(far_b, 6)
    onward_1, onward_2, piece_3 = over_own(onward_1, 1), over_own(onward_2, 2), over_own(piece_3, 3)
    weights = [joined, joined_1, joined_2]
    acts = call(act_kernel, [shape(slots, 2 * width, F32)], 1)(own, x, *weights)[0]

    message = shape(slots + depth // 2, 2 * width)
    *back, own_term, grads, message_1, message_2, message_3 = call(
        grad_kernel,
        [shape(block, model_width)] * parts
        + [shape(depth, width, F32), shape(slots, 2 * width), message, message, message],
        1,
        [slot_rows],
        earlier=[piece_3],
    )(own, acts, x, own_dy, near, far_a, far_b, *weights, onward_2, onward_1)
    returned = [back[0]] + [over_rep(back[k], 2 * k) for k in range(1, parts)]
    messages = [over_own(message_1, 1), over_own(message_2, 2), over_own(message_3, 3)]

    mine, other = call(unpack_kernel, [shape(tok_rows, model_width)] * 2, 0, [slot_rows], earlier=messages)(
        pick, *returned
    )
    x_grad = mine + over_rep(other, 1)
    out = call(sum_kernel, [shape(depth, width, F32)] * 3)(
        piece_0, onward_1, onward_2, piece_3, grads, *messages, own_term
    )
    return (x_grad, *(grad[None] for grad in out))


def shards_whole(tokens, cotangent, route, host, w_gate, w_up, w_down_t):
    tok_rows, model_width = tokens.shape
    hot = host.shape[0]
    width = w_gate.shape[2]
    capacity = max(2, (3 * tok_rows + 2 * hot - 1) // (2 * hot))
    slots = hot * capacity
    labels = lax.broadcasted_iota(jnp.int32, (tok_rows, hot), 1)
    target = jnp.sum(jnp.where(route == labels, host[None, :], 0), axis=1)
    marked = (target[:, None] == labels).astype(jnp.int32)
    arrival = jnp.sum(jnp.cumsum(marked, axis=0) * marked, axis=1) - 1
    position = target * capacity + arrival
    pick = (lax.broadcasted_iota(jnp.int32, (slots, tok_rows), 0) == position[None, :]).astype(BF16)

    def exchange(value):
        split = value.astype(BF16).reshape(hot, capacity, model_width)
        return lax.all_to_all(split, "rep", split_axis=0, concat_axis=0, tiled=True).reshape(slots, model_width)

    slot_x, slot_dy = exchange(dot(pick, tokens, 1, 0)), exchange(dot(pick, cotangent, 1, 0))
    gate, up, down = (lax.all_gather(w[0], "own", axis=0, tiled=True) for w in (w_gate, w_up, w_down_t))
    gate_act, up_act, back_grad = dot(slot_x, gate, 1, 0), dot(slot_x, up, 1, 0), dot(slot_dy, down, 1, 0)
    sigmoid_g = jax.nn.sigmoid(gate_act)
    silu_gate = gate_act * sigmoid_g
    hidden = (silu_gate * up_act).astype(BF16)
    grad_gate_h = (back_grad * up_act * sigmoid_g * (1.0 + gate_act * (1.0 - sigmoid_g))).astype(BF16)
    grad_up_h = (back_grad * silu_gate).astype(BF16)
    returned = exchange(dot(grad_gate_h, gate, 1, 1) + dot(grad_up_h, up, 1, 1))
    x_grad = dot(pick, returned, 0, 0).astype(BF16)
    terms = [dot(slot_x, grad_gate_h, 0, 0), dot(slot_x, grad_up_h, 0, 0), dot(slot_dy, hidden, 0, 0)]
    summed = lax.psum_scatter(
        jnp.concatenate(terms, axis=1).astype(BF16), "own", scatter_dimension=0, tiled=True
    ).astype(F32)
    return (x_grad, *(summed[None, :, i * width : (i + 1) * width] for i in range(3)))


def solution(mesh):
    n_own, n_rep = mesh.shape["own"], mesh.shape["rep"]

    def shards(tokens, *rest):
        capacity = (3 * tokens.shape[0] + 2 * n_rep - 1) // (2 * n_rep)
        if n_own == 4 and n_rep == 8 and capacity % 8 == 0:
            return shards_by_partner(n_rep, tokens, *rest)
        return shards_whole(tokens, *rest)

    return jax.shard_map(
        shards,
        mesh=mesh,
        in_specs=(
            P(("own", "rep"), None),
            P(("own", "rep"), None),
            P(("own", "rep"), None),
            P(),
            P("rep", "own", None),
            P("rep", "own", None),
            P("rep", "own", None),
        ),
        out_specs=(
            P(("own", "rep"), None),
            P("rep", "own", None),
            P("rep", "own", None),
            P("rep", "own", None),
        ),
        check_vma=False,
    )
```

```python
import functools

import jax
import jax.numpy as jnp
from jax import lax
from jax.experimental import pallas as pl
from jax.experimental.pallas import tpu as pltpu
from jax.sharding import PartitionSpec as P

VMEM = pl.BlockSpec(memory_space=pltpu.VMEM)
SMEM = pl.BlockSpec(memory_space=pltpu.SMEM)
ANY = pl.BlockSpec(memory_space=pl.ANY)
MIB = 1024 * 1024
BF16 = jnp.bfloat16
F32 = jnp.float32


def dot(left, right, left_dim, right_dim):
    return lax.dot_general(
        left, right, (((left_dim,), (right_dim,)), ((), ())), preferred_element_type=F32
    )


def shape(rows, cols, dtype=BF16):
    return jax.ShapeDtypeStruct((rows, cols), dtype)


def call(kernel, outs, scalars=0, scratch=(), earlier=()):
    earlier = list(earlier)

    def body(*refs):
        inputs = len(refs) - len(outs) - len(scratch)
        kernel(*refs[: inputs - len(earlier)], *refs[inputs:])

    def run(*operands):
        moved = sum(value.size * value.dtype.itemsize for value in (*operands, *outs))
        return pl.pallas_call(
            body,
            out_shape=outs,
            in_specs=[SMEM] * scalars + [VMEM] * (len(operands) - scalars) + [ANY] * len(earlier),
            out_specs=[VMEM] * len(outs),
            scratch_shapes=list(scratch),
            cost_estimate=pl.CostEstimate(flops=0, bytes_accessed=moved, transcendentals=0),
            compiler_params=pltpu.CompilerParams(vmem_limit_bytes=32 * MIB),
        )(*operands, *earlier)

    return run


def after(values, *earlier):
    return pl.pallas_call(
        lambda *refs: None,
        out_shape=[shape(*value.shape, value.dtype) for value in values],
        in_specs=[ANY] * (len(values) + len(earlier)),
        out_specs=[ANY] * len(values),
        input_output_aliases={i: i for i in range(len(values))},
        compiler_params=pltpu.CompilerParams(vmem_limit_bytes=MIB),
    )(*values, *earlier)


def picks(capacity, offset, rank_ref, host_ref, route_ref, slots):
    hot = host_ref.shape[0]
    tokens = route_ref.shape[1]
    label = lax.broadcasted_iota(jnp.int32, (hot, tokens), 0)
    base = jnp.zeros((hot, tokens), jnp.int32)
    for e in range(hot):
        apart = host_ref[e] ^ rank_ref[0]
        start = jnp.where((apart & 1) == 0, (apart >> 1) * (2 * capacity), -2 * slots)
        base = jnp.where(label == e, start, base)
    earlier = lax.broadcasted_iota(jnp.int32, (tokens, tokens), 0) < lax.broadcasted_iota(
        jnp.int32, (tokens, tokens), 1
    )
    marked = route_ref[...] == label
    before = dot(jnp.where(marked, 1.0, 0.0).astype(BF16), jnp.where(earlier, 1.0, 0.0).astype(BF16), 1, 0)
    position = jnp.sum(jnp.where(marked, before.astype(jnp.int32) + base, 0), axis=0, keepdims=True) + offset
    slot = lax.broadcasted_iota(jnp.int32, (slots, tokens), 0)
    return jnp.where(slot == position, 1.0, 0.0).astype(BF16)


def pack_kernel(capacity, rank_ref, host_ref, route_a, route_b, x_a, x_b, dy_a, dy_b, pick_ref, *refs):
    *send_refs, rows_ref = refs
    slots = pick_ref.shape[0]
    tokens = route_a.shape[1]
    block = 2 * capacity
    pick_ref[:, :tokens] = picks(capacity, 0, rank_ref, host_ref, route_a, slots)
    pick_ref[:, tokens:] = picks(capacity, capacity, rank_ref, host_ref, route_b, slots)
    rows_ref[:tokens] = x_a[...]
    rows_ref[tokens:] = x_b[...]
    filled = dot(pick_ref[...], rows_ref[...], 1, 0).astype(BF16)
    for k, ref in enumerate(send_refs):
        ref[:block] = filled[k * block : (k + 1) * block]
    near = slice(block, 2 * block)
    send_refs[1][block:] = (
        dot(pick_ref[near, :tokens], dy_a[...], 1, 0) + dot(pick_ref[near, tokens:], dy_b[...], 1, 0)
    ).astype(BF16)


def pack_more_kernel(pick_ref, own_ref, other_ref, *send_refs):
    tokens = own_ref.shape[0]
    block = send_refs[0].shape[0]
    filled = (
        dot(pick_ref[:, :tokens], own_ref[...], 1, 0) + dot(pick_ref[:, tokens:], other_ref[...], 1, 0)
    ).astype(BF16)
    for k, ref in zip((0, 2, 3), send_refs):
        ref[...] = filled[k * block : (k + 1) * block]


def columns_of(own_ref, depth):
    return [pl.ds(pl.multiple_of((own_ref[0] ^ k) * depth, depth), depth) for k in range(4)]


def onward_parts(own_ref, onward):
    for at, ref in enumerate(onward):
        half = ref.shape[1] // 2
        quarter = half // 2
        start = ((own_ref[0] ^ 3) * 2 + at) * half
        both = pl.ds(pl.multiple_of(start, half), half), ref[:half]
        downs = [
            (
                pl.ds(pl.multiple_of(start + i * quarter, quarter), quarter),
                ref[half : half + quarter, i * half : (i + 1) * half],
            )
            for i in range(2)
        ]
        yield both, downs


def spread_kernel(own_ref, *refs):
    got, (joined_1, joined_2), (x_ref, piece_0, piece_3, onward_1, onward_2) = refs[:4], refs[4:6], refs[6:]
    slots, depth = piece_0.shape
    block = slots // 4
    half, quarter = depth // 2, depth // 4
    columns = columns_of(own_ref, depth)
    for j, ref in enumerate(got):
        rows = pl.ds(j * block, block)
        x_ref[rows] = ref[:block]
        for into, cols in zip(
            (piece_0, onward_1.at[pl.ds(half + quarter, slots)], onward_2.at[pl.ds(half + quarter, slots)], piece_3),
            columns,
        ):
            into[rows] = ref[:block, cols]
    for joined, start, into in ((joined_2, half, onward_1), (joined_1, 0, onward_2)):
        into[:half] = joined[start : start + half, :depth]
        into[half : half + quarter, :half] = joined[start : start + quarter, depth:]
        into[half : half + quarter, half:] = joined[start + quarter : start + half, depth:]


def act_kernel(own_ref, x_ref, *refs):
    weights, acts_ref = refs[:-1], refs[-1]
    both = acts_ref.shape[1]
    columns = columns_of(own_ref, weights[0].shape[0])
    acts_ref[...] = sum(dot(x_ref[:, cols], ref[:, :both], 1, 0) for cols, ref in zip(columns, weights))


def grad_kernel(own_ref, acts_ref, x_ref, *refs):
    got, weights, onward, outs, dy_ref = refs[:4], refs[4:7], refs[7:9], refs[9:-1], refs[-1]
    back_refs, own_term, (own_grads, *messages) = outs[:4], outs[4], outs[5:]
    slots, both = acts_ref.shape
    width = both // 2
    block = slots // 4
    depth = weights[0].shape[0]
    half = depth // 2
    columns = columns_of(own_ref, depth)
    for j, ref in enumerate(got):
        dy_ref[j * block : (j + 1) * block] = ref[ref.shape[0] - block :]
    acts = acts_ref[...]
    back_grad = sum(dot(dy_ref[:, cols], ref[:, both:], 1, 0) for cols, ref in zip(columns, weights))
    for (cols, rows), downs in onward_parts(own_ref, onward):
        acts += dot(x_ref[:, cols], rows, 1, 0)
        for cols, rows in downs:
            back_grad += dot(dy_ref[:, cols], rows, 1, 0)
    gate_act, up_act = acts[:, :width], acts[:, width:]
    sigmoid_g = jax.nn.sigmoid(gate_act)
    silu_gate = gate_act * sigmoid_g
    hidden = (silu_gate * up_act).astype(BF16)
    gate_h = back_grad * up_act * sigmoid_g * (1.0 + gate_act * (1.0 - sigmoid_g))
    own_grads[:, :width] = gate_h.astype(BF16)
    own_grads[:, width:] = (back_grad * silu_gate).astype(BF16)
    grads = own_grads[...]
    for k, cols in enumerate(columns):
        term = dot(dy_ref[:, cols], hidden, 0, 0)
        if k == 0:
            own_term[...] = term
        else:
            messages[k - 1][:slots] = grads
            messages[k - 1][slots:, :width] = term[:half].astype(BF16)
            messages[k - 1][slots:, width:] = term[half:].astype(BF16)
    pairs = [(cols, ref[:, :both]) for cols, ref in zip(columns, weights)]
    for cols, rows in pairs + [part for part, _ in onward_parts(own_ref, onward)]:
        slot_grad = dot(grads, rows, 1, 1).astype(BF16)
        for j, back_ref in enumerate(back_refs):
            back_ref[:, cols] = slot_grad[j * block : (j + 1) * block]


def sum_kernel(*refs):
    pieces, messages, own_term = refs[:4], refs[4:8], refs[8]
    (gate_ref, up_ref, down_ref), (x_ref, grads_ref) = refs[9:12], refs[12:]
    slots = pieces[0].shape[0]
    depth, width = gate_ref.shape
    half = depth // 2
    for k, (piece, got) in enumerate(zip(pieces, messages)):
        x_ref[k * slots : (k + 1) * slots] = piece[-slots:]
        grads_ref[k * slots : (k + 1) * slots] = got[:slots]
    total = dot(x_ref[...], grads_ref[...], 0, 0)
    gate_ref[...] = total[:, :width]
    up_ref[...] = total[:, width:]
    for rows, cols in ((slice(0, half), slice(0, width)), (slice(half, depth), slice(width, 2 * width))):
        down_ref[rows] = own_term[rows] + sum(got[slots:, cols].astype(F32) for got in messages[1:])


def unpack_kernel(pick_ref, *refs):
    returned, (mine_ref, other_ref, rows_ref) = refs[:-3], refs[-3:]
    tokens = mine_ref.shape[0]
    block = returned[0].shape[0]
    for k, ref in enumerate(returned):
        rows_ref[k * block : (k + 1) * block] = ref[...]
    both = dot(pick_ref[...], rows_ref[...], 0, 0).astype(BF16)
    mine_ref[...] = both[:tokens]
    other_ref[...] = both[tokens:]


def shards_by_partner(n_rep, tokens, cotangent, route, host, w_gate, w_up, w_down_t):
    tok_rows, model_width = tokens.shape
    hot = host.shape[0]
    _, depth, width = w_gate.shape
    capacity = (3 * tok_rows + 2 * hot - 1) // (2 * hot)
    slots = hot * capacity
    parts = n_rep // 2
    block = 2 * capacity
    own = lax.axis_index("own").astype(jnp.int32).reshape(1)
    rank = lax.axis_index("rep").astype(jnp.int32).reshape(1)

    def over_own(value, k):
        return lax.ppermute(value, "own", [(i, i ^ k) for i in range(4)])

    def over_rep(value, k):
        return lax.ppermute(value, "rep", [(i, i ^ k) for i in range(n_rep)])

    route = route.reshape(1, tok_rows)
    route_b, tokens_b, cotangent_b = over_rep(route, 1), over_rep(tokens, 1), over_rep(cotangent, 1)
    joined = jnp.concatenate([w_gate[0], w_up[0], w_down_t[0]], axis=1)
    joined_1, joined_2 = over_own(joined, 1), over_own(joined, 2)
    slot_rows = pltpu.VMEM((slots, model_width), BF16)
    pick, own_x, near, far_xa, far_xb = call(
        functools.partial(pack_kernel, capacity),
        [shape(slots, 2 * tok_rows), shape(block, model_width), shape(2 * block, model_width)]
        + [shape(block, model_width)] * 2,
        2,
        [pltpu.VMEM((2 * tok_rows, model_width), BF16)],
    )(rank, host, route, route_b, tokens, tokens_b, cotangent, cotangent_b)
    near, far_xa, far_xb = over_rep(near, 2), over_rep(far_xa, 4), over_rep(far_xb, 6)
    own_dy, far_a, far_b = call(pack_more_kernel, [shape(block, model_width)] * 3)(pick, cotangent, cotangent_b)

    onward = shape(depth // 2 + depth // 4 + slots, depth)
    x, piece_0, piece_3, onward_1, onward_2 = call(
        spread_kernel,
        [shape(slots, model_width), shape(slots, depth), shape(slots, depth), onward, onward],
        1,
        earlier=[own_dy],
    )(own, own_x, near, far_xa, far_xb, joined_1, joined_2)
    far_a, far_b = after([far_a, far_b], piece_0)
    far_a, far_b = over_rep(far_a, 4), over_rep(far_b, 6)
    onward_1, onward_2, piece_3 = over_own(onward_1, 1), over_own(onward_2, 2), over_own(piece_3, 3)
    weights = [joined, joined_1, joined_2]
    acts = call(act_kernel, [shape(slots, 2 * width, F32)], 1)(own, x, *weights)[0]

    message = shape(slots + depth // 2, 2 * width)
    *back, own_term, grads, message_1, message_2, message_3 = call(
        grad_kernel,
        [shape(block, model_width)] * parts
        + [shape(depth, width, F32), shape(slots, 2 * width), message, message, message],
        1,
        [slot_rows],
        earlier=[piece_3],
    )(own, acts, x, own_dy, near, far_a, far_b, *weights, onward_2, onward_1)
    returned = [back[0]] + [over_rep(back[k], 2 * k) for k in range(1, parts)]
    messages = [over_own(message_1, 1), over_own(message_2, 2), over_own(message_3, 3)]

    mine, other = call(unpack_kernel, [shape(tok_rows, model_width)] * 2, 0, [slot_rows], earlier=messages)(
        pick, *returned
    )
    x_grad = mine + over_rep(other, 1)
    out = call(sum_kernel, [shape(depth, width, F32)] * 3, 0, [pltpu.VMEM((4 * slots, depth), BF16)] * 2)(
        piece_0, onward_1, onward_2, piece_3, grads, *messages, own_term
    )
    return (x_grad, *(grad[None] for grad in out))


def shards_whole(tokens, cotangent, route, host, w_gate, w_up, w_down_t):
    tok_rows, model_width = tokens.shape
    hot = host.shape[0]
    width = w_gate.shape[2]
    capacity = max(2, (3 * tok_rows + 2 * hot - 1) // (2 * hot))
    slots = hot * capacity
    labels = lax.broadcasted_iota(jnp.int32, (tok_rows, hot), 1)
    target = jnp.sum(jnp.where(route == labels, host[None, :], 0), axis=1)
    marked = (target[:, None] == labels).astype(jnp.int32)
    arrival = jnp.sum(jnp.cumsum(marked, axis=0) * marked, axis=1) - 1
    position = target * capacity + arrival
    pick = (lax.broadcasted_iota(jnp.int32, (slots, tok_rows), 0) == position[None, :]).astype(BF16)

    def exchange(value):
        split = value.astype(BF16).reshape(hot, capacity, model_width)
        return lax.all_to_all(split, "rep", split_axis=0, concat_axis=0, tiled=True).reshape(slots, model_width)

    slot_x, slot_dy = exchange(dot(pick, tokens, 1, 0)), exchange(dot(pick, cotangent, 1, 0))
    gate, up, down = (lax.all_gather(w[0], "own", axis=0, tiled=True) for w in (w_gate, w_up, w_down_t))
    gate_act, up_act, back_grad = dot(slot_x, gate, 1, 0), dot(slot_x, up, 1, 0), dot(slot_dy, down, 1, 0)
    sigmoid_g = jax.nn.sigmoid(gate_act)
    silu_gate = gate_act * sigmoid_g
    hidden = (silu_gate * up_act).astype(BF16)
    grad_gate_h = (back_grad * up_act * sigmoid_g * (1.0 + gate_act * (1.0 - sigmoid_g))).astype(BF16)
    grad_up_h = (back_grad * silu_gate).astype(BF16)
    returned = exchange(dot(grad_gate_h, gate, 1, 1) + dot(grad_up_h, up, 1, 1))
    x_grad = dot(pick, returned, 0, 0).astype(BF16)
    terms = [dot(slot_x, grad_gate_h, 0, 0), dot(slot_x, grad_up_h, 0, 0), dot(slot_dy, hidden, 0, 0)]
    summed = lax.psum_scatter(
        jnp.concatenate(terms, axis=1).astype(BF16), "own", scatter_dimension=0, tiled=True
    ).astype(F32)
    return (x_grad, *(summed[None, :, i * width : (i + 1) * width] for i in range(3)))


def solution(mesh):
    n_own, n_rep = mesh.shape["own"], mesh.shape["rep"]

    def shards(tokens, *rest):
        capacity = (3 * tokens.shape[0] + 2 * n_rep - 1) // (2 * n_rep)
        if n_own == 4 and n_rep == 8 and capacity % 8 == 0:
            return shards_by_partner(n_rep, tokens, *rest)
        return shards_whole(tokens, *rest)

    return jax.shard_map(
        shards,
        mesh=mesh,
        in_specs=(
            P(("own", "rep"), None),
            P(("own", "rep"), None),
            P(("own", "rep"), None),
            P(),
            P("rep", "own", None),
            P("rep", "own", None),
            P("rep", "own", None),
        ),
        out_specs=(
            P(("own", "rep"), None),
            P("rep", "own", None),
            P("rep", "own", None),
            P("rep", "own", None),
        ),
        check_vma=False,
    )
```

```python
import functools

import jax
import jax.numpy as jnp
from jax import lax
from jax.experimental import pallas as pl
from jax.experimental.pallas import tpu as pltpu
from jax.sharding import PartitionSpec as P

VMEM = pl.BlockSpec(memory_space=pltpu.VMEM)
SMEM = pl.BlockSpec(memory_space=pltpu.SMEM)
ANY = pl.BlockSpec(memory_space=pl.ANY)
MIB = 1024 * 1024
AHEAD = 1 << 33
BF16 = jnp.bfloat16
F32 = jnp.float32


def dot(left, right, left_dim, right_dim):
    return lax.dot_general(
        left, right, (((left_dim,), (right_dim,)), ((), ())), preferred_element_type=F32
    )


def shape(rows, cols, dtype=BF16):
    return jax.ShapeDtypeStruct((rows, cols), dtype)


def call(kernel, outs, scalars=0, scratch=(), earlier=()):
    earlier = list(earlier)

    def body(*refs):
        inputs = len(refs) - len(outs) - len(scratch)
        kernel(*refs[: inputs - len(earlier)], *refs[inputs:])

    def run(*operands):
        moved = sum(value.size * value.dtype.itemsize for value in (*operands, *outs))
        return pl.pallas_call(
            body,
            out_shape=outs,
            in_specs=[SMEM] * scalars + [VMEM] * (len(operands) - scalars) + [ANY] * len(earlier),
            out_specs=[VMEM] * len(outs),
            scratch_shapes=list(scratch),
            cost_estimate=pl.CostEstimate(flops=0, bytes_accessed=moved, transcendentals=0),
            compiler_params=pltpu.CompilerParams(vmem_limit_bytes=32 * MIB),
        )(*operands, *earlier)

    return run


def after(values, *earlier, ahead=0):
    return pl.pallas_call(
        lambda *refs: None,
        out_shape=[shape(*value.shape, value.dtype) for value in values],
        in_specs=[ANY] * (len(values) + len(earlier)),
        out_specs=[ANY] * len(values),
        input_output_aliases={i: i for i in range(len(values))},
        cost_estimate=pl.CostEstimate(flops=ahead, bytes_accessed=0, transcendentals=0),
        compiler_params=pltpu.CompilerParams(vmem_limit_bytes=MIB),
    )(*values, *earlier)


def picks(capacity, offset, rank_ref, host_ref, route_ref, slots):
    hot = host_ref.shape[0]
    tokens = route_ref.shape[1]
    label = lax.broadcasted_iota(jnp.int32, (hot, tokens), 0)
    base = jnp.zeros((hot, tokens), jnp.int32)
    for e in range(hot):
        apart = host_ref[e] ^ rank_ref[0]
        start = jnp.where((apart & 1) == 0, (apart >> 1) * (2 * capacity), -2 * slots)
        base = jnp.where(label == e, start, base)
    earlier = lax.broadcasted_iota(jnp.int32, (tokens, tokens), 0) < lax.broadcasted_iota(
        jnp.int32, (tokens, tokens), 1
    )
    marked = route_ref[...] == label
    before = dot(jnp.where(marked, 1.0, 0.0).astype(BF16), jnp.where(earlier, 1.0, 0.0).astype(BF16), 1, 0)
    position = jnp.sum(jnp.where(marked, before.astype(jnp.int32) + base, 0), axis=0, keepdims=True) + offset
    slot = lax.broadcasted_iota(jnp.int32, (slots, tokens), 0)
    return jnp.where(slot == position, 1.0, 0.0).astype(BF16)


def pack_kernel(capacity, rank_ref, host_ref, route_a, route_b, x_a, x_b, dy_a, dy_b, pick_ref, *refs):
    *send_refs, rows_ref = refs
    slots = pick_ref.shape[0]
    tokens = route_a.shape[1]
    block = 2 * capacity
    pick_ref[:, :tokens] = picks(capacity, 0, rank_ref, host_ref, route_a, slots)
    pick_ref[:, tokens:] = picks(capacity, capacity, rank_ref, host_ref, route_b, slots)
    rows_ref[:tokens] = x_a[...]
    rows_ref[tokens:] = x_b[...]
    filled = dot(pick_ref[...], rows_ref[...], 1, 0).astype(BF16)
    for k, ref in enumerate(send_refs):
        ref[:block] = filled[k * block : (k + 1) * block]
    near = slice(block, 2 * block)
    send_refs[1][block:] = (
        dot(pick_ref[near, :tokens], dy_a[...], 1, 0) + dot(pick_ref[near, tokens:], dy_b[...], 1, 0)
    ).astype(BF16)


def pack_more_kernel(pick_ref, own_ref, other_ref, *send_refs):
    tokens = own_ref.shape[0]
    block = send_refs[0].shape[0]
    filled = (
        dot(pick_ref[:, :tokens], own_ref[...], 1, 0) + dot(pick_ref[:, tokens:], other_ref[...], 1, 0)
    ).astype(BF16)
    for k, ref in zip((0, 2, 3), send_refs):
        ref[...] = filled[k * block : (k + 1) * block]


def columns_of(own_ref, depth):
    return [pl.ds(pl.multiple_of((own_ref[0] ^ k) * depth, depth), depth) for k in range(4)]


def onward_parts(own_ref, onward):
    for at, ref in enumerate(onward):
        half = ref.shape[1] // 2
        quarter = half // 2
        start = ((own_ref[0] ^ 3) * 2 + at) * half
        both = pl.ds(pl.multiple_of(start, half), half), ref[:half]
        downs = [
            (
                pl.ds(pl.multiple_of(start + i * quarter, quarter), quarter),
                ref[half : half + quarter, i * half : (i + 1) * half],
            )
            for i in range(2)
        ]
        yield both, downs


def spread_kernel(own_ref, *refs):
    got, (joined_1, joined_2), (x_ref, piece_0, piece_3, onward_1, onward_2) = refs[:4], refs[4:6], refs[6:]
    slots, depth = piece_0.shape
    block = slots // 4
    half, quarter = depth // 2, depth // 4
    columns = columns_of(own_ref, depth)
    for j, ref in enumerate(got):
        rows = pl.ds(j * block, block)
        x_ref[rows] = ref[:block]
        for into, cols in zip(
            (piece_0, onward_1.at[pl.ds(half + quarter, slots)], onward_2.at[pl.ds(half + quarter, slots)], piece_3),
            columns,
        ):
            into[rows] = ref[:block, cols]
    for joined, start, into in ((joined_2, half, onward_1), (joined_1, 0, onward_2)):
        into[:half] = joined[start : start + half, :depth]
        into[half : half + quarter, :half] = joined[start : start + quarter, depth:]
        into[half : half + quarter, half:] = joined[start + quarter : start + half, depth:]


def act_kernel(own_ref, x_ref, *refs):
    weights, acts_ref = refs[:-1], refs[-1]
    both = acts_ref.shape[1]
    columns = columns_of(own_ref, weights[0].shape[0])
    acts_ref[...] = sum(dot(x_ref[:, cols], ref[:, :both], 1, 0) for cols, ref in zip(columns, weights))


def grad_kernel(own_ref, acts_ref, x_ref, *refs):
    got, weights, onward, outs, dy_ref = refs[:4], refs[4:7], refs[7:9], refs[9:-1], refs[-1]
    back_refs, own_term, (own_grads, *messages) = outs[:4], outs[4], outs[5:]
    slots, both = acts_ref.shape
    width = both // 2
    block = slots // 4
    depth = weights[0].shape[0]
    half = depth // 2
    columns = columns_of(own_ref, depth)
    for j, ref in enumerate(got):
        dy_ref[j * block : (j + 1) * block] = ref[ref.shape[0] - block :]
    acts = acts_ref[...]
    back_grad = sum(dot(dy_ref[:, cols], ref[:, both:], 1, 0) for cols, ref in zip(columns, weights))
    for (cols, rows), downs in onward_parts(own_ref, onward):
        acts += dot(x_ref[:, cols], rows, 1, 0)
        for cols, rows in downs:
            back_grad += dot(dy_ref[:, cols], rows, 1, 0)
    gate_act, up_act = acts[:, :width], acts[:, width:]
    sigmoid_g = jax.nn.sigmoid(gate_act)
    silu_gate = gate_act * sigmoid_g
    hidden = (silu_gate * up_act).astype(BF16)
    gate_h = back_grad * up_act * sigmoid_g * (1.0 + gate_act * (1.0 - sigmoid_g))
    own_grads[:, :width] = gate_h.astype(BF16)
    own_grads[:, width:] = (back_grad * silu_gate).astype(BF16)
    grads = own_grads[...]
    for k, cols in enumerate(columns):
        term = dot(dy_ref[:, cols], hidden, 0, 0)
        if k == 0:
            own_term[...] = term
        else:
            messages[k - 1][:slots] = grads
            messages[k - 1][slots:, :width] = term[:half].astype(BF16)
            messages[k - 1][slots:, width:] = term[half:].astype(BF16)
    pairs = [(cols, ref[:, :both]) for cols, ref in zip(columns, weights)]
    for cols, rows in pairs + [part for part, _ in onward_parts(own_ref, onward)]:
        slot_grad = dot(grads, rows, 1, 1).astype(BF16)
        for j, back_ref in enumerate(back_refs):
            back_ref[:, cols] = slot_grad[j * block : (j + 1) * block]


def sum_kernel(*refs):
    pieces, messages, own_term = refs[:4], refs[4:8], refs[8]
    (gate_ref, up_ref, down_ref), (x_ref, grads_ref) = refs[9:12], refs[12:]
    slots = pieces[0].shape[0]
    depth, width = gate_ref.shape
    half = depth // 2
    for k, (piece, got) in enumerate(zip(pieces, messages)):
        x_ref[k * slots : (k + 1) * slots] = piece[-slots:]
        grads_ref[k * slots : (k + 1) * slots] = got[:slots]
    total = dot(x_ref[...], grads_ref[...], 0, 0)
    gate_ref[...] = total[:, :width]
    up_ref[...] = total[:, width:]
    for rows, cols in ((slice(0, half), slice(0, width)), (slice(half, depth), slice(width, 2 * width))):
        down_ref[rows] = own_term[rows] + sum(got[slots:, cols].astype(F32) for got in messages[1:])


def unpack_kernel(pick_ref, *refs):
    returned, (mine_ref, other_ref, rows_ref) = refs[:-3], refs[-3:]
    tokens = mine_ref.shape[0]
    block = returned[0].shape[0]
    for k, ref in enumerate(returned):
        rows_ref[k * block : (k + 1) * block] = ref[...]
    both = dot(pick_ref[...], rows_ref[...], 0, 0).astype(BF16)
    mine_ref[...] = both[:tokens]
    other_ref[...] = both[tokens:]


def shards_by_partner(n_rep, tokens, cotangent, route, host, w_gate, w_up, w_down_t):
    tok_rows, model_width = tokens.shape
    hot = host.shape[0]
    _, depth, width = w_gate.shape
    capacity = (3 * tok_rows + 2 * hot - 1) // (2 * hot)
    slots = hot * capacity
    parts = n_rep // 2
    block = 2 * capacity
    own = lax.axis_index("own").astype(jnp.int32).reshape(1)
    rank = lax.axis_index("rep").astype(jnp.int32).reshape(1)

    def over_own(value, k):
        return lax.ppermute(value, "own", [(i, i ^ k) for i in range(4)])

    def over_rep(value, k):
        return lax.ppermute(value, "rep", [(i, i ^ k) for i in range(n_rep)])

    route = route.reshape(1, tok_rows)
    route_b, tokens_b, cotangent_b = over_rep(route, 1), over_rep(tokens, 1), over_rep(cotangent, 1)
    route_b = after([route_b], ahead=1<<33)[0]
    joined = jnp.concatenate([w_gate[0], w_up[0], w_down_t[0]], axis=1)
    joined_1, joined_2 = over_own(joined, 1), over_own(joined, 2)
    slot_rows = pltpu.VMEM((slots, model_width), BF16)
    pick, own_x, near, far_xa, far_xb = call(
        functools.partial(pack_kernel, capacity),
        [shape(slots, 2 * tok_rows), shape(block, model_width), shape(2 * block, model_width)]
        + [shape(block, model_width)] * 2,
        2,
        [pltpu.VMEM((2 * tok_rows, model_width), BF16)],
    )(rank, host, route, route_b, tokens, tokens_b, cotangent, cotangent_b)
    far_xa, far_xb = after([over_rep(far_xa, 4), over_rep(far_xb, 6)], ahead=1<<29)
    near = over_rep(near, 2)
    own_dy, far_a, far_b = call(pack_more_kernel, [shape(block, model_width)] * 3)(pick, cotangent, cotangent_b)

    onward = shape(depth // 2 + depth // 4 + slots, depth)
    x, piece_0, piece_3, onward_1, onward_2 = call(
        spread_kernel,
        [shape(slots, model_width), shape(slots, depth), shape(slots, depth), onward, onward],
        1,
        earlier=[own_dy],
    )(own, own_x, near, far_xa, far_xb, joined_1, joined_2)
    far_a, far_b = after([far_a, far_b], far_xa, far_xb)
    far_a, far_b = after([over_rep(far_a, 4), over_rep(far_b, 6)], ahead=AHEAD)
    onward_1, onward_2, piece_3 = over_own(onward_1, 1), over_own(onward_2, 2), over_own(piece_3, 3)
    weights = [joined, joined_1, joined_2]
    acts = call(act_kernel, [shape(slots, 2 * width, F32)], 1)(own, x, *weights)[0]

    message = shape(slots + depth // 2, 2 * width)
    *back, own_term, grads, message_1, message_2, message_3 = call(
        grad_kernel,
        [shape(block, model_width)] * parts
        + [shape(depth, width, F32), shape(slots, 2 * width), message, message, message],
        1,
        [slot_rows],
        earlier=[piece_3],
    )(own, acts, x, own_dy, near, far_a, far_b, *weights, onward_2, onward_1)
    far_a, far_b = after([over_rep(back[2], 4), over_rep(back[3], 6)], ahead=1<<33)
    returned = [back[0], over_rep(after(back[1:2], far_a, far_b)[0], 2), far_a, far_b]
    messages = after([over_own(message_1, 1), over_own(message_2, 2), over_own(message_3, 3)], ahead=AHEAD)

    mine, other = call(unpack_kernel, [shape(tok_rows, model_width)] * 2, 0, [slot_rows])(
        pick, *returned
    )
    x_grad = mine + over_rep(other, 1)
    out = call(sum_kernel, [shape(depth, width, F32)] * 3, 0, [pltpu.VMEM((4 * slots, depth), BF16)] * 2)(
        piece_0, onward_1, onward_2, piece_3, grads, *messages, own_term
    )
    return (x_grad, *(grad[None] for grad in out))


def shards_whole(tokens, cotangent, route, host, w_gate, w_up, w_down_t):
    tok_rows, model_width = tokens.shape
    hot = host.shape[0]
    width = w_gate.shape[2]
    capacity = max(2, (3 * tok_rows + 2 * hot - 1) // (2 * hot))
    slots = hot * capacity
    labels = lax.broadcasted_iota(jnp.int32, (tok_rows, hot), 1)
    target = jnp.sum(jnp.where(route == labels, host[None, :], 0), axis=1)
    marked = (target[:, None] == labels).astype(jnp.int32)
    arrival = jnp.sum(jnp.cumsum(marked, axis=0) * marked, axis=1) - 1
    position = target * capacity + arrival
    pick = (lax.broadcasted_iota(jnp.int32, (slots, tok_rows), 0) == position[None, :]).astype(BF16)

    def exchange(value):
        split = value.astype(BF16).reshape(hot, capacity, model_width)
        return lax.all_to_all(split, "rep", split_axis=0, concat_axis=0, tiled=True).reshape(slots, model_width)

    slot_x, slot_dy = exchange(dot(pick, tokens, 1, 0)), exchange(dot(pick, cotangent, 1, 0))
    gate, up, down = (lax.all_gather(w[0], "own", axis=0, tiled=True) for w in (w_gate, w_up, w_down_t))
    gate_act, up_act, back_grad = dot(slot_x, gate, 1, 0), dot(slot_x, up, 1, 0), dot(slot_dy, down, 1, 0)
    sigmoid_g = jax.nn.sigmoid(gate_act)
    silu_gate = gate_act * sigmoid_g
    hidden = (silu_gate * up_act).astype(BF16)
    grad_gate_h = (back_grad * up_act * sigmoid_g * (1.0 + gate_act * (1.0 - sigmoid_g))).astype(BF16)
    grad_up_h = (back_grad * silu_gate).astype(BF16)
    returned = exchange(dot(grad_gate_h, gate, 1, 1) + dot(grad_up_h, up, 1, 1))
    x_grad = dot(pick, returned, 0, 0).astype(BF16)
    terms = [dot(slot_x, grad_gate_h, 0, 0), dot(slot_x, grad_up_h, 0, 0), dot(slot_dy, hidden, 0, 0)]
    summed = lax.psum_scatter(
        jnp.concatenate(terms, axis=1).astype(BF16), "own", scatter_dimension=0, tiled=True
    ).astype(F32)
    return (x_grad, *(summed[None, :, i * width : (i + 1) * width] for i in range(3)))


def solution(mesh):
    n_own, n_rep = mesh.shape["own"], mesh.shape["rep"]

    def shards(tokens, *rest):
        capacity = (3 * tokens.shape[0] + 2 * n_rep - 1) // (2 * n_rep)
        if n_own == 4 and n_rep == 8 and capacity % 8 == 0:
            return shards_by_partner(n_rep, tokens, *rest)
        return shards_whole(tokens, *rest)

    return jax.shard_map(
        shards,
        mesh=mesh,
        in_specs=(
            P(("own", "rep"), None),
            P(("own", "rep"), None),
            P(("own", "rep"), None),
            P(),
            P("rep", "own", None),
            P("rep", "own", None),
            P("rep", "own", None),
        ),
        out_specs=(
            P(("own", "rep"), None),
            P("rep", "own", None),
            P("rep", "own", None),
            P("rep", "own", None),
        ),
        check_vma=False,
    )
```

```python
import functools

import jax
import jax.numpy as jnp
from jax import lax
from jax.experimental import pallas as pl
from jax.experimental.pallas import tpu as pltpu
from jax.sharding import PartitionSpec as P

VMEM = pl.BlockSpec(memory_space=pltpu.VMEM)
SMEM = pl.BlockSpec(memory_space=pltpu.SMEM)
ANY = pl.BlockSpec(memory_space=pl.ANY)
MIB = 1024 * 1024
AHEAD = 1 << 33
BF16 = jnp.bfloat16
F32 = jnp.float32


def dot(left, right, left_dim, right_dim):
    return lax.dot_general(
        left, right, (((left_dim,), (right_dim,)), ((), ())), preferred_element_type=F32
    )


def shape(rows, cols, dtype=BF16):
    return jax.ShapeDtypeStruct((rows, cols), dtype)


def call(kernel, outs, scalars=0, scratch=(), earlier=()):
    earlier = list(earlier)

    def body(*refs):
        inputs = len(refs) - len(outs) - len(scratch)
        kernel(*refs[: inputs - len(earlier)], *refs[inputs:])

    def run(*operands):
        moved = sum(value.size * value.dtype.itemsize for value in (*operands, *outs))
        return pl.pallas_call(
            body,
            out_shape=outs,
            in_specs=[SMEM] * scalars + [VMEM] * (len(operands) - scalars) + [ANY] * len(earlier),
            out_specs=[VMEM] * len(outs),
            scratch_shapes=list(scratch),
            cost_estimate=pl.CostEstimate(flops=0, bytes_accessed=moved, transcendentals=0),
            compiler_params=pltpu.CompilerParams(vmem_limit_bytes=32 * MIB),
        )(*operands, *earlier)

    return run


def after(values, *earlier, ahead=0):
    return pl.pallas_call(
        lambda *refs: None,
        out_shape=[shape(*value.shape, value.dtype) for value in values],
        in_specs=[ANY] * (len(values) + len(earlier)),
        out_specs=[ANY] * len(values),
        input_output_aliases={i: i for i in range(len(values))},
        cost_estimate=pl.CostEstimate(flops=ahead, bytes_accessed=0, transcendentals=0),
        compiler_params=pltpu.CompilerParams(vmem_limit_bytes=MIB),
    )(*values, *earlier)


def picks(capacity, offset, rank_ref, host_ref, route_ref, slots):
    hot = host_ref.shape[0]
    tokens = route_ref.shape[1]
    label = lax.broadcasted_iota(jnp.int32, (hot, tokens), 0)
    base = jnp.zeros((hot, tokens), jnp.int32)
    for e in range(hot):
        apart = host_ref[e] ^ rank_ref[0]
        start = jnp.where((apart & 1) == 0, (apart >> 1) * (2 * capacity), -2 * slots)
        base = jnp.where(label == e, start, base)
    earlier = lax.broadcasted_iota(jnp.int32, (tokens, tokens), 0) < lax.broadcasted_iota(
        jnp.int32, (tokens, tokens), 1
    )
    marked = route_ref[...] == label
    before = dot(jnp.where(marked, 1.0, 0.0).astype(BF16), jnp.where(earlier, 1.0, 0.0).astype(BF16), 1, 0)
    position = jnp.sum(jnp.where(marked, before.astype(jnp.int32) + base, 0), axis=0, keepdims=True) + offset
    slot = lax.broadcasted_iota(jnp.int32, (slots, tokens), 0)
    return jnp.where(slot == position, 1.0, 0.0).astype(BF16)


def pack_kernel(capacity, rank_ref, host_ref, route_a, route_b, x_a, x_b, dy_a, dy_b, pick_ref, *refs):
    *send_refs, rows_ref = refs
    slots = pick_ref.shape[0]
    tokens = route_a.shape[1]
    block = 2 * capacity
    pick_ref[:, :tokens] = picks(capacity, 0, rank_ref, host_ref, route_a, slots)
    pick_ref[:, tokens:] = picks(capacity, capacity, rank_ref, host_ref, route_b, slots)
    rows_ref[:tokens] = x_a[...]
    rows_ref[tokens:] = x_b[...]
    filled = dot(pick_ref[...], rows_ref[...], 1, 0).astype(BF16)
    for k, ref in enumerate(send_refs):
        ref[:block] = filled[k * block : (k + 1) * block]
    near = slice(block, 2 * block)
    send_refs[1][block:] = (
        dot(pick_ref[near, :tokens], dy_a[...], 1, 0) + dot(pick_ref[near, tokens:], dy_b[...], 1, 0)
    ).astype(BF16)


def pack_more_kernel(pick_ref, own_ref, other_ref, *send_refs):
    tokens = own_ref.shape[0]
    block = send_refs[0].shape[0]
    filled = (
        dot(pick_ref[:, :tokens], own_ref[...], 1, 0) + dot(pick_ref[:, tokens:], other_ref[...], 1, 0)
    ).astype(BF16)
    for k, ref in zip((0, 2, 3), send_refs):
        ref[...] = filled[k * block : (k + 1) * block]


def columns_of(own_ref, depth):
    return [pl.ds(pl.multiple_of((own_ref[0] ^ k) * depth, depth), depth) for k in range(4)]


def onward_parts(own_ref, onward):
    for at, ref in enumerate(onward):
        half = ref.shape[1] // 2
        quarter = half // 2
        start = ((own_ref[0] ^ 3) * 2 + at) * half
        both = pl.ds(pl.multiple_of(start, half), half), ref[:half]
        downs = [
            (
                pl.ds(pl.multiple_of(start + i * quarter, quarter), quarter),
                ref[half : half + quarter, i * half : (i + 1) * half],
            )
            for i in range(2)
        ]
        yield both, downs


def spread_kernel(own_ref, *refs):
    got, (joined_1, joined_2), (x_ref, piece_0, piece_3, onward_1, onward_2) = refs[:4], refs[4:6], refs[6:]
    slots, depth = piece_0.shape
    block = slots // 4
    half, quarter = depth // 2, depth // 4
    columns = columns_of(own_ref, depth)
    for j, ref in enumerate(got):
        rows = pl.ds(j * block, block)
        x_ref[rows] = ref[:block]
        for into, cols in zip(
            (piece_0, onward_1.at[pl.ds(half + quarter, slots)], onward_2.at[pl.ds(half + quarter, slots)], piece_3),
            columns,
        ):
            into[rows] = ref[:block, cols]
    for joined, start, into in ((joined_2, half, onward_1), (joined_1, 0, onward_2)):
        into[:half] = joined[start : start + half, :depth]
        into[half : half + quarter, :half] = joined[start : start + quarter, depth:]
        into[half : half + quarter, half:] = joined[start + quarter : start + half, depth:]


def act_kernel(own_ref, x_ref, *refs):
    weights, acts_ref = refs[:-1], refs[-1]
    both = acts_ref.shape[1]
    columns = columns_of(own_ref, weights[0].shape[0])
    acts_ref[...] = sum(dot(x_ref[:, cols], ref[:, :both], 1, 0) for cols, ref in zip(columns, weights))


def grad_kernel(own_ref, acts_ref, x_ref, *refs):
    got, weights, onward, outs, dy_ref = refs[:4], refs[4:7], refs[7:9], refs[9:-1], refs[-1]
    back_refs, own_term, (own_grads, *messages) = outs[:4], outs[4], outs[5:]
    slots, both = acts_ref.shape
    width = both // 2
    block = slots // 4
    depth = weights[0].shape[0]
    half = depth // 2
    columns = columns_of(own_ref, depth)
    for j, ref in enumerate(got):
        dy_ref[j * block : (j + 1) * block] = ref[ref.shape[0] - block :]
    acts = acts_ref[...]
    back_grad = sum(dot(dy_ref[:, cols], ref[:, both:], 1, 0) for cols, ref in zip(columns, weights))
    for (cols, rows), downs in onward_parts(own_ref, onward):
        acts += dot(x_ref[:, cols], rows, 1, 0)
        for cols, rows in downs:
            back_grad += dot(dy_ref[:, cols], rows, 1, 0)
    gate_act, up_act = acts[:, :width], acts[:, width:]
    sigmoid_g = jax.nn.sigmoid(gate_act)
    silu_gate = gate_act * sigmoid_g
    hidden = (silu_gate * up_act).astype(BF16)
    gate_h = back_grad * up_act * sigmoid_g * (1.0 + gate_act * (1.0 - sigmoid_g))
    own_grads[:, :width] = gate_h.astype(BF16)
    own_grads[:, width:] = (back_grad * silu_gate).astype(BF16)
    grads = own_grads[...]
    for k, cols in enumerate(columns):
        term = dot(dy_ref[:, cols], hidden, 0, 0)
        if k == 0:
            own_term[...] = term
        else:
            messages[k - 1][:slots] = grads
            messages[k - 1][slots:, :width] = term[:half].astype(BF16)
            messages[k - 1][slots:, width:] = term[half:].astype(BF16)
    pairs = [(cols, ref[:, :both]) for cols, ref in zip(columns, weights)]
    for cols, rows in pairs + [part for part, _ in onward_parts(own_ref, onward)]:
        slot_grad = dot(grads, rows, 1, 1).astype(BF16)
        for j, back_ref in enumerate(back_refs):
            back_ref[:, cols] = slot_grad[j * block : (j + 1) * block]


def sum_kernel(*refs):
    pieces, messages, own_term = refs[:4], refs[4:8], refs[8]
    (gate_ref, up_ref, down_ref), (x_ref, grads_ref) = refs[9:12], refs[12:]
    slots = pieces[0].shape[0]
    depth, width = gate_ref.shape
    half = depth // 2
    for k, (piece, got) in enumerate(zip(pieces, messages)):
        x_ref[k * slots : (k + 1) * slots] = piece[-slots:]
        grads_ref[k * slots : (k + 1) * slots] = got[:slots]
    total = dot(x_ref[...], grads_ref[...], 0, 0)
    gate_ref[...] = total[:, :width]
    up_ref[...] = total[:, width:]
    for rows, cols in ((slice(0, half), slice(0, width)), (slice(half, depth), slice(width, 2 * width))):
        down_ref[rows] = own_term[rows] + sum(got[slots:, cols].astype(F32) for got in messages[1:])


def unpack_kernel(pick_ref, *refs):
    returned, (mine_ref, other_ref, rows_ref) = refs[:-3], refs[-3:]
    tokens = mine_ref.shape[0]
    block = returned[0].shape[0]
    for k, ref in enumerate(returned):
        rows_ref[k * block : (k + 1) * block] = ref[...]
    both = dot(pick_ref[...], rows_ref[...], 0, 0).astype(BF16)
    mine_ref[...] = both[:tokens]
    other_ref[...] = both[tokens:]


def shards_by_partner(n_rep, tokens, cotangent, route, host, w_gate, w_up, w_down_t):
    tok_rows, model_width = tokens.shape
    hot = host.shape[0]
    _, depth, width = w_gate.shape
    capacity = (3 * tok_rows + 2 * hot - 1) // (2 * hot)
    slots = hot * capacity
    parts = n_rep // 2
    block = 2 * capacity
    own = lax.axis_index("own").astype(jnp.int32).reshape(1)
    rank = lax.axis_index("rep").astype(jnp.int32).reshape(1)

    def over_own(value, k):
        return lax.ppermute(value, "own", [(i, i ^ k) for i in range(4)])

    def over_rep(value, k):
        return lax.ppermute(value, "rep", [(i, i ^ k) for i in range(n_rep)])

    route = route.reshape(1, tok_rows)
    route_b, tokens_b, cotangent_b = over_rep(route, 1), over_rep(tokens, 1), over_rep(cotangent, 1)
    joined = jnp.concatenate([w_gate[0], w_up[0], w_down_t[0]], axis=1)
    joined_1, joined_2 = over_own(joined, 1), over_own(joined, 2)
    slot_rows = pltpu.VMEM((slots, model_width), BF16)
    pick, own_x, near, far_xa, far_xb = call(
        functools.partial(pack_kernel, capacity),
        [shape(slots, 2 * tok_rows), shape(block, model_width), shape(2 * block, model_width)]
        + [shape(block, model_width)] * 2,
        2,
        [pltpu.VMEM((2 * tok_rows, model_width), BF16)],
    )(rank, host, route, route_b, tokens, tokens_b, cotangent, cotangent_b)
    far_xa, far_xb = after([over_rep(far_xa, 4), over_rep(far_xb, 6)], ahead=1 << 31)
    near = over_rep(near, 2)
    own_dy, far_a, far_b = call(pack_more_kernel, [shape(block, model_width)] * 3)(pick, cotangent, cotangent_b)

    onward = shape(depth // 2 + depth // 4 + slots, depth)
    x, piece_0, piece_3, onward_1, onward_2 = call(
        spread_kernel,
        [shape(slots, model_width), shape(slots, depth), shape(slots, depth), onward, onward],
        1,
        earlier=[own_dy],
    )(own, own_x, near, far_xa, far_xb, joined_1, joined_2)
    far_a, far_b = after([far_a, far_b], piece_0)
    far_a, far_b = after([over_rep(far_a, 4), over_rep(far_b, 6)], ahead=AHEAD)
    onward_1, onward_2, piece_3 = over_own(onward_1, 1), over_own(onward_2, 2), over_own(piece_3, 3)
    weights = [joined, joined_1, joined_2]
    acts = call(act_kernel, [shape(slots, 2 * width, F32)], 1)(own, x, *weights)[0]

    message = shape(slots + depth // 2, 2 * width)
    *back, own_term, grads, message_1, message_2, message_3 = call(
        grad_kernel,
        [shape(block, model_width)] * parts
        + [shape(depth, width, F32), shape(slots, 2 * width), message, message, message],
        1,
        [slot_rows],
        earlier=[piece_3],
    )(own, acts, x, own_dy, near, far_a, far_b, *weights, onward_2, onward_1)
    returned = [over_rep(back[1], 2), over_rep(back[2], 4)]
    last = over_rep(after(back[3:], returned[0])[0], 6)
    returned = [back[0], *after(returned, ahead=AHEAD), last]
    messages = after([over_own(message_1, 1), over_own(message_2, 2), over_own(message_3, 3)], ahead=AHEAD)

    mine, other = call(unpack_kernel, [shape(tok_rows, model_width)] * 2, 0, [slot_rows])(
        pick, *returned
    )
    x_grad = mine + over_rep(other, 1)
    out = call(sum_kernel, [shape(depth, width, F32)] * 3, 0, [pltpu.VMEM((4 * slots, depth), BF16)] * 2)(
        piece_0, onward_1, onward_2, piece_3, grads, *messages, own_term
    )
    return (x_grad, *(grad[None] for grad in out))


def shards_whole(tokens, cotangent, route, host, w_gate, w_up, w_down_t):
    tok_rows, model_width = tokens.shape
    hot = host.shape[0]
    width = w_gate.shape[2]
    capacity = max(2, (3 * tok_rows + 2 * hot - 1) // (2 * hot))
    slots = hot * capacity
    labels = lax.broadcasted_iota(jnp.int32, (tok_rows, hot), 1)
    target = jnp.sum(jnp.where(route == labels, host[None, :], 0), axis=1)
    marked = (target[:, None] == labels).astype(jnp.int32)
    arrival = jnp.sum(jnp.cumsum(marked, axis=0) * marked, axis=1) - 1
    position = target * capacity + arrival
    pick = (lax.broadcasted_iota(jnp.int32, (slots, tok_rows), 0) == position[None, :]).astype(BF16)

    def exchange(value):
        split = value.astype(BF16).reshape(hot, capacity, model_width)
        return lax.all_to_all(split, "rep", split_axis=0, concat_axis=0, tiled=True).reshape(slots, model_width)

    slot_x, slot_dy = exchange(dot(pick, tokens, 1, 0)), exchange(dot(pick, cotangent, 1, 0))
    gate, up, down = (lax.all_gather(w[0], "own", axis=0, tiled=True) for w in (w_gate, w_up, w_down_t))
    gate_act, up_act, back_grad = dot(slot_x, gate, 1, 0), dot(slot_x, up, 1, 0), dot(slot_dy, down, 1, 0)
    sigmoid_g = jax.nn.sigmoid(gate_act)
    silu_gate = gate_act * sigmoid_g
    hidden = (silu_gate * up_act).astype(BF16)
    grad_gate_h = (back_grad * up_act * sigmoid_g * (1.0 + gate_act * (1.0 - sigmoid_g))).astype(BF16)
    grad_up_h = (back_grad * silu_gate).astype(BF16)
    returned = exchange(dot(grad_gate_h, gate, 1, 1) + dot(grad_up_h, up, 1, 1))
    x_grad = dot(pick, returned, 0, 0).astype(BF16)
    terms = [dot(slot_x, grad_gate_h, 0, 0), dot(slot_x, grad_up_h, 0, 0), dot(slot_dy, hidden, 0, 0)]
    summed = lax.psum_scatter(
        jnp.concatenate(terms, axis=1).astype(BF16), "own", scatter_dimension=0, tiled=True
    ).astype(F32)
    return (x_grad, *(summed[None, :, i * width : (i + 1) * width] for i in range(3)))


def solution(mesh):
    n_own, n_rep = mesh.shape["own"], mesh.shape["rep"]

    def shards(tokens, *rest):
        capacity = (3 * tokens.shape[0] + 2 * n_rep - 1) // (2 * n_rep)
        if n_own == 4 and n_rep == 8 and capacity % 8 == 0:
            return shards_by_partner(n_rep, tokens, *rest)
        return shards_whole(tokens, *rest)

    return jax.shard_map(
        shards,
        mesh=mesh,
        in_specs=(
            P(("own", "rep"), None),
            P(("own", "rep"), None),
            P(("own", "rep"), None),
            P(),
            P("rep", "own", None),
            P("rep", "own", None),
            P("rep", "own", None),
        ),
        out_specs=(
            P(("own", "rep"), None),
            P("rep", "own", None),
            P("rep", "own", None),
            P("rep", "own", None),
        ),
        check_vma=False,
    )
```

```python
import functools

import jax
import jax.numpy as jnp
from jax import lax
from jax.experimental import pallas as pl
from jax.experimental.pallas import tpu as pltpu
from jax.sharding import PartitionSpec as P

VMEM = pl.BlockSpec(memory_space=pltpu.VMEM)
SMEM = pl.BlockSpec(memory_space=pltpu.SMEM)
ANY = pl.BlockSpec(memory_space=pl.ANY)
MIB = 1024 * 1024
BF16 = jnp.bfloat16
F32 = jnp.float32


def dot(left, right, left_dim, right_dim):
    return lax.dot_general(
        left, right, (((left_dim,), (right_dim,)), ((), ())), preferred_element_type=F32
    )


def shape(rows, cols, dtype=BF16):
    return jax.ShapeDtypeStruct((rows, cols), dtype)


def call(kernel, outs, scalars=0, scratch=(), earlier=()):
    earlier = list(earlier)

    def body(*refs):
        inputs = len(refs) - len(outs) - len(scratch)
        kernel(*refs[: inputs - len(earlier)], *refs[inputs:])

    def run(*operands):
        moved = sum(value.size * value.dtype.itemsize for value in (*operands, *outs))
        return pl.pallas_call(
            body,
            out_shape=outs,
            in_specs=[SMEM] * scalars + [VMEM] * (len(operands) - scalars) + [ANY] * len(earlier),
            out_specs=[VMEM] * len(outs),
            scratch_shapes=list(scratch),
            cost_estimate=pl.CostEstimate(flops=0, bytes_accessed=moved, transcendentals=0),
            compiler_params=pltpu.CompilerParams(vmem_limit_bytes=32 * MIB),
        )(*operands, *earlier)

    return run


def after(values, *earlier, ahead=0):
    return pl.pallas_call(
        lambda *refs: None,
        out_shape=[shape(*value.shape, value.dtype) for value in values],
        in_specs=[ANY] * (len(values) + len(earlier)),
        out_specs=[ANY] * len(values),
        input_output_aliases={i: i for i in range(len(values))},
        cost_estimate=pl.CostEstimate(flops=ahead, bytes_accessed=0, transcendentals=0),
        compiler_params=pltpu.CompilerParams(vmem_limit_bytes=MIB),
    )(*values, *earlier)


def picks(capacity, offset, rank_ref, host_ref, route_ref, slots):
    hot = host_ref.shape[0]
    tokens = route_ref.shape[1]
    label = lax.broadcasted_iota(jnp.int32, (hot, tokens), 0)
    base = jnp.zeros((hot, tokens), jnp.int32)
    for e in range(hot):
        apart = host_ref[e] ^ rank_ref[0]
        start = jnp.where((apart & 1) == 0, (apart >> 1) * (2 * capacity), -2 * slots)
        base = jnp.where(label == e, start, base)
    earlier = lax.broadcasted_iota(jnp.int32, (tokens, tokens), 0) < lax.broadcasted_iota(
        jnp.int32, (tokens, tokens), 1
    )
    marked = route_ref[...] == label
    before = dot(jnp.where(marked, 1.0, 0.0).astype(BF16), jnp.where(earlier, 1.0, 0.0).astype(BF16), 1, 0)
    position = jnp.sum(jnp.where(marked, before.astype(jnp.int32) + base, 0), axis=0, keepdims=True) + offset
    slot = lax.broadcasted_iota(jnp.int32, (slots, tokens), 0)
    return jnp.where(slot == position, 1.0, 0.0).astype(BF16)


def pack_kernel(capacity, rank_ref, host_ref, route_a, route_b, x_a, x_b, dy_a, dy_b, pick_ref, *refs):
    *send_refs, rows_ref = refs
    slots = pick_ref.shape[0]
    tokens = route_a.shape[1]
    block = 2 * capacity
    pick_ref[:, :tokens] = picks(capacity, 0, rank_ref, host_ref, route_a, slots)
    pick_ref[:, tokens:] = picks(capacity, capacity, rank_ref, host_ref, route_b, slots)
    rows_ref[:tokens] = x_a[...]
    rows_ref[tokens:] = x_b[...]
    filled = dot(pick_ref[...], rows_ref[...], 1, 0).astype(BF16)
    for k, ref in enumerate(send_refs):
        ref[:block] = filled[k * block : (k + 1) * block]
    near = slice(block, 2 * block)
    send_refs[1][block:] = (
        dot(pick_ref[near, :tokens], dy_a[...], 1, 0) + dot(pick_ref[near, tokens:], dy_b[...], 1, 0)
    ).astype(BF16)


def pack_more_kernel(pick_ref, own_ref, other_ref, *send_refs):
    tokens = own_ref.shape[0]
    block = send_refs[0].shape[0]
    filled = (
        dot(pick_ref[:, :tokens], own_ref[...], 1, 0) + dot(pick_ref[:, tokens:], other_ref[...], 1, 0)
    ).astype(BF16)
    for k, ref in zip((0, 2, 3), send_refs):
        ref[...] = filled[k * block : (k + 1) * block]


def weight_parts(own_ref, weights):
    depth = weights[0].shape[0]
    half = depth // 2
    for k, ref in enumerate(weights):
        partner, start = (k, 0) if k < 3 else (3, (k - 3) * half)
        yield pl.ds(pl.multiple_of((own_ref[0] ^ partner) * depth + start, half), ref.shape[0]), ref


def columns_of(own_ref, depth):
    return [pl.ds(pl.multiple_of((own_ref[0] ^ k) * depth, depth), depth) for k in range(4)]


def spread_kernel(own_ref, *refs):
    got, own_dy, (x_ref, *piece_refs) = refs[:4], refs[4], refs[5:]
    slots = x_ref.shape[0]
    block = slots // 4
    columns = columns_of(own_ref, piece_refs[0].shape[1])
    for j, ref in enumerate(got):
        rows = slice(j * block, (j + 1) * block)
        x_ref[rows] = ref[:block]
        for cols, piece_ref in zip(columns, piece_refs):
            piece_ref[rows] = ref[:block, cols]
    for cols, piece_ref in zip(columns, piece_refs):
        piece_ref[slots : slots + block] = own_dy[:, cols]
        piece_ref[slots + block :] = got[1][block:, cols]


def act_kernel(own_ref, x_ref, *refs):
    weights, acts_ref = refs[:-1], refs[-1]
    both = acts_ref.shape[1]
    acts_ref[...] = sum(dot(x_ref[:, cols], ref[:, :both], 1, 0) for cols, ref in weight_parts(own_ref, weights))


def grad_kernel(parts, own_ref, acts_ref, *refs):
    got, weights, outs, dy_ref = refs[:parts], refs[parts : parts + 5], refs[parts + 5 : -1], refs[-1]
    back_refs, messages = outs[:parts], outs[parts:]
    slots, both = acts_ref.shape
    width = both // 2
    half = slots // 2
    block = slots // parts
    depth = weights[0].shape[0]
    for j, ref in enumerate(got):
        dy_ref[j * block : (j + 1) * block] = ref[ref.shape[0] - block :]
    back_grad = sum(dot(dy_ref[:, cols], ref[:, both:], 1, 0) for cols, ref in weight_parts(own_ref, weights))
    gate_act, up_act = acts_ref[:, :width], acts_ref[:, width:]
    sigmoid_g = jax.nn.sigmoid(gate_act)
    silu_gate = gate_act * sigmoid_g
    hidden = (silu_gate * up_act).astype(BF16)
    gate_h = (back_grad * up_act * sigmoid_g * (1.0 + gate_act * (1.0 - sigmoid_g))).astype(BF16)
    up_h = (back_grad * silu_gate).astype(BF16)
    for message, cols in zip(messages, columns_of(own_ref, depth)):
        message[:slots, :width] = gate_h
        message[:slots, width:] = up_h
        message[slots : slots + half, :width] = hidden[:half]
        message[slots : slots + half, width:] = hidden[half:]
        message[slots + half :] = dy_ref[half:, cols]
    grads = messages[0][:slots]
    for cols, ref in weight_parts(own_ref, weights):
        slot_grad = dot(grads, ref[:, :both], 1, 1).astype(BF16)
        for j, back_ref in enumerate(back_refs):
            back_ref[:, cols] = slot_grad[j * block : (j + 1) * block]


def sum_kernel(*refs):
    pieces, messages = refs[:4], refs[4:8]
    (gate_ref, up_ref, down_ref), (x_ref, dy_ref, grads_ref, hidden_ref) = refs[8:11], refs[11:]
    width = gate_ref.shape[1]
    slots = x_ref.shape[0] // 4
    half = slots // 2
    for k, (piece, got) in enumerate(zip(pieces, messages)):
        start, middle, stop = k * slots, k * slots + half, (k + 1) * slots
        x_ref[start:stop] = piece[:slots]
        dy_ref[start:middle] = piece[slots:]
        dy_ref[middle:stop] = got[slots + half :]
        grads_ref[start:stop] = got[:slots]
        hidden_ref[start:middle] = got[slots : slots + half, :width]
        hidden_ref[middle:stop] = got[slots : slots + half, width:]
    total = dot(x_ref[...], grads_ref[...], 0, 0)
    gate_ref[...] = total[:, :width]
    up_ref[...] = total[:, width:]
    down_ref[...] = dot(dy_ref[...], hidden_ref[...], 0, 0)


def unpack_kernel(pick_ref, *refs):
    returned, (mine_ref, other_ref, rows_ref) = refs[:-3], refs[-3:]
    tokens = mine_ref.shape[0]
    block = returned[0].shape[0]
    for k, ref in enumerate(returned):
        rows_ref[k * block : (k + 1) * block] = ref[...]
    both = dot(pick_ref[...], rows_ref[...], 0, 0).astype(BF16)
    mine_ref[...] = both[:tokens]
    other_ref[...] = both[tokens:]


def shards_by_partner(n_rep, tokens, cotangent, route, host, w_gate, w_up, w_down_t):
    tok_rows, model_width = tokens.shape
    hot = host.shape[0]
    _, depth, width = w_gate.shape
    capacity = (3 * tok_rows + 2 * hot - 1) // (2 * hot)
    slots = hot * capacity
    parts = n_rep // 2
    block = 2 * capacity
    own = lax.axis_index("own").astype(jnp.int32).reshape(1)
    rank = lax.axis_index("rep").astype(jnp.int32).reshape(1)

    def over_own(value, k):
        return lax.ppermute(value, "own", [(i, i ^ k) for i in range(4)])

    def over_rep(value, k):
        return lax.ppermute(value, "rep", [(i, i ^ k) for i in range(n_rep)])

    route = route.reshape(1, tok_rows)
    route_b, tokens_b, cotangent_b = over_rep(route, 1), over_rep(tokens, 1), over_rep(cotangent, 1)
    joined = jnp.concatenate([w_gate[0], w_up[0], w_down_t[0]], axis=1)
    joined_1, joined_2 = over_own(joined, 1), over_own(joined, 2)
    slot_rows = pltpu.VMEM((slots, model_width), BF16)
    pick, own_x, near, far_xa, far_xb = call(
        functools.partial(pack_kernel, capacity),
        [shape(slots, 2 * tok_rows), shape(block, model_width), shape(2 * block, model_width)]
        + [shape(block, model_width)] * 2,
        2,
        [pltpu.VMEM((2 * tok_rows, model_width), BF16)],
    )(rank, host, route, route_b, tokens, tokens_b, cotangent, cotangent_b)
    far_x = [over_rep(far_xa, 4), over_rep(far_xb, 6)]
    far_x = after(far_x, ahead=1<<31)
    near = over_rep(near, 2)
    own_dy, far_a, far_b = call(pack_more_kernel, [shape(block, model_width)] * 3)(pick, cotangent, cotangent_b)
    joined_3 = [over_own(joined_1[: depth // 2], 2), over_own(joined_2[depth // 2 :], 1)]
    joined_3 = after(joined_3, ahead=1<<33)
    weights = [joined, joined_1, joined_2, *joined_3]

    x, *pieces = call(spread_kernel, [shape(slots, model_width)] + [shape(slots + slots // 2, depth)] * 4, 1)(
        own, own_x, near, *far_x, own_dy
    )
    far_dy = after([far_a, far_b], pieces[0])
    far_dy = [over_rep(far_dy[0], 4), over_rep(far_dy[1], 6)]
    pieces = [pieces[0]] + [over_own(pieces[k], k) for k in range(1, 4)]
    acts = call(act_kernel, [shape(slots, 2 * width, F32)], 1)(own, x, *weights)[0]

    *back, own_message, message_1, message_2, message_3 = call(
        functools.partial(grad_kernel, parts),
        [shape(block, model_width)] * parts + [shape(2 * slots, 2 * width)] * 4,
        1,
        [slot_rows],
        earlier=pieces[1:],
    )(own, acts, own_dy, near, *far_dy, *weights)
    returned = [back[0]] + [over_rep(back[k], 2 * k) for k in range(1, parts)]
    messages = [own_message, over_own(message_1, 1), over_own(message_2, 2), over_own(message_3, 3)]

    mine, other = call(unpack_kernel, [shape(tok_rows, model_width)] * 2, 0, [slot_rows], earlier=messages[1:])(
        pick, *returned
    )
    x_grad = mine + over_rep(other, 1)
    out = call(
        sum_kernel,
        [shape(depth, width, F32)] * 3,
        0,
        [pltpu.VMEM((4 * slots, cols), BF16) for cols in (depth, depth, 2 * width, width)],
    )(*pieces, *messages)
    return (x_grad, *(grad[None] for grad in out))


def shards_whole(tokens, cotangent, route, host, w_gate, w_up, w_down_t):
    tok_rows, model_width = tokens.shape
    hot = host.shape[0]
    width = w_gate.shape[2]
    capacity = max(2, (3 * tok_rows + 2 * hot - 1) // (2 * hot))
    slots = hot * capacity
    labels = lax.broadcasted_iota(jnp.int32, (tok_rows, hot), 1)
    target = jnp.sum(jnp.where(route == labels, host[None, :], 0), axis=1)
    marked = (target[:, None] == labels).astype(jnp.int32)
    arrival = jnp.sum(jnp.cumsum(marked, axis=0) * marked, axis=1) - 1
    position = target * capacity + arrival
    pick = (lax.broadcasted_iota(jnp.int32, (slots, tok_rows), 0) == position[None, :]).astype(BF16)

    def exchange(value):
        split = value.astype(BF16).reshape(hot, capacity, model_width)
        return lax.all_to_all(split, "rep", split_axis=0, concat_axis=0, tiled=True).reshape(slots, model_width)

    slot_x, slot_dy = exchange(dot(pick, tokens, 1, 0)), exchange(dot(pick, cotangent, 1, 0))
    gate, up, down = (lax.all_gather(w[0], "own", axis=0, tiled=True) for w in (w_gate, w_up, w_down_t))
    gate_act, up_act, back_grad = dot(slot_x, gate, 1, 0), dot(slot_x, up, 1, 0), dot(slot_dy, down, 1, 0)
    sigmoid_g = jax.nn.sigmoid(gate_act)
    silu_gate = gate_act * sigmoid_g
    hidden = (silu_gate * up_act).astype(BF16)
    grad_gate_h = (back_grad * up_act * sigmoid_g * (1.0 + gate_act * (1.0 - sigmoid_g))).astype(BF16)
    grad_up_h = (back_grad * silu_gate).astype(BF16)
    returned = exchange(dot(grad_gate_h, gate, 1, 1) + dot(grad_up_h, up, 1, 1))
    x_grad = dot(pick, returned, 0, 0).astype(BF16)
    terms = [dot(slot_x, grad_gate_h, 0, 0), dot(slot_x, grad_up_h, 0, 0), dot(slot_dy, hidden, 0, 0)]
    summed = lax.psum_scatter(
        jnp.concatenate(terms, axis=1).astype(BF16), "own", scatter_dimension=0, tiled=True
    ).astype(F32)
    return (x_grad, *(summed[None, :, i * width : (i + 1) * width] for i in range(3)))


def solution(mesh):
    n_own, n_rep = mesh.shape["own"], mesh.shape["rep"]

    def shards(tokens, *rest):
        capacity = (3 * tokens.shape[0] + 2 * n_rep - 1) // (2 * n_rep)
        if n_own == 4 and n_rep == 8 and capacity % 8 == 0:
            return shards_by_partner(n_rep, tokens, *rest)
        return shards_whole(tokens, *rest)

    return jax.shard_map(
        shards,
        mesh=mesh,
        in_specs=(
            P(("own", "rep"), None),
            P(("own", "rep"), None),
            P(("own", "rep"), None),
            P(),
            P("rep", "own", None),
            P("rep", "own", None),
            P("rep", "own", None),
        ),
        out_specs=(
            P(("own", "rep"), None),
            P("rep", "own", None),
            P("rep", "own", None),
            P("rep", "own", None),
        ),
        check_vma=False,
    )
```

```python
import functools

import jax
import jax.numpy as jnp
from jax import lax
from jax.experimental import pallas as pl
from jax.experimental.pallas import tpu as pltpu
from jax.sharding import PartitionSpec as P

VMEM = pl.BlockSpec(memory_space=pltpu.VMEM)
SMEM = pl.BlockSpec(memory_space=pltpu.SMEM)
ANY = pl.BlockSpec(memory_space=pl.ANY)
MIB = 1024 * 1024
AHEAD = 1 << 33
BF16 = jnp.bfloat16
F32 = jnp.float32


def dot(left, right, left_dim, right_dim):
    return lax.dot_general(
        left, right, (((left_dim,), (right_dim,)), ((), ())), preferred_element_type=F32
    )


def shape(rows, cols, dtype=BF16):
    return jax.ShapeDtypeStruct((rows, cols), dtype)


def call(kernel, outs, scalars=0, scratch=(), earlier=()):
    earlier = list(earlier)

    def body(*refs):
        inputs = len(refs) - len(outs) - len(scratch)
        kernel(*refs[: inputs - len(earlier)], *refs[inputs:])

    def run(*operands):
        moved = sum(value.size * value.dtype.itemsize for value in (*operands, *outs))
        return pl.pallas_call(
            body,
            out_shape=outs,
            in_specs=[SMEM] * scalars + [VMEM] * (len(operands) - scalars) + [ANY] * len(earlier),
            out_specs=[VMEM] * len(outs),
            scratch_shapes=list(scratch),
            cost_estimate=pl.CostEstimate(flops=0, bytes_accessed=moved, transcendentals=0),
            compiler_params=pltpu.CompilerParams(vmem_limit_bytes=32 * MIB),
        )(*operands, *earlier)

    return run


def after(values, *earlier, ahead=0):
    return pl.pallas_call(
        lambda *refs: None,
        out_shape=[shape(*value.shape, value.dtype) for value in values],
        in_specs=[ANY] * (len(values) + len(earlier)),
        out_specs=[ANY] * len(values),
        input_output_aliases={i: i for i in range(len(values))},
        cost_estimate=pl.CostEstimate(flops=ahead, bytes_accessed=0, transcendentals=0),
        compiler_params=pltpu.CompilerParams(vmem_limit_bytes=MIB),
    )(*values, *earlier)


def picks(capacity, offset, rank_ref, host_ref, route_ref, slots):
    hot = host_ref.shape[0]
    tokens = route_ref.shape[1]
    label = lax.broadcasted_iota(jnp.int32, (hot, tokens), 0)
    base = jnp.zeros((hot, tokens), jnp.int32)
    for e in range(hot):
        apart = host_ref[e] ^ rank_ref[0]
        start = jnp.where((apart & 1) == 0, (apart >> 1) * (2 * capacity), -2 * slots)
        base = jnp.where(label == e, start, base)
    earlier = lax.broadcasted_iota(jnp.int32, (tokens, tokens), 0) < lax.broadcasted_iota(
        jnp.int32, (tokens, tokens), 1
    )
    marked = route_ref[...] == label
    before = dot(jnp.where(marked, 1.0, 0.0).astype(BF16), jnp.where(earlier, 1.0, 0.0).astype(BF16), 1, 0)
    position = jnp.sum(jnp.where(marked, before.astype(jnp.int32) + base, 0), axis=0, keepdims=True) + offset
    slot = lax.broadcasted_iota(jnp.int32, (slots, tokens), 0)
    return jnp.where(slot == position, 1.0, 0.0).astype(BF16)


def pack_kernel(capacity, rank_ref, host_ref, route_a, route_b, x_a, x_b, dy_a, dy_b, pick_ref, *refs):
    *send_refs, rows_ref = refs
    slots = pick_ref.shape[0]
    tokens = route_a.shape[1]
    block = 2 * capacity
    pick_ref[:, :tokens] = picks(capacity, 0, rank_ref, host_ref, route_a, slots)
    pick_ref[:, tokens:] = picks(capacity, capacity, rank_ref, host_ref, route_b, slots)
    rows_ref[:tokens] = x_a[...]
    rows_ref[tokens:] = x_b[...]
    filled = dot(pick_ref[...], rows_ref[...], 1, 0).astype(BF16)
    for k, ref in enumerate(send_refs):
        ref[:block] = filled[k * block : (k + 1) * block]
    near = slice(block, 2 * block)
    send_refs[1][block:] = (
        dot(pick_ref[near, :tokens], dy_a[...], 1, 0) + dot(pick_ref[near, tokens:], dy_b[...], 1, 0)
    ).astype(BF16)


def pack_more_kernel(pick_ref, own_ref, other_ref, *send_refs):
    tokens = own_ref.shape[0]
    block = send_refs[0].shape[0]
    filled = (
        dot(pick_ref[:, :tokens], own_ref[...], 1, 0) + dot(pick_ref[:, tokens:], other_ref[...], 1, 0)
    ).astype(BF16)
    for k, ref in zip((0, 2, 3), send_refs):
        ref[...] = filled[k * block : (k + 1) * block]


def weight_parts(own_ref, weights):
    depth = weights[0].shape[0]
    half = depth // 2
    for k, ref in enumerate(weights):
        partner, start = (k, 0) if k < 3 else (3, (k - 3) * half)
        yield pl.ds(pl.multiple_of((own_ref[0] ^ partner) * depth + start, half), ref.shape[0]), ref


def columns_of(own_ref, depth):
    return [pl.ds(pl.multiple_of((own_ref[0] ^ k) * depth, depth), depth) for k in range(4)]


def spread_kernel(own_ref, *refs):
    got, own_dy, (x_ref, *piece_refs) = refs[:4], refs[4], refs[5:]
    slots = x_ref.shape[0]
    block = slots // 4
    columns = columns_of(own_ref, piece_refs[0].shape[1])
    for j, ref in enumerate(got):
        rows = slice(j * block, (j + 1) * block)
        x_ref[rows] = ref[:block]
        for cols, piece_ref in zip(columns, piece_refs):
            piece_ref[rows] = ref[:block, cols]
    for cols, piece_ref in zip(columns, piece_refs):
        piece_ref[slots : slots + block] = own_dy[:, cols]
        piece_ref[slots + block :] = got[1][block:, cols]


def act_kernel(own_ref, x_ref, *refs):
    weights, acts_ref = refs[:-1], refs[-1]
    both = acts_ref.shape[1]
    acts_ref[...] = sum(dot(x_ref[:, cols], ref[:, :both], 1, 0) for cols, ref in weight_parts(own_ref, weights))


def grad_kernel(parts, own_ref, acts_ref, *refs):
    got, weights, outs, dy_ref = refs[:parts], refs[parts : parts + 5], refs[parts + 5 : -1], refs[-1]
    back_refs, messages = outs[:parts], outs[parts:]
    slots, both = acts_ref.shape
    width = both // 2
    half = slots // 2
    block = slots // parts
    depth = weights[0].shape[0]
    for j, ref in enumerate(got):
        dy_ref[j * block : (j + 1) * block] = ref[ref.shape[0] - block :]
    back_grad = sum(dot(dy_ref[:, cols], ref[:, both:], 1, 0) for cols, ref in weight_parts(own_ref, weights))
    gate_act, up_act = acts_ref[:, :width], acts_ref[:, width:]
    sigmoid_g = jax.nn.sigmoid(gate_act)
    silu_gate = gate_act * sigmoid_g
    hidden = (silu_gate * up_act).astype(BF16)
    gate_h = (back_grad * up_act * sigmoid_g * (1.0 + gate_act * (1.0 - sigmoid_g))).astype(BF16)
    up_h = (back_grad * silu_gate).astype(BF16)
    for message, cols in zip(messages, columns_of(own_ref, depth)):
        message[:slots, :width] = gate_h
        message[:slots, width:] = up_h
        message[slots : slots + half, :width] = hidden[:half]
        message[slots : slots + half, width:] = hidden[half:]
        message[slots + half :] = dy_ref[half:, cols]
    grads = messages[0][:slots]
    for cols, ref in weight_parts(own_ref, weights):
        slot_grad = dot(grads, ref[:, :both], 1, 1).astype(BF16)
        for j, back_ref in enumerate(back_refs):
            back_ref[:, cols] = slot_grad[j * block : (j + 1) * block]


def sum_kernel(*refs):
    pieces, messages = refs[:4], refs[4:8]
    (gate_ref, up_ref, down_ref), (x_ref, dy_ref, grads_ref, hidden_ref) = refs[8:11], refs[11:]
    width = gate_ref.shape[1]
    slots = x_ref.shape[0] // 4
    half = slots // 2
    for k, (piece, got) in enumerate(zip(pieces, messages)):
        start, middle, stop = k * slots, k * slots + half, (k + 1) * slots
        x_ref[start:stop] = piece[:slots]
        dy_ref[start:middle] = piece[slots:]
        dy_ref[middle:stop] = got[slots + half :]
        grads_ref[start:stop] = got[:slots]
        hidden_ref[start:middle] = got[slots : slots + half, :width]
        hidden_ref[middle:stop] = got[slots : slots + half, width:]
    total = dot(x_ref[...], grads_ref[...], 0, 0)
    gate_ref[...] = total[:, :width]
    up_ref[...] = total[:, width:]
    down_ref[...] = dot(dy_ref[...], hidden_ref[...], 0, 0)


def unpack_kernel(pick_ref, *refs):
    returned, (mine_ref, other_ref, rows_ref) = refs[:-3], refs[-3:]
    tokens = mine_ref.shape[0]
    block = returned[0].shape[0]
    for k, ref in enumerate(returned):
        rows_ref[k * block : (k + 1) * block] = ref[...]
    both = dot(pick_ref[...], rows_ref[...], 0, 0).astype(BF16)
    mine_ref[...] = both[:tokens]
    other_ref[...] = both[tokens:]


def shards_by_partner(n_rep, tokens, cotangent, route, host, w_gate, w_up, w_down_t):
    tok_rows, model_width = tokens.shape
    hot = host.shape[0]
    _, depth, width = w_gate.shape
    capacity = (3 * tok_rows + 2 * hot - 1) // (2 * hot)
    slots = hot * capacity
    parts = n_rep // 2
    block = 2 * capacity
    own = lax.axis_index("own").astype(jnp.int32).reshape(1)
    rank = lax.axis_index("rep").astype(jnp.int32).reshape(1)

    def over_own(value, k):
        return lax.ppermute(value, "own", [(i, i ^ k) for i in range(4)])

    def over_rep(value, k):
        return lax.ppermute(value, "rep", [(i, i ^ k) for i in range(n_rep)])

    route = route.reshape(1, tok_rows)
    route_b, tokens_b, cotangent_b = over_rep(route, 1), over_rep(tokens, 1), over_rep(cotangent, 1)
    joined = jnp.concatenate([w_gate[0], w_up[0], w_down_t[0]], axis=1)
    joined_1, joined_2 = over_own(joined, 1), over_own(joined, 2)
    slot_rows = pltpu.VMEM((slots, model_width), BF16)
    pick, own_x, near, far_xa, far_xb = call(
        functools.partial(pack_kernel, capacity),
        [shape(slots, 2 * tok_rows), shape(block, model_width), shape(2 * block, model_width)]
        + [shape(block, model_width)] * 2,
        2,
        [pltpu.VMEM((2 * tok_rows, model_width), BF16)],
    )(rank, host, route, route_b, tokens, tokens_b, cotangent, cotangent_b)
    far_x = [over_rep(far_xa, 4), over_rep(far_xb, 6)]
    near, *far_x = after([over_rep(near, 2), *far_x], ahead=1<<31)
    own_dy, far_a, far_b = call(pack_more_kernel, [shape(block, model_width)] * 3)(pick, cotangent, cotangent_b)
    joined_3 = [over_own(joined_1[: depth // 2], 2), over_own(joined_2[depth // 2 :], 1)]
    joined_3 = after(joined_3, ahead=1<<33)
    weights = [joined, joined_1, joined_2, *joined_3]

    x, *pieces = call(spread_kernel, [shape(slots, model_width)] + [shape(slots + slots // 2, depth)] * 4, 1)(
        own, own_x, near, *far_x, own_dy
    )
    far_dy = after([far_a, far_b], pieces[0])
    far_dy = [over_rep(far_dy[0], 4), over_rep(far_dy[1], 6)]
    pieces = [pieces[0]] + [over_own(pieces[k], k) for k in range(1, 4)]
    acts = call(act_kernel, [shape(slots, 2 * width, F32)], 1)(own, x, *weights)[0]

    *back, own_message, message_1, message_2, message_3 = call(
        functools.partial(grad_kernel, parts),
        [shape(block, model_width)] * parts + [shape(2 * slots, 2 * width)] * 4,
        1,
        [slot_rows],
        earlier=pieces[1:],
    )(own, acts, own_dy, near, *far_dy, *weights)
    far_back = after([over_rep(back[2], 4), over_rep(back[3], 6)], ahead=AHEAD)
    returned = [back[0], over_rep(back[1], 2), *far_back]
    message_3 = after([message_3], returned[1])[0]
    messages = after([over_own(message_1, 1), over_own(message_2, 2), over_own(message_3, 3)], ahead=AHEAD)
    messages = [own_message, *messages]

    mine, other = call(unpack_kernel, [shape(tok_rows, model_width)] * 2, 0, [slot_rows])(
        pick, *returned
    )
    x_grad = mine + over_rep(other, 1)
    out = call(
        sum_kernel,
        [shape(depth, width, F32)] * 3,
        0,
        [pltpu.VMEM((4 * slots, cols), BF16) for cols in (depth, depth, 2 * width, width)],
    )(*pieces, *messages)
    return (x_grad, *(grad[None] for grad in out))


def shards_whole(tokens, cotangent, route, host, w_gate, w_up, w_down_t):
    tok_rows, model_width = tokens.shape
    hot = host.shape[0]
    width = w_gate.shape[2]
    capacity = max(2, (3 * tok_rows + 2 * hot - 1) // (2 * hot))
    slots = hot * capacity
    labels = lax.broadcasted_iota(jnp.int32, (tok_rows, hot), 1)
    target = jnp.sum(jnp.where(route == labels, host[None, :], 0), axis=1)
    marked = (target[:, None] == labels).astype(jnp.int32)
    arrival = jnp.sum(jnp.cumsum(marked, axis=0) * marked, axis=1) - 1
    position = target * capacity + arrival
    pick = (lax.broadcasted_iota(jnp.int32, (slots, tok_rows), 0) == position[None, :]).astype(BF16)

    def exchange(value):
        split = value.astype(BF16).reshape(hot, capacity, model_width)
        return lax.all_to_all(split, "rep", split_axis=0, concat_axis=0, tiled=True).reshape(slots, model_width)

    slot_x, slot_dy = exchange(dot(pick, tokens, 1, 0)), exchange(dot(pick, cotangent, 1, 0))
    gate, up, down = (lax.all_gather(w[0], "own", axis=0, tiled=True) for w in (w_gate, w_up, w_down_t))
    gate_act, up_act, back_grad = dot(slot_x, gate, 1, 0), dot(slot_x, up, 1, 0), dot(slot_dy, down, 1, 0)
    sigmoid_g = jax.nn.sigmoid(gate_act)
    silu_gate = gate_act * sigmoid_g
    hidden = (silu_gate * up_act).astype(BF16)
    grad_gate_h = (back_grad * up_act * sigmoid_g * (1.0 + gate_act * (1.0 - sigmoid_g))).astype(BF16)
    grad_up_h = (back_grad * silu_gate).astype(BF16)
    returned = exchange(dot(grad_gate_h, gate, 1, 1) + dot(grad_up_h, up, 1, 1))
    x_grad = dot(pick, returned, 0, 0).astype(BF16)
    terms = [dot(slot_x, grad_gate_h, 0, 0), dot(slot_x, grad_up_h, 0, 0), dot(slot_dy, hidden, 0, 0)]
    summed = lax.psum_scatter(
        jnp.concatenate(terms, axis=1).astype(BF16), "own", scatter_dimension=0, tiled=True
    ).astype(F32)
    return (x_grad, *(summed[None, :, i * width : (i + 1) * width] for i in range(3)))


def solution(mesh):
    n_own, n_rep = mesh.shape["own"], mesh.shape["rep"]

    def shards(tokens, *rest):
        capacity = (3 * tokens.shape[0] + 2 * n_rep - 1) // (2 * n_rep)
        if n_own == 4 and n_rep == 8 and capacity % 8 == 0:
            return shards_by_partner(n_rep, tokens, *rest)
        return shards_whole(tokens, *rest)

    return jax.shard_map(
        shards,
        mesh=mesh,
        in_specs=(
            P(("own", "rep"), None),
            P(("own", "rep"), None),
            P(("own", "rep"), None),
            P(),
            P("rep", "own", None),
            P("rep", "own", None),
            P("rep", "own", None),
        ),
        out_specs=(
            P(("own", "rep"), None),
            P("rep", "own", None),
            P("rep", "own", None),
            P("rep", "own", None),
        ),
        check_vma=False,
    )
```

```python
import functools

import jax
import jax.numpy as jnp
from jax import lax
from jax.experimental import pallas as pl
from jax.experimental.pallas import tpu as pltpu
from jax.sharding import PartitionSpec as P

VMEM = pl.BlockSpec(memory_space=pltpu.VMEM)
SMEM = pl.BlockSpec(memory_space=pltpu.SMEM)
ANY = pl.BlockSpec(memory_space=pl.ANY)
MIB = 1024 * 1024
AHEAD = 1 << 33
BF16 = jnp.bfloat16
F32 = jnp.float32


def dot(left, right, left_dim, right_dim):
    return lax.dot_general(
        left, right, (((left_dim,), (right_dim,)), ((), ())), preferred_element_type=F32
    )


def shape(rows, cols, dtype=BF16):
    return jax.ShapeDtypeStruct((rows, cols), dtype)


def call(kernel, outs, scalars=0, scratch=(), earlier=()):
    earlier = list(earlier)

    def body(*refs):
        inputs = len(refs) - len(outs) - len(scratch)
        kernel(*refs[: inputs - len(earlier)], *refs[inputs:])

    def run(*operands):
        moved = sum(value.size * value.dtype.itemsize for value in (*operands, *outs))
        return pl.pallas_call(
            body,
            out_shape=outs,
            in_specs=[SMEM] * scalars + [VMEM] * (len(operands) - scalars) + [ANY] * len(earlier),
            out_specs=[VMEM] * len(outs),
            scratch_shapes=list(scratch),
            cost_estimate=pl.CostEstimate(flops=0, bytes_accessed=moved, transcendentals=0),
            compiler_params=pltpu.CompilerParams(vmem_limit_bytes=32 * MIB),
        )(*operands, *earlier)

    return run


def after(values, *earlier, ahead=0):
    return pl.pallas_call(
        lambda *refs: None,
        out_shape=[shape(*value.shape, value.dtype) for value in values],
        in_specs=[ANY] * (len(values) + len(earlier)),
        out_specs=[ANY] * len(values),
        input_output_aliases={i: i for i in range(len(values))},
        cost_estimate=pl.CostEstimate(flops=ahead, bytes_accessed=0, transcendentals=0),
        compiler_params=pltpu.CompilerParams(vmem_limit_bytes=MIB),
    )(*values, *earlier)


def picks(capacity, offset, rank_ref, host_ref, route_ref, slots):
    hot = host_ref.shape[0]
    tokens = route_ref.shape[1]
    label = lax.broadcasted_iota(jnp.int32, (hot, tokens), 0)
    base = jnp.zeros((hot, tokens), jnp.int32)
    for e in range(hot):
        apart = host_ref[e] ^ rank_ref[0]
        start = jnp.where((apart & 1) == 0, (apart >> 1) * (2 * capacity), -2 * slots)
        base = jnp.where(label == e, start, base)
    earlier = lax.broadcasted_iota(jnp.int32, (tokens, tokens), 0) < lax.broadcasted_iota(
        jnp.int32, (tokens, tokens), 1
    )
    marked = route_ref[...] == label
    before = dot(jnp.where(marked, 1.0, 0.0).astype(BF16), jnp.where(earlier, 1.0, 0.0).astype(BF16), 1, 0)
    position = jnp.sum(jnp.where(marked, before.astype(jnp.int32) + base, 0), axis=0, keepdims=True) + offset
    slot = lax.broadcasted_iota(jnp.int32, (slots, tokens), 0)
    return jnp.where(slot == position, 1.0, 0.0).astype(BF16)


def pack_kernel(capacity, rank_ref, host_ref, route_a, route_b, x_a, x_b, dy_a, dy_b, pick_ref, *refs):
    *send_refs, rows_ref = refs
    slots = pick_ref.shape[0]
    tokens = route_a.shape[1]
    block = 2 * capacity
    pick_ref[:, :tokens] = picks(capacity, 0, rank_ref, host_ref, route_a, slots)
    pick_ref[:, tokens:] = picks(capacity, capacity, rank_ref, host_ref, route_b, slots)
    rows_ref[:tokens] = x_a[...]
    rows_ref[tokens:] = x_b[...]
    filled = dot(pick_ref[...], rows_ref[...], 1, 0).astype(BF16)
    for k, ref in enumerate(send_refs):
        ref[:block] = filled[k * block : (k + 1) * block]
    near = slice(block, 2 * block)
    send_refs[1][block:] = (
        dot(pick_ref[near, :tokens], dy_a[...], 1, 0) + dot(pick_ref[near, tokens:], dy_b[...], 1, 0)
    ).astype(BF16)


def pack_more_kernel(pick_ref, own_ref, other_ref, *send_refs):
    tokens = own_ref.shape[0]
    block = send_refs[0].shape[0]
    filled = (
        dot(pick_ref[:, :tokens], own_ref[...], 1, 0) + dot(pick_ref[:, tokens:], other_ref[...], 1, 0)
    ).astype(BF16)
    for k, ref in zip((0, 2, 3), send_refs):
        ref[...] = filled[k * block : (k + 1) * block]


def weight_parts(own_ref, weights):
    depth = weights[0].shape[0]
    half = depth // 2
    for k, ref in enumerate(weights):
        partner, start = (k, 0) if k < 3 else (3, (k - 3) * half)
        yield pl.ds(pl.multiple_of((own_ref[0] ^ partner) * depth + start, half), ref.shape[0]), ref


def columns_of(own_ref, depth):
    return [pl.ds(pl.multiple_of((own_ref[0] ^ k) * depth, depth), depth) for k in range(4)]


def spread_kernel(own_ref, *refs):
    got, own_dy, (x_ref, *piece_refs) = refs[:4], refs[4], refs[5:]
    slots = x_ref.shape[0]
    block = slots // 4
    columns = columns_of(own_ref, piece_refs[0].shape[1])
    for j, ref in enumerate(got):
        rows = slice(j * block, (j + 1) * block)
        x_ref[rows] = ref[:block]
        for cols, piece_ref in zip(columns, piece_refs):
            piece_ref[rows] = ref[:block, cols]
    for cols, piece_ref in zip(columns, piece_refs):
        piece_ref[slots : slots + block] = own_dy[:, cols]
        piece_ref[slots + block :] = got[1][block:, cols]


def act_kernel(own_ref, x_ref, *refs):
    weights, acts_ref = refs[:-1], refs[-1]
    both = acts_ref.shape[1]
    acts_ref[...] = sum(dot(x_ref[:, cols], ref[:, :both], 1, 0) for cols, ref in weight_parts(own_ref, weights))


def grad_kernel(parts, own_ref, acts_ref, *refs):
    got, weights, outs, dy_ref = refs[:parts], refs[parts : parts + 5], refs[parts + 5 : -1], refs[-1]
    back_refs, messages = outs[:parts], outs[parts:]
    slots, both = acts_ref.shape
    width = both // 2
    half = slots // 2
    block = slots // parts
    depth = weights[0].shape[0]
    for j, ref in enumerate(got):
        dy_ref[j * block : (j + 1) * block] = ref[ref.shape[0] - block :]
    back_grad = sum(dot(dy_ref[:, cols], ref[:, both:], 1, 0) for cols, ref in weight_parts(own_ref, weights))
    gate_act, up_act = acts_ref[:, :width], acts_ref[:, width:]
    sigmoid_g = jax.nn.sigmoid(gate_act)
    silu_gate = gate_act * sigmoid_g
    hidden = (silu_gate * up_act).astype(BF16)
    gate_h = (back_grad * up_act * sigmoid_g * (1.0 + gate_act * (1.0 - sigmoid_g))).astype(BF16)
    up_h = (back_grad * silu_gate).astype(BF16)
    for message, cols in zip(messages, columns_of(own_ref, depth)):
        message[:slots, :width] = gate_h
        message[:slots, width:] = up_h
        message[slots : slots + half, :width] = hidden[:half]
        message[slots : slots + half, width:] = hidden[half:]
        message[slots + half :] = dy_ref[half:, cols]
    grads = messages[0][:slots]
    for cols, ref in weight_parts(own_ref, weights):
        slot_grad = dot(grads, ref[:, :both], 1, 1).astype(BF16)
        for j, back_ref in enumerate(back_refs):
            back_ref[:, cols] = slot_grad[j * block : (j + 1) * block]


def sum_kernel(*refs):
    pieces, messages = refs[:4], refs[4:8]
    (gate_ref, up_ref, down_ref), (x_ref, dy_ref, grads_ref, hidden_ref) = refs[8:11], refs[11:]
    width = gate_ref.shape[1]
    slots = x_ref.shape[0] // 4
    half = slots // 2
    for k, (piece, got) in enumerate(zip(pieces, messages)):
        start, middle, stop = k * slots, k * slots + half, (k + 1) * slots
        x_ref[start:stop] = piece[:slots]
        dy_ref[start:middle] = piece[slots:]
        dy_ref[middle:stop] = got[slots + half :]
        grads_ref[start:stop] = got[:slots]
        hidden_ref[start:middle] = got[slots : slots + half, :width]
        hidden_ref[middle:stop] = got[slots : slots + half, width:]
    total = dot(x_ref[...], grads_ref[...], 0, 0)
    gate_ref[...] = total[:, :width]
    up_ref[...] = total[:, width:]
    down_ref[...] = dot(dy_ref[...], hidden_ref[...], 0, 0)


def unpack_kernel(pick_ref, *refs):
    returned, (mine_ref, other_ref, rows_ref) = refs[:-3], refs[-3:]
    tokens = mine_ref.shape[0]
    block = returned[0].shape[0]
    for k, ref in enumerate(returned):
        rows_ref[k * block : (k + 1) * block] = ref[...]
    both = dot(pick_ref[...], rows_ref[...], 0, 0).astype(BF16)
    mine_ref[...] = both[:tokens]
    other_ref[...] = both[tokens:]


def shards_by_partner(n_rep, tokens, cotangent, route, host, w_gate, w_up, w_down_t):
    tok_rows, model_width = tokens.shape
    hot = host.shape[0]
    _, depth, width = w_gate.shape
    capacity = (3 * tok_rows + 2 * hot - 1) // (2 * hot)
    slots = hot * capacity
    parts = n_rep // 2
    block = 2 * capacity
    own = lax.axis_index("own").astype(jnp.int32).reshape(1)
    rank = lax.axis_index("rep").astype(jnp.int32).reshape(1)

    def over_own(value, k):
        return lax.ppermute(value, "own", [(i, i ^ k) for i in range(4)])

    def over_rep(value, k):
        return lax.ppermute(value, "rep", [(i, i ^ k) for i in range(n_rep)])

    route = route.reshape(1, tok_rows)
    route_b, tokens_b, cotangent_b = over_rep(route, 1), over_rep(tokens, 1), over_rep(cotangent, 1)
    joined = jnp.concatenate([w_gate[0], w_up[0], w_down_t[0]], axis=1)
    joined_1, joined_2 = over_own(joined, 1), over_own(joined, 2)
    slot_rows = pltpu.VMEM((slots, model_width), BF16)
    pick, own_x, near, far_xa, far_xb = call(
        functools.partial(pack_kernel, capacity),
        [shape(slots, 2 * tok_rows), shape(block, model_width), shape(2 * block, model_width)]
        + [shape(block, model_width)] * 2,
        2,
        [pltpu.VMEM((2 * tok_rows, model_width), BF16)],
    )(rank, host, route, route_b, tokens, tokens_b, cotangent, cotangent_b)
    far_x = [over_rep(far_xa, 4), over_rep(far_xb, 6)]
    near, *far_x = after([over_rep(near, 2), *far_x], ahead=1<<31)
    own_dy, far_a, far_b = call(pack_more_kernel, [shape(block, model_width)] * 3)(pick, cotangent, cotangent_b)
    joined_3 = [over_own(joined_1[: depth // 2], 2), over_own(joined_2[depth // 2 :], 1)]
    joined_3 = after(joined_3, ahead=1<<33)
    weights = [joined, joined_1, joined_2, *joined_3]

    x, *pieces = call(spread_kernel, [shape(slots, model_width)] + [shape(slots + slots // 2, depth)] * 4, 1)(
        own, own_x, near, *far_x, own_dy
    )
    far_dy = after([far_a, far_b], pieces[0])
    far_dy = [over_rep(far_dy[0], 4), over_rep(far_dy[1], 6)]
    pieces = [pieces[0]] + [over_own(pieces[k], k) for k in range(1, 4)]
    acts = call(act_kernel, [shape(slots, 2 * width, F32)], 1)(own, x, *weights)[0]

    *back, own_message, message_1, message_2, message_3 = call(
        functools.partial(grad_kernel, parts),
        [shape(block, model_width)] * parts + [shape(2 * slots, 2 * width)] * 4,
        1,
        [slot_rows],
    )(own, acts, own_dy, near, *far_dy, *weights)
    far_back = after([over_rep(back[2], 4), over_rep(back[3], 6)], ahead=AHEAD)
    returned = [back[0], over_rep(back[1], 2), *far_back]
    message_1, message_2 = after([message_1, message_2], *pieces[1:])
    message_3 = after([message_3], returned[1])[0]
    messages = after([over_own(message_1, 1), over_own(message_2, 2), over_own(message_3, 3)], ahead=AHEAD)
    messages = [own_message, *messages]

    mine, other = call(unpack_kernel, [shape(tok_rows, model_width)] * 2, 0, [slot_rows])(
        pick, *returned
    )
    x_grad = mine + over_rep(other, 1)
    out = call(
        sum_kernel,
        [shape(depth, width, F32)] * 3,
        0,
        [pltpu.VMEM((4 * slots, cols), BF16) for cols in (depth, depth, 2 * width, width)],
    )(*pieces, *messages)
    return (x_grad, *(grad[None] for grad in out))


def shards_whole(tokens, cotangent, route, host, w_gate, w_up, w_down_t):
    tok_rows, model_width = tokens.shape
    hot = host.shape[0]
    width = w_gate.shape[2]
    capacity = max(2, (3 * tok_rows + 2 * hot - 1) // (2 * hot))
    slots = hot * capacity
    labels = lax.broadcasted_iota(jnp.int32, (tok_rows, hot), 1)
    target = jnp.sum(jnp.where(route == labels, host[None, :], 0), axis=1)
    marked = (target[:, None] == labels).astype(jnp.int32)
    arrival = jnp.sum(jnp.cumsum(marked, axis=0) * marked, axis=1) - 1
    position = target * capacity + arrival
    pick = (lax.broadcasted_iota(jnp.int32, (slots, tok_rows), 0) == position[None, :]).astype(BF16)

    def exchange(value):
        split = value.astype(BF16).reshape(hot, capacity, model_width)
        return lax.all_to_all(split, "rep", split_axis=0, concat_axis=0, tiled=True).reshape(slots, model_width)

    slot_x, slot_dy = exchange(dot(pick, tokens, 1, 0)), exchange(dot(pick, cotangent, 1, 0))
    gate, up, down = (lax.all_gather(w[0], "own", axis=0, tiled=True) for w in (w_gate, w_up, w_down_t))
    gate_act, up_act, back_grad = dot(slot_x, gate, 1, 0), dot(slot_x, up, 1, 0), dot(slot_dy, down, 1, 0)
    sigmoid_g = jax.nn.sigmoid(gate_act)
    silu_gate = gate_act * sigmoid_g
    hidden = (silu_gate * up_act).astype(BF16)
    grad_gate_h = (back_grad * up_act * sigmoid_g * (1.0 + gate_act * (1.0 - sigmoid_g))).astype(BF16)
    grad_up_h = (back_grad * silu_gate).astype(BF16)
    returned = exchange(dot(grad_gate_h, gate, 1, 1) + dot(grad_up_h, up, 1, 1))
    x_grad = dot(pick, returned, 0, 0).astype(BF16)
    terms = [dot(slot_x, grad_gate_h, 0, 0), dot(slot_x, grad_up_h, 0, 0), dot(slot_dy, hidden, 0, 0)]
    summed = lax.psum_scatter(
        jnp.concatenate(terms, axis=1).astype(BF16), "own", scatter_dimension=0, tiled=True
    ).astype(F32)
    return (x_grad, *(summed[None, :, i * width : (i + 1) * width] for i in range(3)))


def solution(mesh):
    n_own, n_rep = mesh.shape["own"], mesh.shape["rep"]

    def shards(tokens, *rest):
        capacity = (3 * tokens.shape[0] + 2 * n_rep - 1) // (2 * n_rep)
        if n_own == 4 and n_rep == 8 and capacity % 8 == 0:
            return shards_by_partner(n_rep, tokens, *rest)
        return shards_whole(tokens, *rest)

    return jax.shard_map(
        shards,
        mesh=mesh,
        in_specs=(
            P(("own", "rep"), None),
            P(("own", "rep"), None),
            P(("own", "rep"), None),
            P(),
            P("rep", "own", None),
            P("rep", "own", None),
            P("rep", "own", None),
        ),
        out_specs=(
            P(("own", "rep"), None),
            P("rep", "own", None),
            P("rep", "own", None),
            P("rep", "own", None),
        ),
        check_vma=False,
    )
```

```python
import functools

import jax
import jax.numpy as jnp
from jax import lax
from jax.experimental import pallas as pl
from jax.experimental.pallas import tpu as pltpu
from jax.sharding import PartitionSpec as P

VMEM = pl.BlockSpec(memory_space=pltpu.VMEM)
SMEM = pl.BlockSpec(memory_space=pltpu.SMEM)
ANY = pl.BlockSpec(memory_space=pl.ANY)
MIB = 1024 * 1024
AHEAD = 1 << 33
BF16 = jnp.bfloat16
F32 = jnp.float32


def dot(left, right, left_dim, right_dim):
    return lax.dot_general(
        left, right, (((left_dim,), (right_dim,)), ((), ())), preferred_element_type=F32
    )


def shape(rows, cols, dtype=BF16):
    return jax.ShapeDtypeStruct((rows, cols), dtype)


def call(kernel, outs, scalars=0, scratch=(), earlier=()):
    earlier = list(earlier)

    def body(*refs):
        inputs = len(refs) - len(outs) - len(scratch)
        kernel(*refs[: inputs - len(earlier)], *refs[inputs:])

    def run(*operands):
        moved = sum(value.size * value.dtype.itemsize for value in (*operands, *outs))
        return pl.pallas_call(
            body,
            out_shape=outs,
            in_specs=[SMEM] * scalars + [VMEM] * (len(operands) - scalars) + [ANY] * len(earlier),
            out_specs=[VMEM] * len(outs),
            scratch_shapes=list(scratch),
            cost_estimate=pl.CostEstimate(flops=0, bytes_accessed=moved, transcendentals=0),
            compiler_params=pltpu.CompilerParams(vmem_limit_bytes=32 * MIB),
        )(*operands, *earlier)

    return run


def after(values, *earlier, ahead=0):
    return pl.pallas_call(
        lambda *refs: None,
        out_shape=[shape(*value.shape, value.dtype) for value in values],
        in_specs=[ANY] * (len(values) + len(earlier)),
        out_specs=[ANY] * len(values),
        input_output_aliases={i: i for i in range(len(values))},
        cost_estimate=pl.CostEstimate(flops=ahead, bytes_accessed=0, transcendentals=0),
        compiler_params=pltpu.CompilerParams(vmem_limit_bytes=MIB),
    )(*values, *earlier)


def picks(capacity, offset, rank_ref, host_ref, route_ref, slots):
    hot = host_ref.shape[0]
    tokens = route_ref.shape[1]
    label = lax.broadcasted_iota(jnp.int32, (hot, tokens), 0)
    base = jnp.zeros((hot, tokens), jnp.int32)
    for e in range(hot):
        apart = host_ref[e] ^ rank_ref[0]
        start = jnp.where((apart & 1) == 0, (apart >> 1) * (2 * capacity), -2 * slots)
        base = jnp.where(label == e, start, base)
    earlier = lax.broadcasted_iota(jnp.int32, (tokens, tokens), 0) < lax.broadcasted_iota(
        jnp.int32, (tokens, tokens), 1
    )
    marked = route_ref[...] == label
    before = dot(jnp.where(marked, 1.0, 0.0).astype(BF16), jnp.where(earlier, 1.0, 0.0).astype(BF16), 1, 0)
    position = jnp.sum(jnp.where(marked, before.astype(jnp.int32) + base, 0), axis=0, keepdims=True) + offset
    slot = lax.broadcasted_iota(jnp.int32, (slots, tokens), 0)
    return jnp.where(slot == position, 1.0, 0.0).astype(BF16)


def pack_kernel(capacity, rank_ref, host_ref, route_a, route_b, x_a, x_b, dy_a, dy_b, pick_ref, *refs):
    *send_refs, rows_ref = refs
    slots = pick_ref.shape[0]
    tokens = route_a.shape[1]
    block = 2 * capacity
    pick_ref[:, :tokens] = picks(capacity, 0, rank_ref, host_ref, route_a, slots)
    pick_ref[:, tokens:] = picks(capacity, capacity, rank_ref, host_ref, route_b, slots)
    rows_ref[:tokens] = x_a[...]
    rows_ref[tokens:] = x_b[...]
    filled = dot(pick_ref[...], rows_ref[...], 1, 0).astype(BF16)
    for k, ref in enumerate(send_refs):
        ref[:block] = filled[k * block : (k + 1) * block]
    near = slice(block, 2 * block)
    send_refs[1][block:] = (
        dot(pick_ref[near, :tokens], dy_a[...], 1, 0) + dot(pick_ref[near, tokens:], dy_b[...], 1, 0)
    ).astype(BF16)


def pack_more_kernel(pick_ref, own_ref, other_ref, *send_refs):
    tokens = own_ref.shape[0]
    block = send_refs[0].shape[0]
    filled = (
        dot(pick_ref[:, :tokens], own_ref[...], 1, 0) + dot(pick_ref[:, tokens:], other_ref[...], 1, 0)
    ).astype(BF16)
    for k, ref in zip((0, 2, 3), send_refs):
        ref[...] = filled[k * block : (k + 1) * block]


def weight_parts(own_ref, weights):
    depth = weights[0].shape[0]
    half = depth // 2
    for k, ref in enumerate(weights):
        partner, start = (k, 0) if k < 3 else (3, (k - 3) * half)
        yield pl.ds(pl.multiple_of((own_ref[0] ^ partner) * depth + start, half), ref.shape[0]), ref


def columns_of(own_ref, depth):
    return [pl.ds(pl.multiple_of((own_ref[0] ^ k) * depth, depth), depth) for k in range(4)]


def spread_kernel(own_ref, *refs):
    got, own_dy, (x_ref, *piece_refs) = refs[:4], refs[4], refs[5:]
    slots = x_ref.shape[0]
    block = slots // 4
    columns = columns_of(own_ref, piece_refs[0].shape[1])
    for j, ref in enumerate(got):
        rows = slice(j * block, (j + 1) * block)
        x_ref[rows] = ref[:block]
        for cols, piece_ref in zip(columns, piece_refs):
            piece_ref[rows] = ref[:block, cols]
    for cols, piece_ref in zip(columns, piece_refs):
        piece_ref[slots : slots + block] = own_dy[:, cols]
        piece_ref[slots + block :] = got[1][block:, cols]


def act_kernel(own_ref, x_ref, *refs):
    weights, acts_ref = refs[:-1], refs[-1]
    both = acts_ref.shape[1]
    acts_ref[...] = sum(dot(x_ref[:, cols], ref[:, :both], 1, 0) for cols, ref in weight_parts(own_ref, weights))


def grad_kernel(parts, own_ref, acts_ref, *refs):
    got, weights, outs, dy_ref = refs[:parts], refs[parts : parts + 5], refs[parts + 5 : -1], refs[-1]
    back_refs, messages = outs[:parts], outs[parts:]
    slots, both = acts_ref.shape
    width = both // 2
    half = slots // 2
    block = slots // parts
    depth = weights[0].shape[0]
    for j, ref in enumerate(got):
        dy_ref[j * block : (j + 1) * block] = ref[ref.shape[0] - block :]
    back_grad = sum(dot(dy_ref[:, cols], ref[:, both:], 1, 0) for cols, ref in weight_parts(own_ref, weights))
    gate_act, up_act = acts_ref[:, :width], acts_ref[:, width:]
    sigmoid_g = jax.nn.sigmoid(gate_act)
    silu_gate = gate_act * sigmoid_g
    hidden = (silu_gate * up_act).astype(BF16)
    gate_h = (back_grad * up_act * sigmoid_g * (1.0 + gate_act * (1.0 - sigmoid_g))).astype(BF16)
    up_h = (back_grad * silu_gate).astype(BF16)
    for message, cols in zip(messages, columns_of(own_ref, depth)):
        message[:slots, :width] = gate_h
        message[:slots, width:] = up_h
        message[slots : slots + half, :width] = hidden[:half]
        message[slots : slots + half, width:] = hidden[half:]
        message[slots + half :] = dy_ref[half:, cols]
    grads = messages[0][:slots]
    for cols, ref in weight_parts(own_ref, weights):
        slot_grad = dot(grads, ref[:, :both], 1, 1).astype(BF16)
        for j, back_ref in enumerate(back_refs):
            back_ref[:, cols] = slot_grad[j * block : (j + 1) * block]


def sum_kernel(*refs):
    pieces, messages = refs[:4], refs[4:8]
    (gate_ref, up_ref, down_ref), (x_ref, dy_ref, grads_ref, hidden_ref) = refs[8:11], refs[11:]
    width = gate_ref.shape[1]
    slots = x_ref.shape[0] // 4
    half = slots // 2
    for k, (piece, got) in enumerate(zip(pieces, messages)):
        start, middle, stop = k * slots, k * slots + half, (k + 1) * slots
        x_ref[start:stop] = piece[:slots]
        dy_ref[start:middle] = piece[slots:]
        dy_ref[middle:stop] = got[slots + half :]
        grads_ref[start:stop] = got[:slots]
        hidden_ref[start:middle] = got[slots : slots + half, :width]
        hidden_ref[middle:stop] = got[slots : slots + half, width:]
    total = dot(x_ref[...], grads_ref[...], 0, 0)
    gate_ref[...] = total[:, :width]
    up_ref[...] = total[:, width:]
    down_ref[...] = dot(dy_ref[...], hidden_ref[...], 0, 0)


def unpack_kernel(pick_ref, *refs):
    returned, (mine_ref, other_ref, rows_ref) = refs[:-3], refs[-3:]
    tokens = mine_ref.shape[0]
    block = returned[0].shape[0]
    for k, ref in enumerate(returned):
        rows_ref[k * block : (k + 1) * block] = ref[...]
    both = dot(pick_ref[...], rows_ref[...], 0, 0).astype(BF16)
    mine_ref[...] = both[:tokens]
    other_ref[...] = both[tokens:]


def shards_by_partner(n_rep, tokens, cotangent, route, host, w_gate, w_up, w_down_t):
    tok_rows, model_width = tokens.shape
    hot = host.shape[0]
    _, depth, width = w_gate.shape
    capacity = (3 * tok_rows + 2 * hot - 1) // (2 * hot)
    slots = hot * capacity
    parts = n_rep // 2
    block = 2 * capacity
    own = lax.axis_index("own").astype(jnp.int32).reshape(1)
    rank = lax.axis_index("rep").astype(jnp.int32).reshape(1)

    def over_own(value, k):
        return lax.ppermute(value, "own", [(i, i ^ k) for i in range(4)])

    def over_rep(value, k):
        return lax.ppermute(value, "rep", [(i, i ^ k) for i in range(n_rep)])

    route = route.reshape(1, tok_rows)
    route_b, tokens_b, cotangent_b = over_rep(route, 1), over_rep(tokens, 1), over_rep(cotangent, 1)
    joined = jnp.concatenate([w_gate[0], w_up[0], w_down_t[0]], axis=1)
    joined_1, joined_2 = over_own(joined, 1), over_own(joined, 2)
    slot_rows = pltpu.VMEM((slots, model_width), BF16)
    pick, own_x, near, far_xa, far_xb = call(
        functools.partial(pack_kernel, capacity),
        [shape(slots, 2 * tok_rows), shape(block, model_width), shape(2 * block, model_width)]
        + [shape(block, model_width)] * 2,
        2,
        [pltpu.VMEM((2 * tok_rows, model_width), BF16)],
    )(rank, host, route, route_b, tokens, tokens_b, cotangent, cotangent_b)
    far_x = [over_rep(far_xa, 4), over_rep(far_xb, 6)]
    near, *far_x = after([over_rep(near, 2), *far_x], ahead=1<<31)
    own_dy, far_a, far_b = call(pack_more_kernel, [shape(block, model_width)] * 3)(pick, cotangent, cotangent_b)
    joined_3 = [over_own(joined_1[: depth // 2], 2), over_own(joined_2[depth // 2 :], 1)]
    joined_3 = after(joined_3, ahead=1<<33)
    weights = [joined, joined_1, joined_2, *joined_3]

    x, *pieces = call(spread_kernel, [shape(slots, model_width)] + [shape(slots + slots // 2, depth)] * 4, 1)(
        own, own_x, near, *far_x, own_dy
    )
    far_dy = after([far_a, far_b], pieces[0])
    far_dy = [over_rep(far_dy[0], 4), over_rep(far_dy[1], 6)]
    pieces = [pieces[0]] + [over_own(pieces[k], k) for k in range(1, 4)]
    acts = call(act_kernel, [shape(slots, 2 * width, F32)], 1)(own, x, *weights)[0]

    *back, own_message, message_1, message_2, message_3 = call(
        functools.partial(grad_kernel, parts),
        [shape(block, model_width)] * parts + [shape(2 * slots, 2 * width)] * 4,
        1,
        [slot_rows],
        earlier=pieces[1:],
    )(own, acts, own_dy, near, *far_dy, *weights)
    far_back = after([over_rep(back[2], 4), over_rep(back[3], 6)], ahead=AHEAD)
    returned = [back[0], over_rep(back[1], 2), *far_back]
    message_3 = after([message_3], returned[1])[0]
    messages = after([over_own(message_1, 1), over_own(message_2, 2), over_own(message_3, 3)], ahead=AHEAD)
    messages = [own_message, *messages]

    mine, other = call(unpack_kernel, [shape(tok_rows, model_width)] * 2, 0, [slot_rows])(
        pick, *returned
    )
    x_grad = mine + over_rep(other, 1)
    out = call(
        sum_kernel,
        [shape(depth, width, F32)] * 3,
        0,
        [pltpu.VMEM((4 * slots, cols), BF16) for cols in (depth, depth, 2 * width, width)],
        earlier=[x_grad],
    )(*pieces, *messages)
    return (x_grad, *(grad[None] for grad in out))


def shards_whole(tokens, cotangent, route, host, w_gate, w_up, w_down_t):
    tok_rows, model_width = tokens.shape
    hot = host.shape[0]
    width = w_gate.shape[2]
    capacity = max(2, (3 * tok_rows + 2 * hot - 1) // (2 * hot))
    slots = hot * capacity
    labels = lax.broadcasted_iota(jnp.int32, (tok_rows, hot), 1)
    target = jnp.sum(jnp.where(route == labels, host[None, :], 0), axis=1)
    marked = (target[:, None] == labels).astype(jnp.int32)
    arrival = jnp.sum(jnp.cumsum(marked, axis=0) * marked, axis=1) - 1
    position = target * capacity + arrival
    pick = (lax.broadcasted_iota(jnp.int32, (slots, tok_rows), 0) == position[None, :]).astype(BF16)

    def exchange(value):
        split = value.astype(BF16).reshape(hot, capacity, model_width)
        return lax.all_to_all(split, "rep", split_axis=0, concat_axis=0, tiled=True).reshape(slots, model_width)

    slot_x, slot_dy = exchange(dot(pick, tokens, 1, 0)), exchange(dot(pick, cotangent, 1, 0))
    gate, up, down = (lax.all_gather(w[0], "own", axis=0, tiled=True) for w in (w_gate, w_up, w_down_t))
    gate_act, up_act, back_grad = dot(slot_x, gate, 1, 0), dot(slot_x, up, 1, 0), dot(slot_dy, down, 1, 0)
    sigmoid_g = jax.nn.sigmoid(gate_act)
    silu_gate = gate_act * sigmoid_g
    hidden = (silu_gate * up_act).astype(BF16)
    grad_gate_h = (back_grad * up_act * sigmoid_g * (1.0 + gate_act * (1.0 - sigmoid_g))).astype(BF16)
    grad_up_h = (back_grad * silu_gate).astype(BF16)
    returned = exchange(dot(grad_gate_h, gate, 1, 1) + dot(grad_up_h, up, 1, 1))
    x_grad = dot(pick, returned, 0, 0).astype(BF16)
    terms = [dot(slot_x, grad_gate_h, 0, 0), dot(slot_x, grad_up_h, 0, 0), dot(slot_dy, hidden, 0, 0)]
    summed = lax.psum_scatter(
        jnp.concatenate(terms, axis=1).astype(BF16), "own", scatter_dimension=0, tiled=True
    ).astype(F32)
    return (x_grad, *(summed[None, :, i * width : (i + 1) * width] for i in range(3)))


def solution(mesh):
    n_own, n_rep = mesh.shape["own"], mesh.shape["rep"]

    def shards(tokens, *rest):
        capacity = (3 * tokens.shape[0] + 2 * n_rep - 1) // (2 * n_rep)
        if n_own == 4 and n_rep == 8 and capacity % 8 == 0:
            return shards_by_partner(n_rep, tokens, *rest)
        return shards_whole(tokens, *rest)

    return jax.shard_map(
        shards,
        mesh=mesh,
        in_specs=(
            P(("own", "rep"), None),
            P(("own", "rep"), None),
            P(("own", "rep"), None),
            P(),
            P("rep", "own", None),
            P("rep", "own", None),
            P("rep", "own", None),
        ),
        out_specs=(
            P(("own", "rep"), None),
            P("rep", "own", None),
            P("rep", "own", None),
            P("rep", "own", None),
        ),
        check_vma=False,
    )
```
